32 devices in a mesh: section: 2 (over core), dp: 16 (over z, y, x).
Axes of the slice: x: 2, y: 2, z: 4, core: 2. Of those that a mesh axis runs over, the one named last changes fastest.
Arguments:
- raw_series: bfloat16 [128, 1024, 144], P('dp'), may hold values from -12 to 12
- series_ids: int32 [128], P('dp'), may hold values from 0 to 127, each once
- series_median: float32 [128], replicated, may hold values from -4 to 4
- series_scale: float32 [128], replicated, may hold values from 0.5 to 4
- cotangent: bfloat16 [128, 1024, 144], P('dp'), may hold values from -6 to 6
- norm_gains: float32 [2, 2, 144], P('section'), may hold values from 0.1 to 1.9
- qkv_weight: bfloat16 [2, 144, 432], P('section'), may hold values from -0.5 to 0.5
- out_weight: bfloat16 [2, 144, 144], P('section'), may hold values from -1.5 to 1.5
- gate_up_weight: bfloat16 [2, 144, 768], P('section'), may hold values from -0.5 to 0.5
- down_weight: bfloat16 [2, 384, 144], P('section'), may hold values from -0.3125 to 0.3125
Outputs:
- layer_outputs: bfloat16 [2, 128, 1024, 144], P('section', 'dp')
- input_grads: float32 [2, 128, 1024, 144], P('section', 'dp')
- grad_norm_gains: float32 [2, 2, 144], P('section')
- grad_qkv_weight: float32 [2, 144, 432], P('section')
- grad_out_weight: float32 [2, 144, 144], P('section')
- grad_gate_up_weight: float32 [2, 144, 768], P('section')
- grad_down_weight: float32 [2, 384, 144], P('section')
The draws below stay inside these ranges and needn't reach their ends.
Inputs may be any that keep to these rules, and one draw needn't show every extreme that they name: `series_ids`: each series number appears exactly once.
All inputs are finite; a program needn't handle non-finite values.
Results may differ from the reference program's by a relative error of at most 0.012.
Values may be sent and summed in bfloat16 or wider, within the bound.
A program may use at most 256 MiB of HBM per device.

```python
import math
import jax
import jax.numpy as jnp
from jax import lax

D = 144
HEADS = 9
HEAD = 16
FF = 384
SEQ = 1024
SERIES = 128


def level_of(own_key, shape, shards, smallest, high):
    def one(dim, shards_of):
        draws = jax.random.uniform(jax.random.fold_in(jax.random.fold_in(own_key, 6), dim), (shards_of,), jnp.float32, smallest / len(shards), high / len(shards))
        return jnp.repeat(jnp.exp(draws), shape[dim] // shards_of).reshape((-1,) + (1,) * (len(shape) - dim - 1))

    level = one(*shards[0])
    for cut in shards[1:]:
        level = level * one(*cut)
    return level


def centred(key, extent, width, most, cuts=(), held_as=jnp.bfloat16):
    values = jax.random.normal(key, extent, jnp.float32) * width
    if len(cuts) > 0:
        values = level_of(key, extent, cuts, -0.22, 0.18) * values
    return jnp.clip(values, min=-most, max=most).astype(held_as)


def setup_inputs(seed: int = 0) -> dict:
    splits = jax.random.split(jax.random.key(seed), 11)
    return {
        "raw_series": centred(splits[0], (SERIES, SEQ, D), 2.0, 12.0, ((0, 16),)),
        "series_ids": jax.random.permutation(splits[1], SERIES).astype(jnp.int32),
        "series_median": centred(splits[2], (SERIES,), 1.0, 4.0, (), jnp.float32),
        "series_scale": jnp.clip(jnp.exp(jax.random.uniform(splits[3], (SERIES,), jnp.float32, math.log(0.5), math.log(4.0))), 0.5, 4.0),
        "cotangent": centred(splits[4], (SERIES, SEQ, D), 1.0, 6.0, ((0, 16),)),
        "norm_gains": jnp.clip(1.0 + 0.18 * jax.random.normal(splits[5], (2, 2, D), jnp.float32), 0.1, 1.9),
        "qkv_weight": centred(splits[6], (2, D, 3 * D), D ** -0.5, 0.5, ((0, 2),)),
        "out_weight": centred(splits[7], (2, D, D), (D // 8) ** -0.5, 1.5, ((0, 2),)),
        "gate_up_weight": centred(splits[8], (2, D, 2 * FF), D ** -0.5, 0.5, ((0, 2),)),
        "down_weight": centred(splits[9], (2, FF, D), FF ** -0.5, 0.3125, ((0, 2),)),
    }


@jax.custom_vjp
def low(v):
    return lax.optimization_barrier(v.astype(jnp.bfloat16)).astype(jnp.float32)

@jax.custom_vjp
def low_back(v):
    return v

def low_keep(v):
    return (low(v), None)

def low_pass(kept, grad):
    return (grad,)

def back_keep(v):
    return (v, None)

def back_low(kept, grad):
    return (low(grad),)
low.defvjp(low_keep, low_pass)
low_back.defvjp(back_keep, back_low)
epsilon = 1e-06
highest = lax.Precision.HIGHEST
single = jnp.float32

def matmul(left, right):
    return jnp.dot(left, right, precision=highest, preferred_element_type=single)

def rotary_tables(length, head_width):
    half_width = head_width // 2
    frequency = 10000.0 ** (-jnp.arange(half_width, dtype=single) / half_width)
    angles = jnp.arange(length, dtype=single)[:, None] * frequency[None, :]
    return (jnp.cos(angles)[:, None, :], jnp.sin(angles)[:, None, :])

def rotate(values, cosine_table, sine_table):
    half_width = values.shape[-1] // 2
    leading = values[..., :half_width]
    trailing = values[..., half_width:]
    return jnp.concatenate([leading * cosine_table - trailing * sine_table, trailing * cosine_table + leading * sine_table], axis=-1)

def attention(queries, key_rows, values):
    length = queries.shape[0]
    block_rows = min(512, length)
    block_count = length // block_rows
    positions = jnp.arange(length)

    def one_block(pieces):
        query_block, first_row = pieces
        scores = jnp.einsum('qhe,khe->hqk', query_block, key_rows, precision=highest) * HEAD ** (-0.5)
        scores = low_back(scores)
        rows_here = first_row + jnp.arange(block_rows)
        scores = jnp.where(positions[None, None, :] <= rows_here[None, :, None], scores, -1e+30)
        largest = lax.optimization_barrier(jnp.max(scores, axis=-1, keepdims=True))
        exponent = jnp.exp(scores - largest)
        probabilities = low(exponent / lax.optimization_barrier(jnp.sum(exponent, axis=-1, keepdims=True)))
        return jnp.einsum('hqk,khe->qhe', probabilities, values, precision=highest)
    blocks = queries.reshape(block_count, block_rows, HEADS, HEAD)
    starts = jnp.arange(block_count) * block_rows
    return lax.map(jax.checkpoint(one_block), (blocks, starts)).reshape(length, HEADS * HEAD)

def layer(inputs, params, tables):
    norm_gains, qkv_weight, out_weight, gate_up_weight, down_weight = params
    cosine_table, sine_table = tables
    length = inputs.shape[0]
    normed = low(inputs * lax.rsqrt(lax.optimization_barrier(jnp.mean(inputs * inputs, axis=-1, keepdims=True)) + epsilon) * norm_gains[0])
    projected = matmul(normed, qkv_weight).reshape(length, 3, HEADS, HEAD)
    queries = low(rotate(low_back(projected[:, 0]), cosine_table, sine_table))
    key_rows = low(rotate(low_back(projected[:, 1]), cosine_table, sine_table))
    values = low(low_back(projected[:, 2]))
    attended = low(low_back(attention(queries, key_rows, values)))
    residual = inputs + low_back(matmul(attended, out_weight))
    normed_mid = low(residual * lax.rsqrt(lax.optimization_barrier(jnp.mean(residual * residual, axis=-1, keepdims=True)) + epsilon) * norm_gains[1])
    gate_up = matmul(normed_mid, gate_up_weight)
    hidden_width = down_weight.shape[0]
    gate_pre = low_back(gate_up[:, :hidden_width])
    up_pre = low_back(gate_up[:, hidden_width:])
    activated = low(gate_pre * jax.nn.sigmoid(gate_pre) * up_pre)
    return residual + low_back(matmul(activated, down_weight))

def reference(raw_series, series_ids, series_median, series_scale, cotangent, norm_gains, qkv_weight, out_weight, gate_up_weight, down_weight):
    tables = rotary_tables(SEQ, HEAD)
    params = tuple((member.astype(single) for member in (norm_gains, qkv_weight, out_weight, gate_up_weight, down_weight)))
    first_params = tuple((member[0] for member in params))
    second_params = tuple((member[1] for member in params))
    centers = series_median[series_ids]
    spreads = series_scale[series_ids]

    def second_section(sent, layer_params):
        return layer(sent, layer_params, tables)

    def one_series(running, pieces):
        raw_rows, center, spread, grad_rows = pieces

        def first_section(rows_in, layer_params):
            return low(low_back(layer((rows_in - center) / spread, layer_params, tables)))
        sent, first_back = jax.vjp(first_section, raw_rows, first_params)
        result, second_back = jax.vjp(second_section, sent, second_params)
        grad_sent, grad_second = second_back(grad_rows)
        grad_raw, grad_first = first_back(grad_sent)
        running = jax.tree.map(lambda total_term, first_term, second_term: total_term + jnp.stack([first_term, second_term]), running, grad_first, grad_second)
        return (running, (sent, result, grad_raw, grad_sent))
    zero_totals = tuple((jnp.zeros(member.shape, single) for member in params))
    pieces = (raw_series.astype(single), centers, spreads, cotangent.astype(single))
    totals, (sent_all, result_all, grad_raw_all, grad_sent_all) = lax.scan(one_series, zero_totals, pieces)
    layer_outputs = jnp.stack([sent_all, result_all]).astype(jnp.bfloat16)
    input_grads = jnp.stack([grad_raw_all, grad_sent_all])
    return (layer_outputs, input_grads, totals[0], totals[1], totals[2], totals[3], totals[4])
```

```python
import functools
import math

import jax
import jax.numpy as jnp
import numpy as np
from jax import lax
from jax.experimental import pallas as pl
from jax.experimental.pallas import tpu as pltpu
from jax.sharding import PartitionSpec as P

HEAD = 16
HALF = HEAD // 2
TILE = 256
EPSILON = 1e-06
LOG2E = math.log2(math.e)
QKV_REST = 48
OUT_REST = 16
MESH = pl.DeviceIdType.MESH
bfloat = jnp.bfloat16
single = jnp.float32


def dot(left, right):
    return jnp.dot(left, right, preferred_element_type=single)


def dot_nt(left, right):
    return lax.dot_general(left, right, (((1,), (1,)), ((), ())), preferred_element_type=single)


def rms_scale(values):
    return lax.rsqrt(jnp.mean(values * values, axis=0, keepdims=True) + EPSILON)


def rms_backward(grad_normed, values, inverse, gain):
    scaled = grad_normed * gain
    centre = jnp.mean(scaled * values, axis=0, keepdims=True)
    grad_values = inverse * scaled - values * (inverse * inverse * inverse * centre)
    product = grad_normed * values * inverse
    partial = product[:, :128]
    for start in range(128, product.shape[1], 128):
        partial = partial + product[:, start : start + 128]
    return grad_values, partial


def causal(block):
    rows = lax.broadcasted_iota(jnp.int32, block.shape, 0)
    columns = lax.broadcasted_iota(jnp.int32, block.shape, 1)
    return rows <= columns


def tile_start(j):
    return j * (j + 1) // 2 * TILE


def train_kernel(
    heads,
    hidden,
    place,
    series_ids,
    median,
    scale,
    raw,
    cotangent,
    own_gains,
    own_qkv,
    own_out,
    own_gate_up,
    own_down_t,
    other_gains,
    other_qkv,
    other_out,
    other_gate_up,
    other_down_t,
    cosine,
    sine,
    kept_out,
    kept_grad,
    sent_out,
    sent_grad,
    own_total,
    other_total,
    gains,
    qkv_t,
    out_t,
    gate_up_t,
    down_t,
    qkv_w,
    out_w,
    gate_up_w,
    down_w,
    grad_gains,
    grad_qkv,
    grad_out,
    grad_gate_up,
    grad_down,
    inputs,
    inverse1,
    normed,
    queries,
    keys,
    values,
    rows_major,
    exponents,
    attended32,
    reciprocal,
    attended,
    residual,
    inverse2,
    mid,
    gate_up,
    activated,
    grad,
    grad_low,
    grad_pre,
    grad_res_low,
    grad_att,
    grad_q,
    grad_k,
    grad_v,
    grad_proj,
):
    step = pl.program_id(0)
    section = place[0]
    series = place[1] + step
    number = series_ids[series]
    centre = median[number]
    inverse_spread = 1.0 / scale[number]
    width, length = inputs.shape[1:]
    tiles = length // TILE
    query_factor = HEAD**-0.5 * LOG2E

    @pl.when(step == 0)
    def _():
        for ref in (grad_gains, grad_qkv, grad_out, grad_gate_up, grad_down):
            ref[...] = jnp.zeros_like(ref)
        row = lax.broadcasted_iota(jnp.int32, (2, heads, HEAD, length), 2)
        values[:, :, HEAD:, :] = jnp.where(row < 2, 1.0, 0.0).astype(bfloat)
        flipped = lambda w: w.astype(single).T.astype(bfloat)
        for l, (gain, qkv, out, both, down) in (
            (section, (own_gains, own_qkv, own_out, own_gate_up, own_down_t)),
            (1 - section, (other_gains, other_qkv, other_out, other_gate_up, other_down_t)),
        ):
            for part in range(2):
                row = jnp.broadcast_to(gain[part : part + 1, :], (128, width))
                gains[l, part] = row.T
            qkv_w[l] = qkv[...]
            qkv_t[l] = flipped(qkv[...])
            out_w[l] = out[...]
            out_t[l] = flipped(out[...])
            gate_up_w[l] = both[...]
            gate_up_t[l] = flipped(both[...])
            down_t[l] = down[...]
            down_w[l] = flipped(down[...])

    def gain_of(l, part):
        return jnp.concatenate([gains[l, part]] * (TILE // 128), axis=1)

    inputs[0] = (raw[0].astype(single) - centre) * inverse_spread
    grad[...] = cotangent[0].astype(single)

    def rotated(block, cs, sign):
        a, b = block[:, :HALF], block[:, HALF:]
        cos, sin = cosine[:, cs], sine[:, cs] * sign
        return jnp.concatenate([a * cos - b * sin, b * cos + a * sin], axis=1)

    def forward(l, carry):
        largest = jnp.zeros((1, 1, TILE), single)
        largest_q = jnp.zeros((heads, 1, TILE), single)
        largest_k = jnp.zeros((heads, 1, TILE), single)
        for c in range(tiles):
            cs = slice(c * TILE, (c + 1) * TILE)
            u = inputs[l, :, cs]
            inv = rms_scale(u)
            inverse1[l, :, cs] = inv
            low = (u * inv * gain_of(l, 0)).astype(bfloat)
            normed[l, :, cs] = low
            projected = dot(qkv_t[l], low).reshape(3 * heads, HEAD, TILE)
            q = (rotated(projected[:heads], cs, 1.0) * query_factor).astype(bfloat)
            k = rotated(projected[heads : 2 * heads], cs, 1.0)
            queries[l, :, :, cs] = q
            keys[l, :, :, cs] = k.astype(bfloat)
            values[l, :, :HEAD, cs] = projected[2 * heads :].astype(bfloat)
            for h in range(heads):
                rows_major[h, cs, :HEAD] = k[h].T.astype(bfloat)
            q32 = q.astype(single)
            k32 = k.astype(bfloat).astype(single)
            largest_q = jnp.maximum(largest_q, jnp.sum(q32 * q32, axis=1, keepdims=True))
            largest_k = jnp.maximum(largest_k, jnp.sum(k32 * k32, axis=1, keepdims=True))
        bound = jnp.max(jnp.max(largest_q, axis=2) * jnp.max(largest_k, axis=2))

        def finish(h, j, total):
            js = slice(j * TILE, (j + 1) * TILE)
            inverse = 1.0 / total[HEAD : HEAD + 1]
            out = total[:HEAD] * inverse
            reciprocal[l, h, :, js] = inverse
            attended32[l, h, :, js] = out
            attended[l, h, :, js] = out.astype(bfloat)

        small = bound <= 1e4

        @pl.when(small)
        def _():
            group = 3
            ahead = 3

            def some(hh, carry):
                work = [
                    (hh * group + g, j, k)
                    for g in range(group)
                    for j in range(tiles)
                    for k in range(j + 1)
                ]
                scores = {}

                def score(n):
                    h, j, k = work[n]
                    scores[n] = dot(
                        rows_major[h, k * TILE : (k + 1) * TILE, :HEAD],
                        queries[l, h, :, j * TILE : (j + 1) * TILE],
                    )

                for n in range(ahead):
                    score(n)
                total = None
                for n, (h, j, k) in enumerate(work):
                    if n + ahead < len(work):
                        score(n + ahead)
                    e = jnp.exp2(scores.pop(n))
                    if k == j:
                        e = jnp.where(causal(e), e, 0.0)
                    e = e.astype(bfloat)
                    first = tile_start(j) + k * TILE
                    exponents[l, h, first : first + TILE, :] = e
                    part = dot(values[l, h, :, k * TILE : (k + 1) * TILE], e)
                    total = part if k == 0 else total + part
                    if k == j:
                        finish(h, j, total)
                return carry

            lax.fori_loop(0, heads // group, some, 0)

        @pl.when(jnp.logical_not(small))
        def _():
            def one(h, carry):
                for j in range(tiles):
                    count = (j + 1) * TILE
                    js = slice(j * TILE, (j + 1) * TILE)
                    score = dot(rows_major[h, :count, :HEAD], queries[l, h, :, js])
                    rows = lax.broadcasted_iota(jnp.int32, score.shape, 0)
                    columns = lax.broadcasted_iota(jnp.int32, score.shape, 1) + j * TILE
                    score = jnp.where(rows <= columns, score, -1e30)
                    e = jnp.exp2(score - jnp.max(score, axis=0, keepdims=True)).astype(bfloat)
                    exponents[l, h, tile_start(j) : tile_start(j) + count, :] = e
                    finish(h, j, dot(values[l, h, :, :count], e))
                return carry

            lax.fori_loop(0, heads, one, 0)

        for c in range(tiles):
            cs = slice(c * TILE, (c + 1) * TILE)
            res = inputs[l, :, cs] + dot(out_t[l], attended[l, :, :, cs].reshape(width, TILE))
            residual[l, :, cs] = res
            inv = rms_scale(res)
            inverse2[l, :, cs] = inv
            low = (res * inv * gain_of(l, 1)).astype(bfloat)
            mid[l, :, cs] = low
            both = dot(gate_up_t[l], low)
            gate_up[l, :, cs] = both
            gate, up = both[:hidden], both[hidden:]
            act = (gate * jax.nn.sigmoid(gate) * up).astype(bfloat)
            activated[l, :, cs] = act
            result = res + dot(down_t[l], act)
            low = result.astype(bfloat)

            @pl.when(l == section)
            def _():
                kept_out[0, :, cs] = low

            @pl.when(l != section)
            def _():
                sent_out[0, :, cs] = low

            @pl.when(l == 0)
            def _():
                inputs[1, :, cs] = low.astype(single)

        return carry

    lax.fori_loop(0, 2, forward, 0)

    def backward(turn, carry):
        l = 1 - turn
        slot = lax.rem(l + section, 2)
        for c in range(tiles):
            cs = slice(c * TILE, (c + 1) * TILE)
            g = grad[:, cs]
            low = g.astype(bfloat)
            grad_low[:, cs] = low
            grad_act = dot(down_w[l], low)
            gate, up = gate_up[l, :hidden, cs], gate_up[l, hidden:, cs]
            sig = jax.nn.sigmoid(gate)
            inner = grad_act * sig
            grad_gate = inner * up * (1.0 + gate * (1.0 - sig))
            grad_up = inner * gate
            pre = jnp.concatenate([grad_gate, grad_up], axis=0).astype(bfloat)
            grad_pre[:, cs] = pre
            grad_mid = dot(gate_up_w[l], pre)
            res, inv = residual[l, :, cs], inverse2[l, :, cs]
            grad_res, partial = rms_backward(grad_mid, res, inv, gain_of(l, 1))
            grad_gains[slot, 1] += partial
            grad_res = grad_res + g
            grad[:, cs] = grad_res
            low = grad_res.astype(bfloat)
            grad_res_low[:, cs] = low
            back = dot(out_w[l], low).astype(bfloat).astype(single).reshape(heads, HEAD, TILE)
            inverse = reciprocal[l, :, :, cs]
            mean = jnp.sum(back * attended32[l, :, :, cs], axis=1, keepdims=True) * -inverse
            coarse = mean.astype(bfloat).astype(single)
            row = lax.broadcasted_iota(jnp.int32, (heads, HEAD, TILE), 1)
            extra = jnp.where(row == 0, coarse, jnp.where(row == 1, mean - coarse, 0.0))
            grad_att[:, :, cs] = jnp.concatenate([back * inverse, extra], axis=1).astype(bfloat)
        grad_down[slot] += dot_nt(grad_low[...], activated[l])
        grad_gate_up[slot] += dot_nt(mid[l], grad_pre[...])
        grad_out[slot] += dot_nt(attended[l].reshape(width, length), grad_res_low[...])

        for h in range(heads):
            rows_major[h] = values[l, h].astype(single).T.astype(bfloat)

        group = 3
        ahead = 3

        def some(hh, carry):
            work = [
                (g, j, k) for g in range(group) for j in range(tiles) for k in range(j + 1)
            ]
            products = {}

            def product(n):
                g, j, k = work[n]
                products[n] = dot(
                    rows_major[hh * group + g, k * TILE : (k + 1) * TILE, :],
                    grad_att[hh * group + g, :, j * TILE : (j + 1) * TILE],
                )

            for n in range(ahead):
                product(n)
            sums = {}

            def add(key, value):
                sums[key] = sums[key] + value if key in sums else value

            for n, (g, j, k) in enumerate(work):
                h = hh * group + g
                if n + ahead < len(work):
                    product(n + ahead)
                first = tile_start(j) + k * TILE
                e = exponents[l, h, first : first + TILE, :]
                grad_score = e * products.pop(n).astype(bfloat)
                js, ks = slice(j * TILE, (j + 1) * TILE), slice(k * TILE, (k + 1) * TILE)
                add(("q", j), dot(keys[l, h, :, ks], grad_score))
                add(("k", k), dot_nt(queries[l, h, :, js], grad_score))
                add(("v", k), dot_nt(grad_att[h, :HEAD, js], e))
                if (j, k) == (tiles - 1, tiles - 1):
                    for t in range(tiles):
                        ts = slice(t * TILE, (t + 1) * TILE)
                        grad_q[h, :, ts] = sums.pop(("q", t))
                        grad_k[h, :, ts] = sums.pop(("k", t))
                        grad_v[h, :, ts] = sums.pop(("v", t))
            return carry

        lax.fori_loop(0, heads // group, some, 0)

        for c in range(tiles):
            cs = slice(c * TILE, (c + 1) * TILE)
            dq = rotated(grad_q[:, :, cs] * HEAD**-0.5, cs, -1.0)
            dk = rotated(grad_k[:, :, cs] * (1.0 / LOG2E), cs, -1.0)
            low = jnp.concatenate([dq, dk, grad_v[:, :, cs]], axis=0).astype(bfloat)
            low = low.reshape(3 * width, TILE)
            grad_proj[:, cs] = low
            grad_normed = dot(qkv_w[l], low)
            u, inv = inputs[l, :, cs], inverse1[l, :, cs]
            grad_u, partial = rms_backward(grad_normed, u, inv, gain_of(l, 0))
            grad_gains[slot, 0] += partial
            grad_u = grad_u + grad[:, cs]
            grad[:, cs] = grad_u.astype(bfloat).astype(single)
            grad_u = grad_u * jnp.where(l == 0, inverse_spread, 1.0)

            @pl.when(l == section)
            def _():
                kept_grad[0, :, cs] = grad_u

            @pl.when(l != section)
            def _():
                sent_grad[0, :, cs] = grad_u.astype(bfloat)

        grad_qkv[slot] += dot_nt(normed[l], grad_proj[...])
        return carry

    lax.fori_loop(0, 2, backward, 0)

    @pl.when(step == pl.num_programs(0) - 1)
    def _():
        for slot, total in ((0, own_total), (1, other_total)):
            blocks = []
            for ref in (grad_gate_up, grad_down, grad_qkv, grad_out):
                blocks += [ref[slot, :, n : n + 128] for n in range(0, ref.shape[2] - 127, 128)]
            lane = lax.broadcasted_iota(jnp.int32, (width, 128), 1)
            spare = grad_qkv[slot, :, 3 * width - QKV_REST :]
            out_rest = grad_out[slot, :, width - OUT_REST :]
            columns = [jnp.sum(grad_gains[slot, n], axis=1, keepdims=True) for n in range(2)]
            rest = jnp.concatenate(
                [spare, out_rest] + columns
                + [jnp.zeros((width, 128 - QKV_REST - OUT_REST - 2), single)],
                axis=1,
            )
            blocks.append(rest)
            for n, block in enumerate(blocks):
                total[n * width : (n + 1) * width, :] = block.astype(total.dtype)
            used = len(blocks) * width
            total[used:, :] = jnp.zeros((total.shape[0] - used, 128), total.dtype)


def rotary_tables(length):
    frequency = 10000.0 ** (-np.arange(HALF, dtype=np.float64) / HALF)
    frequency = frequency.astype(np.float32)
    angles = np.arange(length, dtype=np.float32)[None, :] * frequency[:, None]
    return np.cos(angles).astype(np.float32), np.sin(angles).astype(np.float32)


def train(section, rows, raw, series_ids, median, scale, cotangent, own, other):
    count = raw.shape[0] // 2
    width, length = raw.shape[1:]
    heads = width // HEAD
    hidden = own[4].shape[1]
    place = jnp.stack([section, section * count]).astype(jnp.int32)
    cosine, sine = rotary_tables(length)
    operands = (raw, cotangent) + own + other + (jnp.asarray(cosine), jnp.asarray(sine))
    smem = pl.BlockSpec(memory_space=pltpu.SMEM)

    def whole(array):
        zeros = (0,) * len(array.shape)
        return pl.BlockSpec(
            array.shape, lambda i, *_: zeros, pipeline_mode=pl.Buffered(buffer_count=1)
        )

    placed_block = pl.BlockSpec((1, width, length), lambda i, place, ids: (place[1] + i, 0, 0))
    block = pl.BlockSpec((1, width, length), lambda i, *_: (i, 0, 0))
    shape = jax.ShapeDtypeStruct
    totals = (shape((rows, 128), single), shape((rows, 128), bfloat))
    pairs = length // TILE * (length // TILE + 1) // 2
    v = pltpu.VMEM
    scratch = [
        v((2, 2, width, 128), single),
        v((2, 3 * width, width), bfloat),
        v((2, width, width), bfloat),
        v((2, 2 * hidden, width), bfloat),
        v((2, width, hidden), bfloat),
        v((2, width, 3 * width), bfloat),
        v((2, width, width), bfloat),
        v((2, width, 2 * hidden), bfloat),
        v((2, hidden, width), bfloat),
        v((2, 2, width, 128), single),
        v((2, width, 3 * width), single),
        v((2, width, width), single),
        v((2, width, 2 * hidden), single),
        v((2, width, hidden), single),
        v((2, width, length), single),
        v((2, 1, length), single),
        v((2, width, length), bfloat),
        v((2, heads, HEAD, length), bfloat),
        v((2, heads, HEAD, length), bfloat),
        v((2, heads, 2 * HEAD, length), bfloat),
        v((heads, length, 2 * HEAD), bfloat),
        v((2, heads, pairs * TILE, TILE), bfloat),
        v((2, heads, HEAD, length), single),
        v((2, heads, 1, length), single),
        v((2, heads, HEAD, length), bfloat),
        v((2, width, length), single),
        v((2, 1, length), single),
        v((2, width, length), bfloat),
        v((2, 2 * hidden, length), single),
        v((2, hidden, length), bfloat),
        v((width, length), single),
        v((width, length), bfloat),
        v((2 * hidden, length), bfloat),
        v((width, length), bfloat),
        v((heads, 2 * HEAD, length), bfloat),
        v((heads, HEAD, length), single),
        v((heads, HEAD, length), single),
        v((heads, HEAD, length), single),
        v((3 * width, length), bfloat),
    ]
    return pl.pallas_call(
        functools.partial(train_kernel, heads, hidden),
        grid_spec=pltpu.PrefetchScalarGridSpec(
            num_scalar_prefetch=2,
            grid=(count,),
            in_specs=[smem, smem, placed_block, placed_block] + [whole(a) for a in operands[2:]],
            out_specs=[placed_block, placed_block, block, block] + [whole(t) for t in totals],
            scratch_shapes=scratch,
        ),
        out_shape=(
            shape(raw.shape, bfloat),
            shape(raw.shape, single),
            shape((count, width, length), bfloat),
            shape((count, width, length), bfloat),
        )
        + totals,
        compiler_params=pltpu.CompilerParams(vmem_limit_bytes=64 * 2**20 - 2**16),
    )(place, series_ids, median, scale, *operands)


def partner():
    return {"section": 1 - lax.axis_index("section")}


def meet(peers):
    barrier = pltpu.get_barrier_semaphore()
    for peer in peers:
        pl.semaphore_signal(barrier, inc=1, device_id=peer, device_id_type=MESH)
    pl.semaphore_wait(barrier, len(peers))


def swap_kernel(count, *refs):
    own, other, send, recv = refs[:count], refs[count : 2 * count], refs[-2], refs[-1]
    meet([partner()])
    copies = [
        pltpu.make_async_remote_copy(
            src_ref=own[n],
            dst_ref=other[n],
            send_sem=send.at[n],
            recv_sem=recv.at[n],
            device_id=partner(),
            device_id_type=MESH,
        )
        for n in range(count)
    ]
    for copy in copies:
        copy.start()
    for copy in copies:
        copy.wait()


def swap_weights(weights):
    count = len(weights)
    anywhere = pl.BlockSpec(memory_space=pl.ANY)
    return pl.pallas_call(
        functools.partial(swap_kernel, count),
        out_shape=tuple(jax.ShapeDtypeStruct(w.shape, w.dtype) for w in weights),
        in_specs=[anywhere] * count,
        out_specs=[anywhere] * count,
        scratch_shapes=[pltpu.SemaphoreType.DMA((count,)), pltpu.SemaphoreType.DMA((count,))],
        compiler_params=pltpu.CompilerParams(collective_id=0, has_side_effects=True),
    )(*weights)


def group_sizes(devices):
    sizes = []
    while devices > 1:
        size = 4 if devices % 4 == 0 else devices
        sizes.append(size)
        devices //= size
    return sizes


def reduce_kernel(
    sizes,
    own_total,
    other_total,
    sent_out,
    sent_grad,
    far_out,
    far_grad,
    grad_gains,
    grad_qkv,
    grad_out,
    grad_gate_up,
    grad_down,
    arrived,
    *scratch,
):
    count = len(sizes)
    parts = scratch[:count]
    slots = scratch[count : 2 * count]
    wholes = scratch[2 * count : 3 * count]
    last, swap_send, swap_recv, sum_send, sum_recv, gather_send, gather_recv = scratch[3 * count :]
    me = lax.axis_index("dp")
    places, groups = [], []
    stride = 1
    for size in sizes:
        place = lax.rem(lax.div(me, stride), size)
        peers = []
        for turn in range(1, size):
            other = lax.rem(place + turn, size)
            peers.append((other, {"dp": me + (other - place) * stride}))
        places.append(place)
        groups.append(peers)
        stride *= size
    meet([partner()] + [device for peers in groups for _, device in peers])

    def copy(source, target, send, recv, device):
        c = pltpu.make_async_remote_copy(
            src_ref=source,
            dst_ref=target,
            send_sem=send,
            recv_sem=recv,
            device_id=device,
            device_id_type=MESH,
        )
        c.start()
        return c

    near = copy(other_total, arrived, swap_send.at[0], swap_recv.at[0], partner())
    far = [
        copy(sent_out, far_out, swap_send.at[1], swap_recv.at[1], partner()),
        copy(sent_grad, far_grad, swap_send.at[2], swap_recv.at[2], partner()),
    ]
    near.wait()
    parts[0][...] = (own_total[...] + arrived[...].astype(single)).astype(bfloat)
    first = 0
    starts = []
    for n, size in enumerate(sizes):
        chunk = parts[n].shape[0] // size
        copies = []
        for turn, (other, device) in enumerate(groups[n]):
            copies.append(
                copy(
                    parts[n].at[pl.ds(pl.multiple_of(other * chunk, 16), chunk)],
                    slots[n].at[turn],
                    sum_send.at[first + turn],
                    sum_recv.at[first + turn],
                    device,
                )
            )
        total = parts[n][pl.ds(pl.multiple_of(places[n] * chunk, 16), chunk), :].astype(single)
        for turn, c in enumerate(copies):
            c.wait()
            total = total + slots[n][turn].astype(single)
        target = parts[n + 1] if n + 1 < count else last
        target[...] = total.astype(bfloat)
        starts.append(first)
        first += size - 1
    source = last
    for n in reversed(range(count)):
        chunk = parts[n].shape[0] // sizes[n]
        mine = pl.ds(pl.multiple_of(places[n] * chunk, 16), chunk)
        copies = []
        for turn, (_, device) in enumerate(groups[n]):
            k = starts[n] + turn
            copies.append(
                copy(source, wholes[n].at[mine], gather_send.at[k], gather_recv.at[k], device)
            )
        wholes[n][mine, :] = source[...]
        for c in copies:
            c.wait()
        source = wholes[n]
    width = grad_qkv.shape[0]
    block = 0
    for ref in (grad_gate_up, grad_down, grad_qkv, grad_out):
        for n in range(0, ref.shape[1] - 127, 128):
            ref[:, n : n + 128] = source[block * width : (block + 1) * width, :].astype(single)
            block += 1
    rest = source[block * width : (block + 1) * width, :].astype(single)
    grad_qkv[:, 3 * width - QKV_REST :] = rest[:, :QKV_REST]
    grad_out[:, width - OUT_REST :] = rest[:, QKV_REST : QKV_REST + OUT_REST]
    grad_gains[...] = rest.T[QKV_REST + OUT_REST : QKV_REST + OUT_REST + 2, :]
    for c in far:
        c.wait()


def reduce(devices, own_total, other_total, sent_out, sent_grad, width, hidden):
    sizes = group_sizes(devices)
    rows = own_total.shape[0]
    v = pltpu.VMEM
    shape = jax.ShapeDtypeStruct
    parts, slots, left = [], [], rows
    for size in sizes:
        parts.append(v((left, 128), bfloat))
        left //= size
        slots.append(v((size - 1, left, 128), bfloat))
    links = sum(size - 1 for size in sizes)
    dma = pltpu.SemaphoreType.DMA
    anywhere = pl.BlockSpec(memory_space=pl.ANY)
    vmem = pl.BlockSpec(memory_space=pltpu.VMEM)
    return pl.pallas_call(
        functools.partial(reduce_kernel, sizes),
        out_shape=(
            shape(sent_out.shape, bfloat),
            shape(sent_grad.shape, bfloat),
            shape((2, width), single),
            shape((width, 3 * width), single),
            shape((width, width), single),
            shape((width, 2 * hidden), single),
            shape((width, hidden), single),
        ),
        in_specs=[vmem, vmem, anywhere, anywhere],
        out_specs=[anywhere, anywhere] + [vmem] * 5,
        scratch_shapes=[v((rows, 128), bfloat)]
        + parts
        + slots
        + parts
        + [v((left, 128), bfloat), dma((3,)), dma((3,))]
        + [dma((links,))] * 4,
        compiler_params=pltpu.CompilerParams(
            collective_id=1, has_side_effects=True, vmem_limit_bytes=40 * 2**20
        ),
    )(own_total, other_total, sent_out, sent_grad)


def on_device(
    devices,
    raw,
    series_ids,
    median,
    scale,
    cotangent,
    norm_gains,
    qkv_weight,
    out_weight,
    gate_up_weight,
    down_weight,
):
    section = lax.axis_index("section")
    turned = lambda a: jnp.swapaxes(a, -1, -2)
    count = raw.shape[0] // 2
    width, hidden = raw.shape[2], down_weight.shape[1]
    own = (norm_gains[0], qkv_weight[0], out_weight[0], gate_up_weight[0], turned(down_weight[0]))
    other = swap_weights(own)
    blocks = 14
    rows = -(-blocks * width // (16 * devices)) * 16 * devices
    kept_out, kept_grad, sent_out, sent_grad, own_total, other_total = train(
        section, rows, turned(raw), series_ids, median, scale, turned(cotangent), own, other
    )
    far_out, far_grad, gain, qkv, out, gate_up, down = reduce(
        devices, own_total, other_total, sent_out, sent_grad, width, hidden
    )
    place = ((1 - section) * count, 0, 0)
    layer_outputs = lax.dynamic_update_slice(kept_out, far_out, place)
    input_grads = lax.dynamic_update_slice(kept_grad, far_grad.astype(single), place)
    return (
        turned(layer_outputs)[None],
        turned(input_grads)[None],
        gain[None],
        qkv[None],
        out[None],
        gate_up[None],
        turned(down)[None],
    )


def solution(mesh):
    placed = (
        P("dp", None, None),
        P("dp"),
        P(),
        P(),
        P("dp", None, None),
        P("section", None, None),
        P("section", None, None),
        P("section", None, None),
        P("section", None, None),
        P("section", None, None),
    )
    return jax.shard_map(
        functools.partial(on_device, mesh.shape["dp"]),
        mesh=mesh,
        in_specs=placed,
        out_specs=(
            P("section", "dp", None, None),
            P("section", "dp", None, None),
            P("section", None, None),
            P("section", None, None),
            P("section", None, None),
            P("section", None, None),
            P("section", None, None),
        ),
        check_vma=False,
    )
```

```python
import functools
import math

import jax
import jax.numpy as jnp
import numpy as np
from jax import lax
from jax.experimental import pallas as pl
from jax.experimental.pallas import tpu as pltpu
from jax.sharding import PartitionSpec as P

HEAD = 16
HALF = HEAD // 2
TILE = 256
EPSILON = 1e-06
LOG2E = math.log2(math.e)
QKV_REST = 48
OUT_REST = 16
MESH = pl.DeviceIdType.MESH
bfloat = jnp.bfloat16
single = jnp.float32


def dot(left, right):
    return jnp.dot(left, right, preferred_element_type=single)


def dot_nt(left, right):
    return lax.dot_general(left, right, (((1,), (1,)), ((), ())), preferred_element_type=single)


def rms_scale(values):
    return lax.rsqrt(jnp.mean(values * values, axis=0, keepdims=True) + EPSILON)


def rms_backward(grad_normed, values, inverse, gain):
    scaled = grad_normed * gain
    centre = jnp.mean(scaled * values, axis=0, keepdims=True)
    grad_values = inverse * scaled - values * (inverse * inverse * inverse * centre)
    product = grad_normed * values * inverse
    partial = product[:, :128]
    for start in range(128, product.shape[1], 128):
        partial = partial + product[:, start : start + 128]
    return grad_values, partial


def causal(block):
    rows = lax.broadcasted_iota(jnp.int32, block.shape, 0)
    columns = lax.broadcasted_iota(jnp.int32, block.shape, 1)
    return rows <= columns


def tile_start(j):
    return j * (j + 1) // 2 * TILE


def lanes(tiles):
    full = [(j, k) for j in range(tiles) for k in range(j + 1)]
    sides = [[(side, j, k) for j, k in full] for side in range(2)]
    for j in reversed(range(tiles)):
        side = min(sides, key=len)
        side += [(2, j, k) for k in range(j + 1)]
    return list(zip(*sides))


def train_kernel(
    heads,
    hidden,
    place,
    series_ids,
    median,
    scale,
    raw,
    cotangent,
    own_gains,
    own_qkv,
    own_out,
    own_gate_up,
    own_down_t,
    other_gains,
    other_qkv,
    other_out,
    other_gate_up,
    other_down_t,
    cosine,
    sine,
    kept_out,
    kept_grad,
    sent_out,
    sent_grad,
    own_total,
    other_total,
    gains,
    qkv_t,
    out_t,
    gate_up_t,
    down_t,
    qkv_w,
    out_w,
    gate_up_w,
    down_w,
    grad_gains,
    grad_qkv,
    grad_out,
    grad_gate_up,
    grad_down,
    inputs,
    inverse1,
    normed,
    queries,
    keys,
    values,
    rows_major,
    exponents,
    attended32,
    reciprocal,
    attended,
    residual,
    inverse2,
    mid,
    gate_up,
    activated,
    grad,
    grad_low,
    grad_pre,
    grad_res_low,
    grad_att,
    grad_q,
    grad_k,
    grad_v,
    grad_proj,
    flipped,
):
    step = pl.program_id(0)
    section = place[0]
    series = place[1] + step
    number = series_ids[series]
    centre = median[number]
    inverse_spread = 1.0 / scale[number]
    width, length = inputs.shape[1:]
    tiles = length // TILE
    query_factor = HEAD**-0.5 * LOG2E

    @pl.when(step == 0)
    def _():
        for ref in (grad_gains, grad_qkv, grad_out, grad_gate_up, grad_down):
            ref[...] = jnp.zeros_like(ref)
        row = lax.broadcasted_iota(jnp.int32, (2, heads, HEAD, length), 2)
        values[:, :, HEAD:, :] = jnp.where(row < 2, 1.0, 0.0).astype(bfloat)
        turned = lambda w: w.astype(single).T.astype(bfloat)
        for l, (gain, qkv, out, both, down) in (
            (section, (own_gains, own_qkv, own_out, own_gate_up, own_down_t)),
            (1 - section, (other_gains, other_qkv, other_out, other_gate_up, other_down_t)),
        ):
            for part in range(2):
                row = jnp.broadcast_to(gain[part : part + 1, :], (128, width))
                gains[l, part] = row.T
            qkv_w[l] = qkv[...]
            qkv_t[l] = turned(qkv[...])
            out_w[l] = out[...]
            out_t[l] = turned(out[...])
            gate_up_w[l] = both[...]
            gate_up_t[l] = turned(both[...])
            down_t[l] = down[...]
            down_w[l] = turned(down[...])

    def gain_of(l, part):
        return jnp.concatenate([gains[l, part]] * (TILE // 128), axis=1)

    inputs[0] = (raw[0].astype(single) - centre) * inverse_spread
    grad[...] = cotangent[0].astype(single)

    def rotated(block, cs, sign):
        a, b = block[:, :HALF], block[:, HALF:]
        cos, sin = cosine[:, cs], sine[:, cs] * sign
        return jnp.concatenate([a * cos - b * sin, b * cos + a * sin], axis=1)

    def forward(l, carry):
        largest = jnp.zeros((1, 1, TILE), single)
        largest_q = jnp.zeros((heads, 1, TILE), single)
        largest_k = jnp.zeros((heads, 1, TILE), single)
        for c in range(tiles):
            cs = slice(c * TILE, (c + 1) * TILE)
            u = inputs[l, :, cs]
            inv = rms_scale(u)
            inverse1[l, :, cs] = inv
            low = (u * inv * gain_of(l, 0)).astype(bfloat)
            normed[l, :, cs] = low
            projected = dot(qkv_t[l], low).reshape(3 * heads, HEAD, TILE)
            q = (rotated(projected[:heads], cs, 1.0) * query_factor).astype(bfloat)
            k = rotated(projected[heads : 2 * heads], cs, 1.0)
            queries[l, :, :, cs] = q
            keys[l, :, :, cs] = k.astype(bfloat)
            values[l, :, :HEAD, cs] = projected[2 * heads :].astype(bfloat)
            for h in range(heads):
                rows_major[h, cs, :HEAD] = k[h].T.astype(bfloat)
            q32 = q.astype(single)
            k32 = k.astype(bfloat).astype(single)
            largest_q = jnp.maximum(largest_q, jnp.sum(q32 * q32, axis=1, keepdims=True))
            largest_k = jnp.maximum(largest_k, jnp.sum(k32 * k32, axis=1, keepdims=True))
        bound = jnp.max(jnp.max(largest_q, axis=2) * jnp.max(largest_k, axis=2))

        def finish(h, j, total):
            js = slice(j * TILE, (j + 1) * TILE)
            inverse = 1.0 / total[HEAD : HEAD + 1]
            out = total[:HEAD] * inverse
            reciprocal[l, h, :, js] = inverse
            attended32[l, h, :, js] = out
            attended[l, h, :, js] = out.astype(bfloat)

        small = bound <= 1e4

        @pl.when(small)
        def _():
            pairs = lanes(tiles)
            ahead = 3

            def some(three, carry):
                scores = {}

                def score(m):
                    for side, (g, j, k) in enumerate(pairs[m]):
                        scores[m, side] = dot(
                            rows_major[three * 3 + g, k * TILE : (k + 1) * TILE, :HEAD],
                            queries[l, three * 3 + g, :, j * TILE : (j + 1) * TILE],
                        )

                for m in range(ahead):
                    score(m)
                totals = {}
                for m, pair in enumerate(pairs):
                    if m + ahead < len(pairs):
                        score(m + ahead)
                    ready = []
                    for side, (g, j, k) in enumerate(pair):
                        e = jnp.exp2(scores.pop((m, side)))
                        if k == j:
                            e = jnp.where(causal(e), e, 0.0)
                        e = e.astype(bfloat)
                        first = tile_start(j) + k * TILE
                        exponents[l, three * 3 + g, first : first + TILE, :] = e.T
                        ready.append(e)
                    for side, (g, j, k) in enumerate(pair):
                        h = three * 3 + g
                        part = dot(values[l, h, :, k * TILE : (k + 1) * TILE], ready[side])
                        totals[g, j] = totals[g, j] + part if k else part
                        if k == j:
                            finish(h, j, totals.pop((g, j)))
                return carry

            lax.fori_loop(0, heads // 3, some, 0)

        @pl.when(jnp.logical_not(small))
        def _():
            def one(h, carry):
                for j in range(tiles):
                    count = (j + 1) * TILE
                    js = slice(j * TILE, (j + 1) * TILE)
                    score = dot(rows_major[h, :count, :HEAD], queries[l, h, :, js])
                    rows = lax.broadcasted_iota(jnp.int32, score.shape, 0)
                    columns = lax.broadcasted_iota(jnp.int32, score.shape, 1) + j * TILE
                    score = jnp.where(rows <= columns, score, -1e30)
                    e = jnp.exp2(score - jnp.max(score, axis=0, keepdims=True)).astype(bfloat)
                    for k in range(j + 1):
                        first = tile_start(j) + k * TILE
                        exponents[l, h, first : first + TILE, :] = e[k * TILE : (k + 1) * TILE].T
                    finish(h, j, dot(values[l, h, :, :count], e))
                return carry

            lax.fori_loop(0, heads, one, 0)

        for c in range(tiles):
            cs = slice(c * TILE, (c + 1) * TILE)
            res = inputs[l, :, cs] + dot(out_t[l], attended[l, :, :, cs].reshape(width, TILE))
            residual[l, :, cs] = res
            inv = rms_scale(res)
            inverse2[l, :, cs] = inv
            low = (res * inv * gain_of(l, 1)).astype(bfloat)
            mid[l, :, cs] = low
            both = dot(gate_up_t[l], low)
            gate_up[l, :, cs] = both
            gate, up = both[:hidden], both[hidden:]
            act = (gate * jax.nn.sigmoid(gate) * up).astype(bfloat)
            activated[l, :, cs] = act
            result = res + dot(down_t[l], act)
            low = result.astype(bfloat)

            @pl.when(l == section)
            def _():
                kept_out[0, :, cs] = low

            @pl.when(l != section)
            def _():
                sent_out[0, :, cs] = low

            @pl.when(l == 0)
            def _():
                inputs[1, :, cs] = low.astype(single)

        return carry

    lax.fori_loop(0, 2, forward, 0)

    def backward(turn, carry):
        l = 1 - turn
        slot = lax.rem(l + section, 2)
        for c in range(tiles):
            cs = slice(c * TILE, (c + 1) * TILE)
            g = grad[:, cs]
            low = g.astype(bfloat)
            grad_low[:, cs] = low
            grad_act = dot(down_w[l], low)
            gate, up = gate_up[l, :hidden, cs], gate_up[l, hidden:, cs]
            sig = jax.nn.sigmoid(gate)
            inner = grad_act * sig
            grad_gate = inner * up * (1.0 + gate * (1.0 - sig))
            grad_up = inner * gate
            pre = jnp.concatenate([grad_gate, grad_up], axis=0).astype(bfloat)
            grad_pre[:, cs] = pre
            grad_mid = dot(gate_up_w[l], pre)
            res, inv = residual[l, :, cs], inverse2[l, :, cs]
            grad_res, partial = rms_backward(grad_mid, res, inv, gain_of(l, 1))
            grad_gains[slot, 1] += partial
            grad_res = grad_res + g
            grad[:, cs] = grad_res
            low = grad_res.astype(bfloat)
            grad_res_low[:, cs] = low
            back = dot(out_w[l], low).astype(bfloat).astype(single).reshape(heads, HEAD, TILE)
            inverse = reciprocal[l, :, :, cs]
            mean = jnp.sum(back * attended32[l, :, :, cs], axis=1, keepdims=True) * -inverse
            coarse = mean.astype(bfloat).astype(single)
            row = lax.broadcasted_iota(jnp.int32, (heads, HEAD, TILE), 1)
            extra = jnp.where(row == 0, coarse, jnp.where(row == 1, mean - coarse, 0.0))
            grad_att[:, :, cs] = jnp.concatenate([back * inverse, extra], axis=1).astype(bfloat)
        grad_down[slot] += dot_nt(grad_low[...], activated[l])
        grad_gate_up[slot] += dot_nt(mid[l], grad_pre[...])
        grad_out[slot] += dot_nt(attended[l].reshape(width, length), grad_res_low[...])

        for h in range(heads):
            rows_major[h] = grad_att[h].astype(single).T.astype(bfloat)

        pairs = lanes(tiles)
        ahead = 2
        half = TILE // 2

        def some(three, carry):
            products, held, sums = {}, {}, {}

            def product(m, part):
                if m < len(pairs):
                    for side, (g, j, k) in enumerate(pairs[m]):
                        first = j * TILE + part * half
                        products[m, side, part] = dot(
                            rows_major[three * 3 + g, first : first + half, :],
                            values[l, three * 3 + g, :, k * TILE : (k + 1) * TILE],
                        )

            def add(name, index, side, g, value):
                key = name, g, index, side
                sums[key] = sums[key] + value if key in sums else value

            for m in range(ahead):
                product(m, 0)
                product(m, 1)
            for m in range(len(pairs) + 1):
                now = pairs[m] if m < len(pairs) else ()
                before = pairs[m - 1] if m > 0 else ()
                product(m + ahead, 0)
                exps = []
                for side, (g, j, k) in enumerate(now):
                    first = tile_start(j) + k * TILE
                    e = exponents[l, three * 3 + g, first : first + TILE, :]
                    parts = [
                        e[p * half : (p + 1) * half] * products.pop((m, side, p)).astype(bfloat)
                        for p in range(2)
                    ]
                    grad_score = jnp.concatenate(parts, axis=0)
                    flipped[m % 2, side] = grad_score.T
                    held[m, side] = grad_score
                    exps.append(e)
                for side, (g, j, k) in enumerate(now):
                    js = slice(j * TILE, (j + 1) * TILE)
                    add("v", k, side, g, dot(grad_att[three * 3 + g, :HEAD, js], exps[side]))
                product(m + ahead, 1)
                for side, (g, j, k) in enumerate(before):
                    js = slice(j * TILE, (j + 1) * TILE)
                    grad_score = held.pop((m - 1, side))
                    add("k", k, side, g, dot(queries[l, three * 3 + g, :, js], grad_score))
                for side, (g, j, k) in enumerate(before):
                    ks = slice(k * TILE, (k + 1) * TILE)
                    turned = flipped[(m - 1) % 2, side]
                    add("q", j, side, g, dot(keys[l, three * 3 + g, :, ks], turned))
            for g in range(3):
                for name, ref in (("q", grad_q), ("k", grad_k), ("v", grad_v)):
                    for t in range(tiles):
                        found = [sums[name, g, t, n] for n in range(2) if (name, g, t, n) in sums]
                        ref[three * 3 + g, :, t * TILE : (t + 1) * TILE] = sum(found[1:], found[0])
            return carry

        lax.fori_loop(0, heads // 3, some, 0)

        for c in range(tiles):
            cs = slice(c * TILE, (c + 1) * TILE)
            dq = rotated(grad_q[:, :, cs] * HEAD**-0.5, cs, -1.0)
            dk = rotated(grad_k[:, :, cs] * (1.0 / LOG2E), cs, -1.0)
            low = jnp.concatenate([dq, dk, grad_v[:, :, cs]], axis=0).astype(bfloat)
            low = low.reshape(3 * width, TILE)
            grad_proj[:, cs] = low
            grad_normed = dot(qkv_w[l], low)
            u, inv = inputs[l, :, cs], inverse1[l, :, cs]
            grad_u, partial = rms_backward(grad_normed, u, inv, gain_of(l, 0))
            grad_gains[slot, 0] += partial
            grad_u = grad_u + grad[:, cs]
            grad[:, cs] = grad_u.astype(bfloat).astype(single)
            grad_u = grad_u * jnp.where(l == 0, inverse_spread, 1.0)

            @pl.when(l == section)
            def _():
                kept_grad[0, :, cs] = grad_u

            @pl.when(l != section)
            def _():
                sent_grad[0, :, cs] = grad_u.astype(bfloat)

        grad_qkv[slot] += dot_nt(normed[l], grad_proj[...])
        return carry

    lax.fori_loop(0, 2, backward, 0)

    @pl.when(step == pl.num_programs(0) - 1)
    def _():
        for slot, total in ((0, own_total), (1, other_total)):
            blocks = []
            for ref in (grad_gate_up, grad_down, grad_qkv, grad_out):
                blocks += [ref[slot, :, n : n + 128] for n in range(0, ref.shape[2] - 127, 128)]
            lane = lax.broadcasted_iota(jnp.int32, (width, 128), 1)
            spare = grad_qkv[slot, :, 3 * width - QKV_REST :]
            out_rest = grad_out[slot, :, width - OUT_REST :]
            columns = [jnp.sum(grad_gains[slot, n], axis=1, keepdims=True) for n in range(2)]
            rest = jnp.concatenate(
                [spare, out_rest] + columns
                + [jnp.zeros((width, 128 - QKV_REST - OUT_REST - 2), single)],
                axis=1,
            )
            blocks.append(rest)
            for n, block in enumerate(blocks):
                total[n * width : (n + 1) * width, :] = block.astype(total.dtype)
            used = len(blocks) * width
            total[used:, :] = jnp.zeros((total.shape[0] - used, 128), total.dtype)


def rotary_tables(length):
    frequency = 10000.0 ** (-np.arange(HALF, dtype=np.float64) / HALF)
    frequency = frequency.astype(np.float32)
    angles = np.arange(length, dtype=np.float32)[None, :] * frequency[:, None]
    return np.cos(angles).astype(np.float32), np.sin(angles).astype(np.float32)


def train(section, rows, raw, series_ids, median, scale, cotangent, own, other):
    count = raw.shape[0] // 2
    width, length = raw.shape[1:]
    heads = width // HEAD
    hidden = own[4].shape[1]
    place = jnp.stack([section, section * count]).astype(jnp.int32)
    cosine, sine = rotary_tables(length)
    operands = (raw, cotangent) + own + other + (jnp.asarray(cosine), jnp.asarray(sine))
    smem = pl.BlockSpec(memory_space=pltpu.SMEM)

    def whole(array):
        zeros = (0,) * len(array.shape)
        return pl.BlockSpec(
            array.shape, lambda i, *_: zeros, pipeline_mode=pl.Buffered(buffer_count=1)
        )

    placed_block = pl.BlockSpec((1, width, length), lambda i, place, ids: (place[1] + i, 0, 0))
    block = pl.BlockSpec((1, width, length), lambda i, *_: (i, 0, 0))
    shape = jax.ShapeDtypeStruct
    totals = (shape((rows, 128), single), shape((rows, 128), bfloat))
    pairs = length // TILE * (length // TILE + 1) // 2
    v = pltpu.VMEM
    scratch = [
        v((2, 2, width, 128), single),
        v((2, 3 * width, width), bfloat),
        v((2, width, width), bfloat),
        v((2, 2 * hidden, width), bfloat),
        v((2, width, hidden), bfloat),
        v((2, width, 3 * width), bfloat),
        v((2, width, width), bfloat),
        v((2, width, 2 * hidden), bfloat),
        v((2, hidden, width), bfloat),
        v((2, 2, width, 128), single),
        v((2, width, 3 * width), single),
        v((2, width, width), single),
        v((2, width, 2 * hidden), single),
        v((2, width, hidden), single),
        v((2, width, length), single),
        v((2, 1, length), single),
        v((2, width, length), bfloat),
        v((2, heads, HEAD, length), bfloat),
        v((2, heads, HEAD, length), bfloat),
        v((2, heads, 2 * HEAD, length), bfloat),
        v((heads, length, 2 * HEAD), bfloat),
        v((2, heads, pairs * TILE, TILE), bfloat),
        v((2, heads, HEAD, length), single),
        v((2, heads, 1, length), single),
        v((2, heads, HEAD, length), bfloat),
        v((2, width, length), single),
        v((2, 1, length), single),
        v((2, width, length), bfloat),
        v((2, 2 * hidden, length), single),
        v((2, hidden, length), bfloat),
        v((width, length), single),
        v((width, length), bfloat),
        v((2 * hidden, length), bfloat),
        v((width, length), bfloat),
        v((heads, 2 * HEAD, length), bfloat),
        v((heads, HEAD, length), single),
        v((heads, HEAD, length), single),
        v((heads, HEAD, length), single),
        v((3 * width, length), bfloat),
        v((2, 2, TILE, TILE), bfloat),
    ]
    return pl.pallas_call(
        functools.partial(train_kernel, heads, hidden),
        grid_spec=pltpu.PrefetchScalarGridSpec(
            num_scalar_prefetch=2,
            grid=(count,),
            in_specs=[smem, smem, placed_block, placed_block] + [whole(a) for a in operands[2:]],
            out_specs=[placed_block, placed_block, block, block] + [whole(t) for t in totals],
            scratch_shapes=scratch,
        ),
        out_shape=(
            shape(raw.shape, bfloat),
            shape(raw.shape, single),
            shape((count, width, length), bfloat),
            shape((count, width, length), bfloat),
        )
        + totals,
        compiler_params=pltpu.CompilerParams(vmem_limit_bytes=64 * 2**20 - 2**16),
    )(place, series_ids, median, scale, *operands)


def partner():
    return {"section": 1 - lax.axis_index("section")}


def meet(peers):
    barrier = pltpu.get_barrier_semaphore()
    for peer in peers:
        pl.semaphore_signal(barrier, inc=1, device_id=peer, device_id_type=MESH)
    pl.semaphore_wait(barrier, len(peers))


def swap_kernel(count, *refs):
    own, other, send, recv = refs[:count], refs[count : 2 * count], refs[-2], refs[-1]
    meet([partner()])
    copies = [
        pltpu.make_async_remote_copy(
            src_ref=own[n],
            dst_ref=other[n],
            send_sem=send.at[n],
            recv_sem=recv.at[n],
            device_id=partner(),
            device_id_type=MESH,
        )
        for n in range(count)
    ]
    for copy in copies:
        copy.start()
    for copy in copies:
        copy.wait()


def swap_weights(weights):
    count = len(weights)
    anywhere = pl.BlockSpec(memory_space=pl.ANY)
    return pl.pallas_call(
        functools.partial(swap_kernel, count),
        out_shape=tuple(jax.ShapeDtypeStruct(w.shape, w.dtype) for w in weights),
        in_specs=[anywhere] * count,
        out_specs=[anywhere] * count,
        scratch_shapes=[pltpu.SemaphoreType.DMA((count,)), pltpu.SemaphoreType.DMA((count,))],
        compiler_params=pltpu.CompilerParams(collective_id=0, has_side_effects=True),
    )(*weights)


def group_sizes(devices):
    sizes = []
    while devices > 1:
        size = 4 if devices % 4 == 0 else devices
        sizes.append(size)
        devices //= size
    return sizes


def reduce_kernel(
    sizes,
    own_total,
    other_total,
    sent_out,
    sent_grad,
    far_out,
    far_grad,
    grad_gains,
    grad_qkv,
    grad_out,
    grad_gate_up,
    grad_down,
    arrived,
    *scratch,
):
    count = len(sizes)
    parts = scratch[:count]
    slots = scratch[count : 2 * count]
    wholes = scratch[2 * count : 3 * count]
    last, swap_send, swap_recv, sum_send, sum_recv, gather_send, gather_recv = scratch[3 * count :]
    me = lax.axis_index("dp")
    places, groups = [], []
    stride = 1
    for size in sizes:
        place = lax.rem(lax.div(me, stride), size)
        peers = []
        for turn in range(1, size):
            other = lax.rem(place + turn, size)
            peers.append((other, {"dp": me + (other - place) * stride}))
        places.append(place)
        groups.append(peers)
        stride *= size
    meet([partner()] + [device for peers in groups for _, device in peers])

    def copy(source, target, send, recv, device):
        c = pltpu.make_async_remote_copy(
            src_ref=source,
            dst_ref=target,
            send_sem=send,
            recv_sem=recv,
            device_id=device,
            device_id_type=MESH,
        )
        c.start()
        return c

    near = copy(other_total, arrived, swap_send.at[0], swap_recv.at[0], partner())
    far = [
        copy(sent_out, far_out, swap_send.at[1], swap_recv.at[1], partner()),
        copy(sent_grad, far_grad, swap_send.at[2], swap_recv.at[2], partner()),
    ]
    near.wait()
    parts[0][...] = (own_total[...] + arrived[...].astype(single)).astype(bfloat)
    first = 0
    starts = []
    for n, size in enumerate(sizes):
        chunk = parts[n].shape[0] // size
        copies = []
        for turn, (other, device) in enumerate(groups[n]):
            copies.append(
                copy(
                    parts[n].at[pl.ds(pl.multiple_of(other * chunk, 16), chunk)],
                    slots[n].at[turn],
                    sum_send.at[first + turn],
                    sum_recv.at[first + turn],
                    device,
                )
            )
        total = parts[n][pl.ds(pl.multiple_of(places[n] * chunk, 16), chunk), :].astype(single)
        for turn, c in enumerate(copies):
            c.wait()
            total = total + slots[n][turn].astype(single)
        target = parts[n + 1] if n + 1 < count else last
        target[...] = total.astype(bfloat)
        starts.append(first)
        first += size - 1
    source = last
    for n in reversed(range(count)):
        chunk = parts[n].shape[0] // sizes[n]
        mine = pl.ds(pl.multiple_of(places[n] * chunk, 16), chunk)
        copies = []
        for turn, (_, device) in enumerate(groups[n]):
            k = starts[n] + turn
            copies.append(
                copy(source, wholes[n].at[mine], gather_send.at[k], gather_recv.at[k], device)
            )
        wholes[n][mine, :] = source[...]
        for c in copies:
            c.wait()
        source = wholes[n]
    width = grad_qkv.shape[0]
    block = 0
    for ref in (grad_gate_up, grad_down, grad_qkv, grad_out):
        for n in range(0, ref.shape[1] - 127, 128):
            ref[:, n : n + 128] = source[block * width : (block + 1) * width, :].astype(single)
            block += 1
    rest = source[block * width : (block + 1) * width, :].astype(single)
    grad_qkv[:, 3 * width - QKV_REST :] = rest[:, :QKV_REST]
    grad_out[:, width - OUT_REST :] = rest[:, QKV_REST : QKV_REST + OUT_REST]
    grad_gains[...] = rest.T[QKV_REST + OUT_REST : QKV_REST + OUT_REST + 2, :]
    for c in far:
        c.wait()


def reduce(devices, own_total, other_total, sent_out, sent_grad, width, hidden):
    sizes = group_sizes(devices)
    rows = own_total.shape[0]
    v = pltpu.VMEM
    shape = jax.ShapeDtypeStruct
    parts, slots, left = [], [], rows
    for size in sizes:
        parts.append(v((left, 128), bfloat))
        left //= size
        slots.append(v((size - 1, left, 128), bfloat))
    links = sum(size - 1 for size in sizes)
    dma = pltpu.SemaphoreType.DMA
    anywhere = pl.BlockSpec(memory_space=pl.ANY)
    vmem = pl.BlockSpec(memory_space=pltpu.VMEM)
    return pl.pallas_call(
        functools.partial(reduce_kernel, sizes),
        out_shape=(
            shape(sent_out.shape, bfloat),
            shape(sent_grad.shape, bfloat),
            shape((2, width), single),
            shape((width, 3 * width), single),
            shape((width, width), single),
            shape((width, 2 * hidden), single),
            shape((width, hidden), single),
        ),
        in_specs=[vmem, vmem, anywhere, anywhere],
        out_specs=[anywhere, anywhere] + [vmem] * 5,
        scratch_shapes=[v((rows, 128), bfloat)]
        + parts
        + slots
        + parts
        + [v((left, 128), bfloat), dma((3,)), dma((3,))]
        + [dma((links,))] * 4,
        compiler_params=pltpu.CompilerParams(
            collective_id=1, has_side_effects=True, vmem_limit_bytes=40 * 2**20
        ),
    )(own_total, other_total, sent_out, sent_grad)


def on_device(
    devices,
    raw,
    series_ids,
    median,
    scale,
    cotangent,
    norm_gains,
    qkv_weight,
    out_weight,
    gate_up_weight,
    down_weight,
):
    section = lax.axis_index("section")
    turned = lambda a: jnp.swapaxes(a, -1, -2)
    count = raw.shape[0] // 2
    width, hidden = raw.shape[2], down_weight.shape[1]
    own = (norm_gains[0], qkv_weight[0], out_weight[0], gate_up_weight[0], turned(down_weight[0]))
    other = swap_weights(own)
    blocks = 14
    rows = -(-blocks * width // (16 * devices)) * 16 * devices
    kept_out, kept_grad, sent_out, sent_grad, own_total, other_total = train(
        section, rows, turned(raw), series_ids, median, scale, turned(cotangent), own, other
    )
    far_out, far_grad, gain, qkv, out, gate_up, down = reduce(
        devices, own_total, other_total, sent_out, sent_grad, width, hidden
    )
    place = ((1 - section) * count, 0, 0)
    layer_outputs = lax.dynamic_update_slice(kept_out, far_out, place)
    input_grads = lax.dynamic_update_slice(kept_grad, far_grad.astype(single), place)
    return (
        turned(layer_outputs)[None],
        turned(input_grads)[None],
        gain[None],
        qkv[None],
        out[None],
        gate_up[None],
        turned(down)[None],
    )


def solution(mesh):
    placed = (
        P("dp", None, None),
        P("dp"),
        P(),
        P(),
        P("dp", None, None),
        P("section", None, None),
        P("section", None, None),
        P("section", None, None),
        P("section", None, None),
        P("section", None, None),
    )
    return jax.shard_map(
        functools.partial(on_device, mesh.shape["dp"]),
        mesh=mesh,
        in_specs=placed,
        out_specs=(
            P("section", "dp", None, None),
            P("section", "dp", None, None),
            P("section", None, None),
            P("section", None, None),
            P("section", None, None),
            P("section", None, None),
            P("section", None, None),
        ),
        check_vma=False,
    )
```

```python
import functools
import math

import jax
import jax.numpy as jnp
import numpy as np
from jax import lax
from jax.experimental import pallas as pl
from jax.experimental.pallas import tpu as pltpu
from jax.sharding import PartitionSpec as P

HEAD = 16
HALF = HEAD // 2
TILE = 256
CHUNK = 512
EPSILON = 1e-06
LOG2E = math.log2(math.e)
QKV_REST = 48
OUT_REST = 16
MESH = pl.DeviceIdType.MESH
bfloat = jnp.bfloat16
single = jnp.float32


def dot(left, right):
    return jnp.dot(left, right, preferred_element_type=single)


def dot_nt(left, right):
    return lax.dot_general(left, right, (((1,), (1,)), ((), ())), preferred_element_type=single)


def rms_scale(values):
    return lax.rsqrt(jnp.mean(values * values, axis=0, keepdims=True) + EPSILON)


def rms_backward(grad_normed, values, inverse, gain):
    scaled = grad_normed * gain
    centre = jnp.mean(scaled * values, axis=0, keepdims=True)
    grad_values = inverse * scaled - values * (inverse * inverse * inverse * centre)
    product = grad_normed * values * inverse
    partial = product[:, :128]
    for start in range(128, product.shape[1], 128):
        partial = partial + product[:, start : start + 128]
    return grad_values, partial


def causal(block):
    rows = lax.broadcasted_iota(jnp.int32, block.shape, 0)
    columns = lax.broadcasted_iota(jnp.int32, block.shape, 1)
    return rows <= columns


def tile_start(j):
    return j * (j + 1) // 2 * TILE


def lanes(tiles):
    full = [(j, k) for j in range(tiles) for k in range(j + 1)]
    sides = [[(side, j, k) for j, k in full] for side in range(2)]
    for j in reversed(range(tiles)):
        side = min(sides, key=len)
        side += [(2, j, k) for k in range(j + 1)]
    return list(zip(*sides))


def train_kernel(
    heads,
    hidden,
    place,
    series_ids,
    median,
    scale,
    raw,
    cotangent,
    own_gains,
    own_qkv,
    own_out,
    own_gate_up,
    own_down_t,
    other_gains,
    other_qkv,
    other_out,
    other_gate_up,
    other_down_t,
    tables,
    kept_out,
    kept_grad,
    sent_out,
    sent_grad,
    own_total,
    other_total,
    gains,
    qkv_t,
    out_t,
    gate_up_t,
    down_t,
    qkv_w,
    out_w,
    gate_up_w,
    down_w,
    grad_gains,
    grad_qkv,
    grad_out,
    grad_gate_up,
    grad_down,
    inputs,
    inverse1,
    normed,
    queries,
    keys,
    values,
    rows_major,
    exponents,
    attended32,
    reciprocal,
    attended,
    residual,
    inverse2,
    mid,
    gate_up,
    activated,
    grad,
    grad_low,
    grad_pre,
    grad_res_low,
    grad_att,
    grad_q,
    grad_k,
    grad_v,
    grad_proj,
    flipped,
    grad_inputs,
):
    step = pl.program_id(0)
    section = place[0]
    series = place[1] + step
    number = series_ids[series]
    centre = median[number]
    inverse_spread = 1.0 / scale[number]
    width, length = inputs.shape[1:]
    tiles = length // TILE
    chunks = [slice(n, n + CHUNK) for n in range(0, length, CHUNK)]

    @pl.when(step == 0)
    def _():
        for ref in (grad_gains, grad_qkv, grad_out, grad_gate_up, grad_down):
            ref[...] = jnp.zeros_like(ref)
        row = lax.broadcasted_iota(jnp.int32, (2, heads, HEAD, length), 2)
        values[:, :, HEAD:, :] = jnp.where(row < 2, 1.0, 0.0).astype(bfloat)
        turned = lambda w: w.astype(single).T.astype(bfloat)
        for l, (gain, qkv, out, both, down) in (
            (section, (own_gains, own_qkv, own_out, own_gate_up, own_down_t)),
            (1 - section, (other_gains, other_qkv, other_out, other_gate_up, other_down_t)),
        ):
            for part in range(2):
                row = jnp.broadcast_to(gain[part : part + 1, :], (128, width))
                gains[l, part] = row.T
            qkv_w[l] = qkv[...]
            qkv_t[l] = turned(qkv[...])
            out_w[l] = out[...]
            out_t[l] = turned(out[...])
            gate_up_w[l] = both[...]
            gate_up_t[l] = turned(both[...])
            down_t[l] = down[...]
            down_w[l] = turned(down[...])

    def gain_of(l, part):
        return jnp.concatenate([gains[l, part]] * (CHUNK // 128), axis=1)

    inputs[0] = (raw[0].astype(single) - centre) * inverse_spread
    grad[...] = cotangent[0].astype(single)

    def rotated(block, cos, sin):
        a, b = block[:, :HALF], block[:, HALF:]
        return jnp.concatenate([a * cos - b * sin, b * cos + a * sin], axis=1)

    head_rows = lax.broadcasted_iota(jnp.int32, (HEAD, width), 0)
    head_columns = lax.broadcasted_iota(jnp.int32, (HEAD, width), 1)
    of_head = jnp.where(
        (head_columns >= head_rows * HEAD) & (head_columns < (head_rows + 1) * HEAD), 1.0, 0.0
    ).astype(bfloat)

    def forward(l, carry):
        largest_q = jnp.zeros((HEAD, CHUNK), single)
        largest_k = jnp.zeros((HEAD, CHUNK), single)
        for cs in chunks:
            u = inputs[l, :, cs]
            inv = rms_scale(u)
            inverse1[l, :, cs] = inv
            low = (u * inv * gain_of(l, 0)).astype(bfloat)
            normed[l, :, cs] = low
            projected = dot(qkv_t[l], low).reshape(3 * heads, HEAD, CHUNK)
            q = rotated(projected[:heads], tables[2, :, cs], tables[3, :, cs])
            k = rotated(projected[heads : 2 * heads], tables[0, :, cs], tables[1, :, cs])
            queries[l, :, :, cs] = q.astype(bfloat)
            keys[l, :, :, cs] = k.astype(bfloat)
            values[l, :, :HEAD, cs] = projected[2 * heads :].astype(bfloat)
            for h in range(heads):
                rows_major[h, cs, :HEAD] = k[h].T.astype(bfloat)
            squares = lambda v: dot(of_head, (v * v).astype(bfloat).reshape(width, CHUNK))
            largest_q = jnp.maximum(largest_q, squares(q))
            largest_k = jnp.maximum(largest_k, squares(k))
        bound = jnp.max(
            jnp.max(largest_q, axis=1, keepdims=True) * jnp.max(largest_k, axis=1, keepdims=True)
        )

        def finish(h, j, total):
            js = slice(j * TILE, (j + 1) * TILE)
            inverse = 1.0 / total[HEAD : HEAD + 1]
            out = total[:HEAD] * inverse
            reciprocal[l, h, :, js] = inverse
            attended32[l, h, :, js] = out
            attended[l, h, :, js] = out.astype(bfloat)

        small = bound <= 1e4

        @pl.when(small)
        def _():
            pairs = lanes(tiles)
            ahead = 3

            def some(three, carry):
                scores = {}

                def score(m):
                    for side, (g, j, k) in enumerate(pairs[m]):
                        scores[m, side] = dot(
                            rows_major[three * 3 + g, k * TILE : (k + 1) * TILE, :HEAD],
                            queries[l, three * 3 + g, :, j * TILE : (j + 1) * TILE],
                        )

                for m in range(ahead):
                    score(m)
                totals = {}
                for m, pair in enumerate(pairs):
                    if m + ahead < len(pairs):
                        score(m + ahead)
                    ready = []
                    for side, (g, j, k) in enumerate(pair):
                        e = jnp.exp2(scores.pop((m, side)))
                        if k == j:
                            e = jnp.where(causal(e), e, 0.0)
                        e = e.astype(bfloat)
                        first = tile_start(j) + k * TILE
                        exponents[l, three * 3 + g, first : first + TILE, :] = e.T
                        ready.append(e)
                    for side, (g, j, k) in enumerate(pair):
                        h = three * 3 + g
                        part = dot(values[l, h, :, k * TILE : (k + 1) * TILE], ready[side])
                        totals[g, j] = totals[g, j] + part if k else part
                        if k == j:
                            finish(h, j, totals.pop((g, j)))
                return carry

            lax.fori_loop(0, heads // 3, some, 0)

        @pl.when(jnp.logical_not(small))
        def _():
            def one(h, carry):
                for j in range(tiles):
                    count = (j + 1) * TILE
                    js = slice(j * TILE, (j + 1) * TILE)
                    score = dot(rows_major[h, :count, :HEAD], queries[l, h, :, js])
                    rows = lax.broadcasted_iota(jnp.int32, score.shape, 0)
                    columns = lax.broadcasted_iota(jnp.int32, score.shape, 1) + j * TILE
                    score = jnp.where(rows <= columns, score, -1e30)
                    e = jnp.exp2(score - jnp.max(score, axis=0, keepdims=True)).astype(bfloat)
                    for k in range(j + 1):
                        first = tile_start(j) + k * TILE
                        exponents[l, h, first : first + TILE, :] = e[k * TILE : (k + 1) * TILE].T
                    finish(h, j, dot(values[l, h, :, :count], e))
                return carry

            lax.fori_loop(0, heads, one, 0)

        for cs in chunks:
            res = inputs[l, :, cs] + dot(out_t[l], attended[l, :, :, cs].reshape(width, CHUNK))
            residual[l, :, cs] = res
            inv = rms_scale(res)
            inverse2[l, :, cs] = inv
            low = (res * inv * gain_of(l, 1)).astype(bfloat)
            mid[l, :, cs] = low
            both = dot(gate_up_t[l], low)
            gate, up = both[:hidden], both[hidden:]
            sig = 0.5 * jnp.tanh(0.5 * gate) + 0.5
            swish = gate * sig
            gate_up[l, :hidden, cs] = up * (sig + swish * (1.0 - sig))
            gate_up[l, hidden:, cs] = swish
            act = (swish * up).astype(bfloat)
            activated[l, :, cs] = act
            result = res + dot(down_t[l], act)
            inputs[l + 1, :, cs] = result.astype(bfloat).astype(single)
        return carry

    lax.fori_loop(0, 2, forward, 0)

    def backward(turn, carry):
        l = 1 - turn
        slot = lax.rem(l + section, 2)
        for cs in chunks:
            g = grad[:, cs]
            low = g.astype(bfloat)
            grad_low[:, cs] = low
            grad_act = dot(down_w[l], low)
            pre = jnp.concatenate(
                [grad_act * gate_up[l, :hidden, cs], grad_act * gate_up[l, hidden:, cs]], axis=0
            ).astype(bfloat)
            grad_pre[:, cs] = pre
            grad_mid = dot(gate_up_w[l], pre)
            res, inv = residual[l, :, cs], inverse2[l, :, cs]
            grad_res, partial = rms_backward(grad_mid, res, inv, gain_of(l, 1))
            grad_gains[slot, 1] += partial
            grad_res = grad_res + g
            grad[:, cs] = grad_res
            low = grad_res.astype(bfloat)
            grad_res_low[:, cs] = low
            back = dot(out_w[l], low).astype(bfloat).astype(single).reshape(heads, HEAD, CHUNK)
            inverse = reciprocal[l, :, :, cs]
            mean = jnp.sum(back * attended32[l, :, :, cs], axis=1, keepdims=True) * -inverse
            coarse = mean.astype(bfloat).astype(single)
            row = lax.broadcasted_iota(jnp.int32, (heads, HALF, CHUNK), 1)
            extra = jnp.where(row == 0, coarse, jnp.where(row == 1, mean - coarse, 0.0))
            rest = jnp.zeros((heads, HALF, CHUNK), single)
            grad_att[:, :, cs] = jnp.concatenate([back * inverse, extra, rest], axis=1).astype(bfloat)
        grad_down[slot] += dot_nt(grad_low[...], activated[l])
        grad_gate_up[slot] += dot_nt(mid[l], grad_pre[...])
        grad_out[slot] += dot_nt(attended[l].reshape(width, length), grad_res_low[...])

        for h in range(heads):
            rows_major[h] = grad_att[h].astype(single).T.astype(bfloat)

        pairs = lanes(tiles)
        ahead = 2
        half = TILE // 2

        def some(three, carry):
            products, held, sums = {}, {}, {}

            def product(m, part):
                if m < len(pairs):
                    for side, (g, j, k) in enumerate(pairs[m]):
                        first = j * TILE + part * half
                        products[m, side, part] = dot(
                            rows_major[three * 3 + g, first : first + half, :],
                            values[l, three * 3 + g, :, k * TILE : (k + 1) * TILE],
                        )

            def add(name, index, side, g, value):
                key = name, g, index, side
                sums[key] = sums[key] + value if key in sums else value

            for m in range(ahead):
                product(m, 0)
                product(m, 1)
            for m in range(len(pairs) + 1):
                now = pairs[m] if m < len(pairs) else ()
                before = pairs[m - 1] if m > 0 else ()
                product(m + ahead, 0)
                exps = []
                for side, (g, j, k) in enumerate(now):
                    first = tile_start(j) + k * TILE
                    e = exponents[l, three * 3 + g, first : first + TILE, :]
                    parts = [
                        e[p * half : (p + 1) * half] * products.pop((m, side, p)).astype(bfloat)
                        for p in range(2)
                    ]
                    grad_score = jnp.concatenate(parts, axis=0)
                    flipped[m % 2, side] = grad_score.T
                    held[m, side] = grad_score
                    exps.append(e)
                for side, (g, j, k) in enumerate(now):
                    js = slice(j * TILE, (j + 1) * TILE)
                    add("v", k, side, g, dot(grad_att[three * 3 + g, :HEAD, js], exps[side]))
                product(m + ahead, 1)
                for side, (g, j, k) in enumerate(before):
                    js = slice(j * TILE, (j + 1) * TILE)
                    grad_score = held.pop((m - 1, side))
                    add("k", k, side, g, dot(queries[l, three * 3 + g, :, js], grad_score))
                for side, (g, j, k) in enumerate(before):
                    ks = slice(k * TILE, (k + 1) * TILE)
                    turned = flipped[(m - 1) % 2, side]
                    add("q", j, side, g, dot(keys[l, three * 3 + g, :, ks], turned))
            for g in range(3):
                for name, ref in (("q", grad_q), ("k", grad_k), ("v", grad_v)):
                    for t in range(tiles):
                        found = [sums[name, g, t, n] for n in range(2) if (name, g, t, n) in sums]
                        ref[three * 3 + g, :, t * TILE : (t + 1) * TILE] = sum(found[1:], found[0])
            return carry

        lax.fori_loop(0, heads // 3, some, 0)

        for cs in chunks:
            dq = rotated(grad_q[:, :, cs], tables[4, :, cs], tables[5, :, cs])
            dk = rotated(grad_k[:, :, cs], tables[6, :, cs], tables[7, :, cs])
            low = jnp.concatenate([dq, dk, grad_v[:, :, cs]], axis=0).astype(bfloat)
            low = low.reshape(3 * width, CHUNK)
            grad_proj[:, cs] = low
            grad_normed = dot(qkv_w[l], low)
            u, inv = inputs[l, :, cs], inverse1[l, :, cs]
            grad_u, partial = rms_backward(grad_normed, u, inv, gain_of(l, 0))
            grad_gains[slot, 0] += partial
            grad_u = grad_u + grad[:, cs]
            grad[:, cs] = grad_u.astype(bfloat).astype(single)
            grad_inputs[l, :, cs] = grad_u
        grad_qkv[slot] += dot_nt(normed[l], grad_proj[...])
        return carry

    lax.fori_loop(0, 2, backward, 0)

    grad_inputs[0] = grad_inputs[0] * inverse_spread
    kept_out[0] = inputs[section + 1].astype(bfloat)
    sent_out[0] = inputs[2 - section].astype(bfloat)
    kept_grad[0] = grad_inputs[section]
    sent_grad[0] = grad_inputs[1 - section].astype(bfloat)

    @pl.when(step == pl.num_programs(0) - 1)
    def _():
        for slot, total in ((0, own_total), (1, other_total)):
            blocks = []
            for ref in (grad_gate_up, grad_down, grad_qkv, grad_out):
                blocks += [ref[slot, :, n : n + 128] for n in range(0, ref.shape[2] - 127, 128)]
            lane = lax.broadcasted_iota(jnp.int32, (width, 128), 1)
            spare = grad_qkv[slot, :, 3 * width - QKV_REST :]
            out_rest = grad_out[slot, :, width - OUT_REST :]
            columns = [jnp.sum(grad_gains[slot, n], axis=1, keepdims=True) for n in range(2)]
            rest = jnp.concatenate(
                [spare, out_rest] + columns
                + [jnp.zeros((width, 128 - QKV_REST - OUT_REST - 2), single)],
                axis=1,
            )
            blocks.append(rest)
            for n, block in enumerate(blocks):
                total[n * width : (n + 1) * width, :] = block.astype(total.dtype)
            used = len(blocks) * width
            total[used:, :] = jnp.zeros((total.shape[0] - used, 128), total.dtype)


def rotary_tables(length):
    frequency = 10000.0 ** (-np.arange(HALF, dtype=np.float64) / HALF)
    frequency = frequency.astype(np.float32)
    angles = np.arange(length, dtype=np.float32)[None, :] * frequency[:, None]
    cos, sin = np.cos(angles), np.sin(angles)
    query, grad_query, grad_key = HEAD**-0.5 * LOG2E, HEAD**-0.5, 1.0 / LOG2E
    tables = [cos, sin, cos * query, sin * query]
    tables += [cos * grad_query, -sin * grad_query, cos * grad_key, -sin * grad_key]
    return np.stack(tables).astype(np.float32)


def train(section, rows, raw, series_ids, median, scale, cotangent, own, other):
    count = raw.shape[0] // 2
    width, length = raw.shape[1:]
    heads = width // HEAD
    hidden = own[4].shape[1]
    place = jnp.stack([section, section * count]).astype(jnp.int32)
    tables = jnp.asarray(rotary_tables(length))
    operands = (raw, cotangent) + own + other + (tables,)
    smem = pl.BlockSpec(memory_space=pltpu.SMEM)

    def whole(array):
        zeros = (0,) * len(array.shape)
        return pl.BlockSpec(
            array.shape, lambda i, *_: zeros, pipeline_mode=pl.Buffered(buffer_count=1)
        )

    placed_block = pl.BlockSpec((1, width, length), lambda i, place, ids: (place[1] + i, 0, 0))
    block = pl.BlockSpec((1, width, length), lambda i, *_: (i, 0, 0))
    shape = jax.ShapeDtypeStruct
    totals = (shape((rows, 128), single), shape((rows, 128), bfloat))
    pairs = length // TILE * (length // TILE + 1) // 2
    v = pltpu.VMEM
    scratch = [
        v((2, 2, width, 128), single),
        v((2, 3 * width, width), bfloat),
        v((2, width, width), bfloat),
        v((2, 2 * hidden, width), bfloat),
        v((2, width, hidden), bfloat),
        v((2, width, 3 * width), bfloat),
        v((2, width, width), bfloat),
        v((2, width, 2 * hidden), bfloat),
        v((2, hidden, width), bfloat),
        v((2, 2, width, 128), single),
        v((2, width, 3 * width), single),
        v((2, width, width), single),
        v((2, width, 2 * hidden), single),
        v((2, width, hidden), single),
        v((3, width, length), single),
        v((2, 1, length), single),
        v((2, width, length), bfloat),
        v((2, heads, HEAD, length), bfloat),
        v((2, heads, HEAD, length), bfloat),
        v((2, heads, 2 * HEAD, length), bfloat),
        v((heads, length, 2 * HEAD), bfloat),
        v((2, heads, pairs * TILE, TILE), bfloat),
        v((2, heads, HEAD, length), single),
        v((2, heads, 1, length), single),
        v((2, heads, HEAD, length), bfloat),
        v((2, width, length), single),
        v((2, 1, length), single),
        v((2, width, length), bfloat),
        v((2, 2 * hidden, length), single),
        v((2, hidden, length), bfloat),
        v((width, length), single),
        v((width, length), bfloat),
        v((2 * hidden, length), bfloat),
        v((width, length), bfloat),
        v((heads, 2 * HEAD, length), bfloat),
        v((heads, HEAD, length), single),
        v((heads, HEAD, length), single),
        v((heads, HEAD, length), single),
        v((3 * width, length), bfloat),
        v((2, 2, TILE, TILE), bfloat),
        v((2, width, length), single),
    ]
    return pl.pallas_call(
        functools.partial(train_kernel, heads, hidden),
        grid_spec=pltpu.PrefetchScalarGridSpec(
            num_scalar_prefetch=2,
            grid=(count,),
            in_specs=[smem, smem, placed_block, placed_block] + [whole(a) for a in operands[2:]],
            out_specs=[placed_block, placed_block, block, block] + [whole(t) for t in totals],
            scratch_shapes=scratch,
        ),
        out_shape=(
            shape(raw.shape, bfloat),
            shape(raw.shape, single),
            shape((count, width, length), bfloat),
            shape((count, width, length), bfloat),
        )
        + totals,
        compiler_params=pltpu.CompilerParams(vmem_limit_bytes=64 * 2**20 - 2**16),
    )(place, series_ids, median, scale, *operands)


def partner():
    return {"section": 1 - lax.axis_index("section")}


def meet(peers):
    barrier = pltpu.get_barrier_semaphore()
    for peer in peers:
        pl.semaphore_signal(barrier, inc=1, device_id=peer, device_id_type=MESH)
    pl.semaphore_wait(barrier, len(peers))


def swap_kernel(count, *refs):
    own, other, send, recv = refs[:count], refs[count : 2 * count], refs[-2], refs[-1]
    meet([partner()])
    copies = [
        pltpu.make_async_remote_copy(
            src_ref=own[n],
            dst_ref=other[n],
            send_sem=send.at[n],
            recv_sem=recv.at[n],
            device_id=partner(),
            device_id_type=MESH,
        )
        for n in range(count)
    ]
    for copy in copies:
        copy.start()
    for copy in copies:
        copy.wait()


def swap_weights(weights):
    count = len(weights)
    anywhere = pl.BlockSpec(memory_space=pl.ANY)
    return pl.pallas_call(
        functools.partial(swap_kernel, count),
        out_shape=tuple(jax.ShapeDtypeStruct(w.shape, w.dtype) for w in weights),
        in_specs=[anywhere] * count,
        out_specs=[anywhere] * count,
        scratch_shapes=[pltpu.SemaphoreType.DMA((count,)), pltpu.SemaphoreType.DMA((count,))],
        compiler_params=pltpu.CompilerParams(collective_id=0, has_side_effects=True),
    )(*weights)


def group_sizes(devices):
    sizes = []
    while devices > 1:
        size = 4 if devices % 4 == 0 else devices
        sizes.append(size)
        devices //= size
    return sizes


def reduce_kernel(
    sizes,
    own_total,
    other_total,
    sent_out,
    sent_grad,
    far_out,
    far_grad,
    grad_gains,
    grad_qkv,
    grad_out,
    grad_gate_up,
    grad_down,
    arrived,
    *scratch,
):
    count = len(sizes)
    parts = scratch[:count]
    slots = scratch[count : 2 * count]
    wholes = scratch[2 * count : 3 * count]
    last, swap_send, swap_recv, sum_send, sum_recv, gather_send, gather_recv = scratch[3 * count :]
    me = lax.axis_index("dp")
    places, groups = [], []
    stride = 1
    for size in sizes:
        place = lax.rem(lax.div(me, stride), size)
        peers = []
        for turn in range(1, size):
            other = lax.rem(place + turn, size)
            peers.append((other, {"dp": me + (other - place) * stride}))
        places.append(place)
        groups.append(peers)
        stride *= size
    meet([partner()] + [device for peers in groups for _, device in peers])

    def copy(source, target, send, recv, device):
        c = pltpu.make_async_remote_copy(
            src_ref=source,
            dst_ref=target,
            send_sem=send,
            recv_sem=recv,
            device_id=device,
            device_id_type=MESH,
        )
        c.start()
        return c

    near = copy(other_total, arrived, swap_send.at[0], swap_recv.at[0], partner())
    far = [
        copy(sent_out, far_out, swap_send.at[1], swap_recv.at[1], partner()),
        copy(sent_grad, far_grad, swap_send.at[2], swap_recv.at[2], partner()),
    ]
    near.wait()
    parts[0][...] = (own_total[...] + arrived[...].astype(single)).astype(bfloat)
    first = 0
    starts = []
    for n, size in enumerate(sizes):
        chunk = parts[n].shape[0] // size
        copies = []
        for turn, (other, device) in enumerate(groups[n]):
            copies.append(
                copy(
                    parts[n].at[pl.ds(pl.multiple_of(other * chunk, 16), chunk)],
                    slots[n].at[turn],
                    sum_send.at[first + turn],
                    sum_recv.at[first + turn],
                    device,
                )
            )
        total = parts[n][pl.ds(pl.multiple_of(places[n] * chunk, 16), chunk), :].astype(single)
        for turn, c in enumerate(copies):
            c.wait()
            total = total + slots[n][turn].astype(single)
        target = parts[n + 1] if n + 1 < count else last
        target[...] = total.astype(bfloat)
        starts.append(first)
        first += size - 1
    source = last
    for n in reversed(range(count)):
        chunk = parts[n].shape[0] // sizes[n]
        mine = pl.ds(pl.multiple_of(places[n] * chunk, 16), chunk)
        copies = []
        for turn, (_, device) in enumerate(groups[n]):
            k = starts[n] + turn
            copies.append(
                copy(source, wholes[n].at[mine], gather_send.at[k], gather_recv.at[k], device)
            )
        wholes[n][mine, :] = source[...]
        for c in copies:
            c.wait()
        source = wholes[n]
    width = grad_qkv.shape[0]
    block = 0
    for ref in (grad_gate_up, grad_down, grad_qkv, grad_out):
        for n in range(0, ref.shape[1] - 127, 128):
            ref[:, n : n + 128] = source[block * width : (block + 1) * width, :].astype(single)
            block += 1
    rest = source[block * width : (block + 1) * width, :].astype(single)
    grad_qkv[:, 3 * width - QKV_REST :] = rest[:, :QKV_REST]
    grad_out[:, width - OUT_REST :] = rest[:, QKV_REST : QKV_REST + OUT_REST]
    grad_gains[...] = rest.T[QKV_REST + OUT_REST : QKV_REST + OUT_REST + 2, :]
    for c in far:
        c.wait()


def reduce(devices, own_total, other_total, sent_out, sent_grad, width, hidden):
    sizes = group_sizes(devices)
    rows = own_total.shape[0]
    v = pltpu.VMEM
    shape = jax.ShapeDtypeStruct
    parts, slots, left = [], [], rows
    for size in sizes:
        parts.append(v((left, 128), bfloat))
        left //= size
        slots.append(v((size - 1, left, 128), bfloat))
    links = sum(size - 1 for size in sizes)
    dma = pltpu.SemaphoreType.DMA
    anywhere = pl.BlockSpec(memory_space=pl.ANY)
    vmem = pl.BlockSpec(memory_space=pltpu.VMEM)
    return pl.pallas_call(
        functools.partial(reduce_kernel, sizes),
        out_shape=(
            shape(sent_out.shape, bfloat),
            shape(sent_grad.shape, bfloat),
            shape((2, width), single),
            shape((width, 3 * width), single),
            shape((width, width), single),
            shape((width, 2 * hidden), single),
            shape((width, hidden), single),
        ),
        in_specs=[vmem, vmem, anywhere, anywhere],
        out_specs=[anywhere, anywhere] + [vmem] * 5,
        scratch_shapes=[v((rows, 128), bfloat)]
        + parts
        + slots
        + parts
        + [v((left, 128), bfloat), dma((3,)), dma((3,))]
        + [dma((links,))] * 4,
        compiler_params=pltpu.CompilerParams(
            collective_id=1, has_side_effects=True, vmem_limit_bytes=40 * 2**20
        ),
    )(own_total, other_total, sent_out, sent_grad)


def on_device(
    devices,
    raw,
    series_ids,
    median,
    scale,
    cotangent,
    norm_gains,
    qkv_weight,
    out_weight,
    gate_up_weight,
    down_weight,
):
    section = lax.axis_index("section")
    turned = lambda a: jnp.swapaxes(a, -1, -2)
    count = raw.shape[0] // 2
    width, hidden = raw.shape[2], down_weight.shape[1]
    own = (norm_gains[0], qkv_weight[0], out_weight[0], gate_up_weight[0], turned(down_weight[0]))
    other = swap_weights(own)
    blocks = 14
    rows = -(-blocks * width // (16 * devices)) * 16 * devices
    kept_out, kept_grad, sent_out, sent_grad, own_total, other_total = train(
        section, rows, turned(raw), series_ids, median, scale, turned(cotangent), own, other
    )
    far_out, far_grad, gain, qkv, out, gate_up, down = reduce(
        devices, own_total, other_total, sent_out, sent_grad, width, hidden
    )
    place = ((1 - section) * count, 0, 0)
    layer_outputs = lax.dynamic_update_slice(kept_out, far_out, place)
    input_grads = lax.dynamic_update_slice(kept_grad, far_grad.astype(single), place)
    return (
        turned(layer_outputs)[None],
        turned(input_grads)[None],
        gain[None],
        qkv[None],
        out[None],
        gate_up[None],
        turned(down)[None],
    )


def solution(mesh):
    placed = (
        P("dp", None, None),
        P("dp"),
        P(),
        P(),
        P("dp", None, None),
        P("section", None, None),
        P("section", None, None),
        P("section", None, None),
        P("section", None, None),
        P("section", None, None),
    )
    return jax.shard_map(
        functools.partial(on_device, mesh.shape["dp"]),
        mesh=mesh,
        in_specs=placed,
        out_specs=(
            P("section", "dp", None, None),
            P("section", "dp", None, None),
            P("section", None, None),
            P("section", None, None),
            P("section", None, None),
            P("section", None, None),
            P("section", None, None),
        ),
        check_vma=False,
    )
```

```python
import functools
import math

import jax
import jax.numpy as jnp
import numpy as np
from jax import lax
from jax.experimental import pallas as pl
from jax.experimental.pallas import tpu as pltpu
from jax.sharding import PartitionSpec as P

HEAD = 16
HALF = HEAD // 2
TILE = 256
CHUNK = 512
VMEM_LIMIT = 64 * 2**20 - 2**16
EPSILON = 1e-06
LOG2E = math.log2(math.e)
QKV_REST = 48
OUT_REST = 16
MESH = pl.DeviceIdType.MESH
bfloat = jnp.bfloat16
single = jnp.float32


def dot(left, right):
    return jnp.dot(left, right, preferred_element_type=single)


def dot_nt(left, right):
    return lax.dot_general(left, right, (((1,), (1,)), ((), ())), preferred_element_type=single)


def rms_scale(values):
    return lax.rsqrt(jnp.mean(values * values, axis=0, keepdims=True) + EPSILON)


def rms_backward(grad_normed, values, inverse, gain):
    scaled = grad_normed * gain
    centre = jnp.mean(scaled * values, axis=0, keepdims=True)
    grad_values = inverse * scaled - values * (inverse * inverse * inverse * centre)
    product = grad_normed * values * inverse
    partial = product[:, :128]
    for start in range(128, product.shape[1], 128):
        partial = partial + product[:, start : start + 128]
    return grad_values, partial


def causal(block):
    rows = lax.broadcasted_iota(jnp.int32, block.shape, 0)
    columns = lax.broadcasted_iota(jnp.int32, block.shape, 1)
    return rows <= columns


def tile_start(j):
    return j * (j + 1) // 2 * TILE


def lanes(tiles):
    full = [(j, k) for j in range(tiles) for k in range(j + 1)]
    sides = [[(side, j, k) for j, k in full] for side in range(2)]
    for j in reversed(range(tiles)):
        side = min(sides, key=len)
        side += [(2, j, k) for k in range(j + 1)]
    return list(zip(*sides))


def train_kernel(
    heads,
    hidden,
    place,
    series_ids,
    median,
    scale,
    raw,
    cotangent,
    own_gains,
    own_qkv,
    own_out,
    own_gate_up,
    own_down_t,
    other_gains,
    other_qkv,
    other_out,
    other_gate_up,
    other_down_t,
    tables,
    kept_out,
    kept_grad,
    sent_out,
    sent_grad,
    own_total,
    other_total,
    gains,
    qkv_t,
    out_t,
    gate_up_t,
    down_t,
    qkv_w,
    out_w,
    gate_up_w,
    down_w,
    grad_gains,
    grad_qkv,
    grad_out,
    grad_gate_up,
    grad_down,
    inputs,
    inverse1,
    normed,
    queries,
    keys,
    values,
    rows_major,
    exponents,
    attended32,
    reciprocal,
    attended,
    residual,
    inverse2,
    mid,
    gate_up,
    activated,
    grad,
    grad_low,
    grad_pre,
    grad_res_low,
    grad_att,
    grad_q,
    grad_k,
    grad_v,
    grad_proj,
    flipped,
    grad_inputs,
):
    step = pl.program_id(0)
    section = place[0]
    series = place[1] + step
    number = series_ids[series]
    centre = median[number]
    inverse_spread = 1.0 / scale[number]
    width, length = inputs.shape[1:]
    tiles = length // TILE
    chunks = [slice(n, n + CHUNK) for n in range(0, length, CHUNK)]

    @pl.when(step == 0)
    def _():
        for ref in (grad_gains, grad_qkv, grad_out, grad_gate_up, grad_down):
            ref[...] = jnp.zeros_like(ref)
        row = lax.broadcasted_iota(jnp.int32, (2, heads, HEAD, length), 2)
        values[:, :, HEAD:, :] = jnp.where(row < 2, 1.0, 0.0).astype(bfloat)
        turned = lambda w: w.astype(single).T.astype(bfloat)
        for l, (gain, qkv, out, both, down) in (
            (section, (own_gains, own_qkv, own_out, own_gate_up, own_down_t)),
            (1 - section, (other_gains, other_qkv, other_out, other_gate_up, other_down_t)),
        ):
            for part in range(2):
                row = jnp.broadcast_to(gain[part : part + 1, :], (128, width))
                gains[l, part] = row.T
            qkv_w[l] = qkv[...]
            qkv_t[l] = turned(qkv[...])
            out_w[l] = out[...]
            out_t[l] = turned(out[...])
            gate_up_w[l] = both[...]
            gate_up_t[l] = turned(both[...])
            down_t[l] = down[...]
            down_w[l] = turned(down[...])

    def gain_of(l, part):
        return jnp.concatenate([gains[l, part]] * (CHUNK // 128), axis=1)

    inputs[0] = (raw[0].astype(single) - centre) * inverse_spread
    grad[...] = cotangent[0].astype(single)

    def rotated(block, cos, sin):
        a, b = block[:, :HALF], block[:, HALF:]
        return jnp.concatenate([a * cos - b * sin, b * cos + a * sin], axis=1)

    head_rows = lax.broadcasted_iota(jnp.int32, (HEAD, width), 0)
    head_columns = lax.broadcasted_iota(jnp.int32, (HEAD, width), 1)
    of_head = jnp.where(
        (head_columns >= head_rows * HEAD) & (head_columns < (head_rows + 1) * HEAD), 1.0, 0.0
    ).astype(bfloat)

    def forward(l, carry):
        largest_q = jnp.zeros((HEAD, CHUNK), single)
        largest_k = jnp.zeros((HEAD, CHUNK), single)
        for cs in chunks:
            u = inputs[l, :, cs]
            inv = rms_scale(u)
            inverse1[l, :, cs] = inv
            low = (u * inv * gain_of(l, 0)).astype(bfloat)
            normed[l, :, cs] = low
            projected = dot(qkv_t[l], low).reshape(3 * heads, HEAD, CHUNK)
            q = rotated(projected[:heads], tables[2, :, cs], tables[3, :, cs])
            k = rotated(projected[heads : 2 * heads], tables[0, :, cs], tables[1, :, cs])
            queries[l, :, :, cs] = q.astype(bfloat)
            keys[l, :, :, cs] = k.astype(bfloat)
            values[l, :, :HEAD, cs] = projected[2 * heads :].astype(bfloat)
            for h in range(heads):
                rows_major[h, cs, :HEAD] = k[h].T.astype(bfloat)
            squares = lambda v: dot(of_head, (v * v).astype(bfloat).reshape(width, CHUNK))
            largest_q = jnp.maximum(largest_q, squares(q))
            largest_k = jnp.maximum(largest_k, squares(k))
        bound = jnp.max(
            jnp.max(largest_q, axis=1, keepdims=True) * jnp.max(largest_k, axis=1, keepdims=True)
        )

        def finish(h, j, total):
            js = slice(j * TILE, (j + 1) * TILE)
            inverse = 1.0 / total[HEAD : HEAD + 1]
            out = total[:HEAD] * inverse
            reciprocal[l, h, :, js] = inverse
            attended32[l, h, :, js] = out
            attended[l, h, :, js] = out.astype(bfloat)

        small = bound <= 1e4

        @pl.when(small)
        def _():
            pairs = lanes(tiles)
            ahead = 3

            def some(three, carry):
                scores = {}

                def score(m):
                    for side, (g, j, k) in enumerate(pairs[m]):
                        scores[m, side] = dot(
                            rows_major[three * 3 + g, k * TILE : (k + 1) * TILE, :HEAD],
                            queries[l, three * 3 + g, :, j * TILE : (j + 1) * TILE],
                        )

                for m in range(ahead):
                    score(m)
                totals = {}
                for m, pair in enumerate(pairs):
                    if m + ahead < len(pairs):
                        score(m + ahead)
                    ready = []
                    for side, (g, j, k) in enumerate(pair):
                        e = jnp.exp2(scores.pop((m, side)))
                        if k == j:
                            e = jnp.where(causal(e), e, 0.0)
                        e = e.astype(bfloat)
                        first = tile_start(j) + k * TILE
                        exponents[l, three * 3 + g, first : first + TILE, :] = e.T
                        ready.append(e)
                    for side, (g, j, k) in enumerate(pair):
                        h = three * 3 + g
                        part = dot(values[l, h, :, k * TILE : (k + 1) * TILE], ready[side])
                        totals[g, j] = totals[g, j] + part if k else part
                        if k == j:
                            finish(h, j, totals.pop((g, j)))
                return carry

            lax.fori_loop(0, heads // 3, some, 0)

        @pl.when(jnp.logical_not(small))
        def _():
            def one(h, carry):
                for j in range(tiles):
                    count = (j + 1) * TILE
                    js = slice(j * TILE, (j + 1) * TILE)
                    score = dot(rows_major[h, :count, :HEAD], queries[l, h, :, js])
                    rows = lax.broadcasted_iota(jnp.int32, score.shape, 0)
                    columns = lax.broadcasted_iota(jnp.int32, score.shape, 1) + j * TILE
                    score = jnp.where(rows <= columns, score, -1e30)
                    e = jnp.exp2(score - jnp.max(score, axis=0, keepdims=True)).astype(bfloat)
                    for k in range(j + 1):
                        first = tile_start(j) + k * TILE
                        exponents[l, h, first : first + TILE, :] = e[k * TILE : (k + 1) * TILE].T
                    finish(h, j, dot(values[l, h, :, :count], e))
                return carry

            lax.fori_loop(0, heads, one, 0)

        for cs in chunks:
            res = inputs[l, :, cs] + dot(out_t[l], attended[l, :, :, cs].reshape(width, CHUNK))
            residual[l, :, cs] = res
            inv = rms_scale(res)
            inverse2[l, :, cs] = inv
            low = (res * inv * gain_of(l, 1)).astype(bfloat)
            mid[l, :, cs] = low
            both = dot(gate_up_t[l], low)
            gate, up = both[:hidden], both[hidden:]
            sig = 0.5 * jnp.tanh(0.5 * gate) + 0.5
            swish = gate * sig
            gate_up[l, :hidden, cs] = up * (sig + swish * (1.0 - sig))
            gate_up[l, hidden:, cs] = swish
            act = (swish * up).astype(bfloat)
            activated[l, :, cs] = act
            result = res + dot(down_t[l], act)
            inputs[l + 1, :, cs] = result.astype(bfloat).astype(single)
        return carry

    lax.fori_loop(0, 2, forward, 0)

    def backward(turn, carry):
        l = 1 - turn
        slot = lax.rem(l + section, 2)
        for cs in chunks:
            g = grad[:, cs]
            low = g.astype(bfloat)
            grad_low[:, cs] = low
            grad_act = dot(down_w[l], low)
            pre = jnp.concatenate(
                [grad_act * gate_up[l, :hidden, cs], grad_act * gate_up[l, hidden:, cs]], axis=0
            ).astype(bfloat)
            grad_pre[:, cs] = pre
            grad_mid = dot(gate_up_w[l], pre)
            res, inv = residual[l, :, cs], inverse2[l, :, cs]
            grad_res, partial = rms_backward(grad_mid, res, inv, gain_of(l, 1))
            grad_gains[slot, 1] += partial
            grad_res = grad_res + g
            grad[:, cs] = grad_res
            low = grad_res.astype(bfloat)
            grad_res_low[:, cs] = low
            back = dot(out_w[l], low).astype(bfloat).astype(single).reshape(heads, HEAD, CHUNK)
            inverse = reciprocal[l, :, :, cs]
            mean = jnp.sum(back * attended32[l, :, :, cs], axis=1, keepdims=True) * -inverse
            coarse = mean.astype(bfloat).astype(single)
            row = lax.broadcasted_iota(jnp.int32, (heads, HALF, CHUNK), 1)
            extra = jnp.where(row == 0, coarse, jnp.where(row == 1, mean - coarse, 0.0))
            rest = jnp.zeros((heads, HALF, CHUNK), single)
            grad_att[:, :, cs] = jnp.concatenate([back * inverse, extra, rest], axis=1).astype(bfloat)
        grad_down[slot] += dot_nt(grad_low[...], activated[l])
        grad_gate_up[slot] += dot_nt(mid[l], grad_pre[...])
        grad_out[slot] += dot_nt(attended[l].reshape(width, length), grad_res_low[...])

        for h in range(heads):
            rows_major[h] = grad_att[h].astype(single).T.astype(bfloat)

        pairs = lanes(tiles)
        ahead = 2
        half = TILE // 2

        def some(three, carry):
            products, held, sums = {}, {}, {}

            def product(m, part):
                if m < len(pairs):
                    for side, (g, j, k) in enumerate(pairs[m]):
                        first = j * TILE + part * half
                        products[m, side, part] = dot(
                            rows_major[three * 3 + g, first : first + half, :],
                            values[l, three * 3 + g, :, k * TILE : (k + 1) * TILE],
                        )

            def add(name, index, side, g, value):
                key = name, g, index, side
                sums[key] = sums[key] + value if key in sums else value

            for m in range(ahead):
                product(m, 0)
                product(m, 1)
            for m in range(len(pairs) + 1):
                now = pairs[m] if m < len(pairs) else ()
                before = pairs[m - 1] if m > 0 else ()
                product(m + ahead, 0)
                exps = []
                for side, (g, j, k) in enumerate(now):
                    first = tile_start(j) + k * TILE
                    e = exponents[l, three * 3 + g, first : first + TILE, :]
                    parts = [
                        e[p * half : (p + 1) * half] * products.pop((m, side, p)).astype(bfloat)
                        for p in range(2)
                    ]
                    grad_score = jnp.concatenate(parts, axis=0)
                    flipped[m % 2, side] = grad_score.T
                    held[m, side] = grad_score
                    exps.append(e)
                for side, (g, j, k) in enumerate(now):
                    js = slice(j * TILE, (j + 1) * TILE)
                    add("v", k, side, g, dot(grad_att[three * 3 + g, :HEAD, js], exps[side]))
                product(m + ahead, 1)
                for side, (g, j, k) in enumerate(before):
                    js = slice(j * TILE, (j + 1) * TILE)
                    grad_score = held.pop((m - 1, side))
                    add("k", k, side, g, dot(queries[l, three * 3 + g, :, js], grad_score))
                for side, (g, j, k) in enumerate(before):
                    ks = slice(k * TILE, (k + 1) * TILE)
                    turned = flipped[(m - 1) % 2, side]
                    add("q", j, side, g, dot(keys[l, three * 3 + g, :, ks], turned))
            for g in range(3):
                for name, ref in (("q", grad_q), ("k", grad_k), ("v", grad_v)):
                    for t in range(tiles):
                        found = [sums[name, g, t, n] for n in range(2) if (name, g, t, n) in sums]
                        ref[three * 3 + g, :, t * TILE : (t + 1) * TILE] = sum(found[1:], found[0])
            return carry

        lax.fori_loop(0, heads // 3, some, 0)

        for cs in chunks:
            dq = rotated(grad_q[:, :, cs], tables[4, :, cs], tables[5, :, cs])
            dk = rotated(grad_k[:, :, cs], tables[6, :, cs], tables[7, :, cs])
            low = jnp.concatenate([dq, dk, grad_v[:, :, cs]], axis=0).astype(bfloat)
            low = low.reshape(3 * width, CHUNK)
            grad_proj[:, cs] = low
            grad_normed = dot(qkv_w[l], low)
            u, inv = inputs[l, :, cs], inverse1[l, :, cs]
            grad_u, partial = rms_backward(grad_normed, u, inv, gain_of(l, 0))
            grad_gains[slot, 0] += partial
            grad_u = grad_u + grad[:, cs]
            grad[:, cs] = grad_u.astype(bfloat).astype(single)
            grad_inputs[l, :, cs] = grad_u
        grad_qkv[slot] += dot_nt(normed[l], grad_proj[...])
        return carry

    lax.fori_loop(0, 2, backward, 0)

    grad_inputs[0] = grad_inputs[0] * inverse_spread
    kept_out[0] = inputs[section + 1].astype(bfloat)
    sent_out[0] = inputs[2 - section].astype(bfloat)
    kept_grad[0] = grad_inputs[section]
    sent_grad[0] = grad_inputs[1 - section].astype(bfloat)

    @pl.when(step == pl.num_programs(0) - 1)
    def _():
        for slot, total in ((0, own_total), (1, other_total)):
            blocks = []
            for ref in (grad_gate_up, grad_down, grad_qkv, grad_out):
                blocks += [ref[slot, :, n : n + 128] for n in range(0, ref.shape[2] - 127, 128)]
            lane = lax.broadcasted_iota(jnp.int32, (width, 128), 1)
            spare = grad_qkv[slot, :, 3 * width - QKV_REST :]
            out_rest = grad_out[slot, :, width - OUT_REST :]
            columns = [jnp.sum(grad_gains[slot, n], axis=1, keepdims=True) for n in range(2)]
            rest = jnp.concatenate(
                [spare, out_rest] + columns
                + [jnp.zeros((width, 128 - QKV_REST - OUT_REST - 2), single)],
                axis=1,
            )
            blocks.append(rest)
            for n, block in enumerate(blocks):
                total[n * width : (n + 1) * width, :] = block.astype(total.dtype)
            used = len(blocks) * width
            total[used:, :] = jnp.zeros((total.shape[0] - used, 128), total.dtype)


def rotary_tables(length):
    frequency = 10000.0 ** (-np.arange(HALF, dtype=np.float64) / HALF)
    frequency = frequency.astype(np.float32)
    angles = np.arange(length, dtype=np.float32)[None, :] * frequency[:, None]
    cos, sin = np.cos(angles), np.sin(angles)
    query, grad_query, grad_key = HEAD**-0.5 * LOG2E, HEAD**-0.5, 1.0 / LOG2E
    tables = [cos, sin, cos * query, sin * query]
    tables += [cos * grad_query, -sin * grad_query, cos * grad_key, -sin * grad_key]
    return np.stack(tables).astype(np.float32)


def train(section, rows, raw, series_ids, median, scale, cotangent, own, other):
    count = raw.shape[0] // 2
    width, length = raw.shape[1:]
    heads = width // HEAD
    hidden = own[4].shape[1]
    place = jnp.stack([section, section * count]).astype(jnp.int32)
    tables = jnp.asarray(rotary_tables(length))
    operands = (raw, cotangent) + own + other + (tables,)
    smem = pl.BlockSpec(memory_space=pltpu.SMEM)

    def whole(array):
        zeros = (0,) * len(array.shape)
        return pl.BlockSpec(
            array.shape, lambda i, *_: zeros, pipeline_mode=pl.Buffered(buffer_count=1)
        )

    placed_block = pl.BlockSpec((1, width, length), lambda i, place, ids: (place[1] + i, 0, 0))
    block = pl.BlockSpec((1, width, length), lambda i, *_: (i, 0, 0))
    shape = jax.ShapeDtypeStruct
    totals = (shape((rows, 128), single), shape((rows, 128), bfloat))
    pairs = length // TILE * (length // TILE + 1) // 2
    v = pltpu.VMEM
    scratch = [
        v((2, 2, width, 128), single),
        v((2, 3 * width, width), bfloat),
        v((2, width, width), bfloat),
        v((2, 2 * hidden, width), bfloat),
        v((2, width, hidden), bfloat),
        v((2, width, 3 * width), bfloat),
        v((2, width, width), bfloat),
        v((2, width, 2 * hidden), bfloat),
        v((2, hidden, width), bfloat),
        v((2, 2, width, 128), single),
        v((2, width, 3 * width), single),
        v((2, width, width), single),
        v((2, width, 2 * hidden), single),
        v((2, width, hidden), single),
        v((3, width, length), single),
        v((2, 1, length), single),
        v((2, width, length), bfloat),
        v((2, heads, HEAD, length), bfloat),
        v((2, heads, HEAD, length), bfloat),
        v((2, heads, 2 * HEAD, length), bfloat),
        v((heads, length, 2 * HEAD), bfloat),
        v((2, heads, pairs * TILE, TILE), bfloat),
        v((2, heads, HEAD, length), single),
        v((2, heads, 1, length), single),
        v((2, heads, HEAD, length), bfloat),
        v((2, width, length), single),
        v((2, 1, length), single),
        v((2, width, length), bfloat),
        v((2, 2 * hidden, length), single),
        v((2, hidden, length), bfloat),
        v((width, length), single),
        v((width, length), bfloat),
        v((2 * hidden, length), bfloat),
        v((width, length), bfloat),
        v((heads, 2 * HEAD, length), bfloat),
        v((heads, HEAD, length), single),
        v((heads, HEAD, length), single),
        v((heads, HEAD, length), single),
        v((3 * width, length), bfloat),
        v((2, 2, TILE, TILE), bfloat),
        v((2, width, length), single),
    ]
    return pl.pallas_call(
        functools.partial(train_kernel, heads, hidden),
        grid_spec=pltpu.PrefetchScalarGridSpec(
            num_scalar_prefetch=2,
            grid=(count,),
            in_specs=[smem, smem, placed_block, placed_block] + [whole(a) for a in operands[2:]],
            out_specs=[placed_block, placed_block, block, block] + [whole(t) for t in totals],
            scratch_shapes=scratch,
        ),
        out_shape=(
            shape(raw.shape, bfloat),
            shape(raw.shape, single),
            shape((count, width, length), bfloat),
            shape((count, width, length), bfloat),
        )
        + totals,
        compiler_params=pltpu.CompilerParams(vmem_limit_bytes=VMEM_LIMIT),
    )(place, series_ids, median, scale, *operands)


def partner():
    return {"section": 1 - lax.axis_index("section")}


def meet(peers):
    barrier = pltpu.get_barrier_semaphore()
    for peer in peers:
        pl.semaphore_signal(barrier, inc=1, device_id=peer, device_id_type=MESH)
    pl.semaphore_wait(barrier, len(peers))


def swap_kernel(count, *refs):
    own, other, send, recv = refs[:count], refs[count : 2 * count], refs[-2], refs[-1]
    meet([partner()])
    copies = [
        pltpu.make_async_remote_copy(
            src_ref=own[n],
            dst_ref=other[n],
            send_sem=send.at[n],
            recv_sem=recv.at[n],
            device_id=partner(),
            device_id_type=MESH,
        )
        for n in range(count)
    ]
    for copy in copies:
        copy.start()
    for copy in copies:
        copy.wait()


def swap_weights(weights):
    count = len(weights)
    anywhere = pl.BlockSpec(memory_space=pl.ANY)
    return pl.pallas_call(
        functools.partial(swap_kernel, count),
        out_shape=tuple(jax.ShapeDtypeStruct(w.shape, w.dtype) for w in weights),
        in_specs=[anywhere] * count,
        out_specs=[anywhere] * count,
        scratch_shapes=[pltpu.SemaphoreType.DMA((count,)), pltpu.SemaphoreType.DMA((count,))],
        compiler_params=pltpu.CompilerParams(
            collective_id=0, has_side_effects=True, vmem_limit_bytes=VMEM_LIMIT
        ),
    )(*weights)


def group_sizes(devices):
    sizes = []
    while devices > 1:
        size = 4 if devices % 4 == 0 else devices
        sizes.append(size)
        devices //= size
    return sizes


def reduce_kernel(
    sizes,
    own_total,
    other_total,
    sent_out,
    sent_grad,
    far_out,
    far_grad,
    gathered,
    arrived,
    *scratch,
):
    count = len(sizes)
    parts = scratch[:count]
    slots = scratch[count : 2 * count]
    wholes = (gathered,) + scratch[2 * count : 3 * count - 1]
    last, swap_send, swap_recv, sum_send, sum_recv, gather_send, gather_recv = scratch[3 * count - 1 :]
    me = lax.axis_index("dp")
    places, groups = [], []
    stride = 1
    for size in sizes:
        place = lax.rem(lax.div(me, stride), size)
        peers = []
        for turn in range(1, size):
            other = lax.rem(place + turn, size)
            peers.append((other, {"dp": me + (other - place) * stride}))
        places.append(place)
        groups.append(peers)
        stride *= size
    meet([partner()] + [device for peers in groups for _, device in peers])

    def copy(source, target, send, recv, device):
        c = pltpu.make_async_remote_copy(
            src_ref=source,
            dst_ref=target,
            send_sem=send,
            recv_sem=recv,
            device_id=device,
            device_id_type=MESH,
        )
        c.start()
        return c

    near = copy(other_total, arrived, swap_send.at[0], swap_recv.at[0], partner())
    near.wait()
    far = [
        copy(sent_out, far_out, swap_send.at[1], swap_recv.at[1], partner()),
        copy(sent_grad, far_grad, swap_send.at[2], swap_recv.at[2], partner()),
    ]
    parts[0][...] = (own_total[...] + arrived[...].astype(single)).astype(bfloat)
    first = 0
    starts = []
    for n, size in enumerate(sizes):
        chunk = parts[n].shape[0] // size
        copies = []
        for turn, (other, device) in enumerate(groups[n]):
            copies.append(
                copy(
                    parts[n].at[pl.ds(pl.multiple_of(other * chunk, 16), chunk)],
                    slots[n].at[turn],
                    sum_send.at[first + turn],
                    sum_recv.at[first + turn],
                    device,
                )
            )
        total = parts[n][pl.ds(pl.multiple_of(places[n] * chunk, 16), chunk), :].astype(single)
        for turn, c in enumerate(copies):
            c.wait()
            total = total + slots[n][turn].astype(single)
        target = parts[n + 1] if n + 1 < count else last
        target[...] = total.astype(bfloat)
        starts.append(first)
        first += size - 1
    source = last
    for n in reversed(range(count)):
        chunk = parts[n].shape[0] // sizes[n]
        mine = pl.ds(pl.multiple_of(places[n] * chunk, 16), chunk)
        copies = []
        for turn, (_, device) in enumerate(groups[n]):
            k = starts[n] + turn
            copies.append(
                copy(source, wholes[n].at[mine], gather_send.at[k], gather_recv.at[k], device)
            )
        wholes[n][mine, :] = source[...]
        for c in copies:
            c.wait()
        source = wholes[n]
    for c in far:
        c.wait()


def unpack_kernel(gathered, grad_gains, grad_qkv, grad_out, grad_gate_up, grad_down):
    width = grad_qkv.shape[0]
    block = 0
    for ref in (grad_gate_up, grad_down, grad_qkv, grad_out):
        for n in range(0, ref.shape[1] - 127, 128):
            ref[:, n : n + 128] = gathered[block * width : (block + 1) * width, :].astype(single)
            block += 1
    rest = gathered[block * width : (block + 1) * width, :].astype(single)
    grad_qkv[:, 3 * width - QKV_REST :] = rest[:, :QKV_REST]
    grad_out[:, width - OUT_REST :] = rest[:, QKV_REST : QKV_REST + OUT_REST]
    grad_gains[...] = rest.T[QKV_REST + OUT_REST : QKV_REST + OUT_REST + 2, :]


def unpack(gathered, width, hidden):
    shape = jax.ShapeDtypeStruct
    vmem = pl.BlockSpec(memory_space=pltpu.VMEM)
    return pl.pallas_call(
        unpack_kernel,
        out_shape=(
            shape((2, width), single),
            shape((width, 3 * width), single),
            shape((width, width), single),
            shape((width, 2 * hidden), single),
            shape((width, hidden), single),
        ),
        in_specs=[vmem],
        out_specs=[vmem] * 5,
    )(gathered)


def reduce(devices, own_total, other_total, sent_out, sent_grad):
    sizes = group_sizes(devices)
    rows = own_total.shape[0]
    v = pltpu.VMEM
    shape = jax.ShapeDtypeStruct
    parts, slots, left = [], [], rows
    for size in sizes:
        parts.append(v((left, 128), bfloat))
        left //= size
        slots.append(v((size - 1, left, 128), bfloat))
    links = sum(size - 1 for size in sizes)
    dma = pltpu.SemaphoreType.DMA
    anywhere = pl.BlockSpec(memory_space=pl.ANY)
    vmem = pl.BlockSpec(memory_space=pltpu.VMEM)
    return pl.pallas_call(
        functools.partial(reduce_kernel, sizes),
        out_shape=(
            shape(sent_out.shape, bfloat),
            shape(sent_grad.shape, bfloat),
            shape((rows, 128), bfloat),
        ),
        in_specs=[vmem, vmem, anywhere, anywhere],
        out_specs=[anywhere, anywhere, vmem],
        scratch_shapes=[v((rows, 128), bfloat)]
        + parts
        + slots
        + parts[1:]
        + [v((left, 128), bfloat), dma((3,)), dma((3,))]
        + [dma((links,))] * 4,
        compiler_params=pltpu.CompilerParams(
            collective_id=1, has_side_effects=True, vmem_limit_bytes=VMEM_LIMIT
        ),
    )(own_total, other_total, sent_out, sent_grad)


def on_device(
    devices,
    raw,
    series_ids,
    median,
    scale,
    cotangent,
    norm_gains,
    qkv_weight,
    out_weight,
    gate_up_weight,
    down_weight,
):
    section = lax.axis_index("section")
    turned = lambda a: jnp.swapaxes(a, -1, -2)
    count = raw.shape[0] // 2
    width, hidden = raw.shape[2], down_weight.shape[1]
    own = (norm_gains[0], qkv_weight[0], out_weight[0], gate_up_weight[0], turned(down_weight[0]))
    other = swap_weights(own)
    blocks = 14
    rows = -(-blocks * width // (16 * devices)) * 16 * devices
    kept_out, kept_grad, sent_out, sent_grad, own_total, other_total = train(
        section, rows, turned(raw), series_ids, median, scale, turned(cotangent), own, other
    )
    far_out, far_grad, gathered = reduce(devices, own_total, other_total, sent_out, sent_grad)
    gain, qkv, out, gate_up, down = unpack(gathered, width, hidden)
    place = ((1 - section) * count, 0, 0)
    layer_outputs = lax.dynamic_update_slice(kept_out, far_out, place)
    input_grads = lax.dynamic_update_slice(kept_grad, far_grad.astype(single), place)
    return (
        turned(layer_outputs)[None],
        turned(input_grads)[None],
        gain[None],
        qkv[None],
        out[None],
        gate_up[None],
        turned(down)[None],
    )


def solution(mesh):
    placed = (
        P("dp", None, None),
        P("dp"),
        P(),
        P(),
        P("dp", None, None),
        P("section", None, None),
        P("section", None, None),
        P("section", None, None),
        P("section", None, None),
        P("section", None, None),
    )
    return jax.shard_map(
        functools.partial(on_device, mesh.shape["dp"]),
        mesh=mesh,
        in_specs=placed,
        out_specs=(
            P("section", "dp", None, None),
            P("section", "dp", None, None),
            P("section", None, None),
            P("section", None, None),
            P("section", None, None),
            P("section", None, None),
            P("section", None, None),
        ),
        check_vma=False,
    )
```

```python
import functools
import math

import jax
import jax.numpy as jnp
import numpy as np
from jax import lax
from jax.experimental import pallas as pl
from jax.experimental.pallas import tpu as pltpu
from jax.sharding import PartitionSpec as P

HEAD = 16
HALF = HEAD // 2
TILE = 256
CHUNK = 512
ROWS = 128
TURN_AT = 3
BACK_AT = 6
VMEM_LIMIT = 64 * 2**20 - 2**16
EPSILON = 1e-06
EXPONENT = HEAD**-0.5 * math.log2(math.e)
QKV_REST = 48
OUT_REST = 16
MESH = pl.DeviceIdType.MESH
bfloat = jnp.bfloat16
single = jnp.float32


def dot(left, right):
    return jnp.dot(left, right, preferred_element_type=single)


def dot_nt(left, right):
    return lax.dot_general(left, right, (((1,), (1,)), ((), ())), preferred_element_type=single)


def rms_scale(values):
    return lax.rsqrt(jnp.mean(values * values, axis=0, keepdims=True) + EPSILON)


def rms_backward(grad_normed, values, inverse, gain):
    scaled = grad_normed * gain
    centre = jnp.mean(scaled * values, axis=0, keepdims=True)
    grad_values = inverse * scaled - values * (inverse * inverse * inverse * centre)
    product = grad_normed * values * inverse
    partial = product[:, :128]
    for start in range(128, product.shape[1], 128):
        partial = partial + product[:, start : start + 128]
    return grad_values, partial


def causal(block):
    rows = lax.broadcasted_iota(jnp.int32, block.shape, 0)
    columns = lax.broadcasted_iota(jnp.int32, block.shape, 1)
    return rows <= columns


def tile_start(j):
    return j * (j + 1) // 2 * TILE


def lanes(tiles):
    full = [(j, k) for j in range(tiles) for k in range(j + 1)]
    sides = [[(side, j, k) for j, k in full] for side in range(2)]
    for j in reversed(range(tiles)):
        side = min(sides, key=len)
        side += [(2, j, k) for k in range(j + 1)]
    return list(zip(*sides))


def train_kernel(
    heads,
    hidden,
    place,
    series_ids,
    median,
    scale,
    raw,
    cotangent,
    own_gains,
    own_qkv,
    own_out,
    own_gate_up,
    own_down_t,
    other_gains,
    other_qkv,
    other_out,
    other_gate_up,
    other_down_t,
    tables,
    kept_out,
    kept_grad,
    sent_out,
    sent_grad,
    own_total,
    other_total,
    gains,
    qkv_t,
    out_t,
    gate_up_t,
    down_t,
    qkv_w,
    out_w,
    gate_up_w,
    down_w,
    grad_gains,
    grad_qkv,
    grad_out,
    grad_gate_up,
    grad_down,
    inputs,
    inverse1,
    normed,
    queries,
    keys,
    values,
    rows_major,
    exponents,
    attended32,
    reciprocal,
    attended,
    residual,
    inverse2,
    mid,
    gate_up,
    activated,
    grad,
    grad_low,
    grad_pre,
    grad_res_low,
    grad_att,
    grad_q,
    grad_k,
    grad_proj,
    flipped,
    grad_inputs,
):
    step = pl.program_id(0)
    section = place[0]
    series = place[1] + step
    number = series_ids[series]
    centre = median[number]
    inverse_spread = 1.0 / scale[number]
    width, length = inputs.shape[1:]
    tiles = length // TILE
    chunks = [slice(n, n + CHUNK) for n in range(0, length, CHUNK)]
    columns = [slice(n, n + TILE) for n in range(0, length, TILE)]

    @pl.when(step == 0)
    def _():
        for ref in (grad_gains, grad_qkv, grad_out, grad_gate_up, grad_down):
            ref[...] = jnp.zeros_like(ref)
        row = lax.broadcasted_iota(jnp.int32, (2, heads, HEAD, length), 2)
        values[:, :, HEAD:, :] = jnp.where(row < 2, 1.0, 0.0).astype(bfloat)
        turned = lambda w: w.astype(single).T.astype(bfloat)
        for l, (gain, qkv, out, both, down) in (
            (section, (own_gains, own_qkv, own_out, own_gate_up, own_down_t)),
            (1 - section, (other_gains, other_qkv, other_out, other_gate_up, other_down_t)),
        ):
            for part in range(2):
                row = jnp.broadcast_to(gain[part : part + 1, :], (128, width))
                gains[l, part] = row.T
            qkv_w[l] = qkv[...]
            qkv_t[l] = turned(qkv[...])
            out_w[l] = out[...]
            out_t[l] = turned(out[...])
            column = lax.broadcasted_iota(jnp.int32, both.shape, 1)
            halved = both[...].astype(single) * jnp.where(column < hidden, 0.5, 1.0)
            gate_up_w[l] = halved.astype(bfloat)
            gate_up_t[l] = halved.T.astype(bfloat)
            down_t[l] = down[...]
            down_w[l] = turned(down[...])

    def gain_of(l, part, count=CHUNK):
        return jnp.concatenate([gains[l, part]] * (count // 128), axis=1)

    inputs[0] = (raw[0].astype(single) - centre) * inverse_spread
    grad[...] = cotangent[0].astype(single)

    def rotated(block, cos, sin):
        a, b = block[:, :HALF], block[:, HALF:]
        return jnp.concatenate([a * cos - b * sin, b * cos + a * sin], axis=1)

    head_rows = lax.broadcasted_iota(jnp.int32, (HEAD, width), 0)
    head_columns = lax.broadcasted_iota(jnp.int32, (HEAD, width), 1)
    of_head = jnp.where(
        (head_columns >= head_rows * HEAD) & (head_columns < (head_rows + 1) * HEAD), 1.0, 0.0
    ).astype(bfloat)

    def forward(l, carry):
        largest_q = jnp.zeros((HEAD, CHUNK), single)
        largest_k = jnp.zeros((HEAD, CHUNK), single)
        for cs in chunks:
            u = inputs[l, :, cs]
            inv = rms_scale(u)
            inverse1[l, :, cs] = inv
            low = (u * inv * gain_of(l, 0)).astype(bfloat)
            normed[l, :, cs] = low
            projected = dot(qkv_t[l], low).reshape(3 * heads, HEAD, CHUNK)
            q, k = projected[:heads], projected[heads : 2 * heads]
            grad_q[:, :, cs] = q
            grad_k[:, :, cs] = k
            values[l, :, :HEAD, cs] = projected[2 * heads :].astype(bfloat)
            squares = lambda v: dot(of_head, (v * v).astype(bfloat).reshape(width, CHUNK))
            largest_q = jnp.maximum(largest_q, squares(q))
            largest_k = jnp.maximum(largest_k, squares(k))
        bound = jnp.max(
            jnp.max(largest_q, axis=1, keepdims=True) * jnp.max(largest_k, axis=1, keepdims=True)
        )

        def finish(h, j, total):
            js = slice(j * TILE, (j + 1) * TILE)
            inverse = 1.0 / total[HEAD : HEAD + 1]
            out = total[:HEAD] * inverse
            reciprocal[l, h, :, js] = inverse
            attended32[l, h, :, js] = out
            attended[l, h, :, js] = out.astype(bfloat)

        def turn(three):
            hs = slice(three * 3, three * 3 + 3)
            for cs in chunks:
                q = rotated(grad_q[hs, :, cs], tables[0, :, cs], tables[1, :, cs])
                k = rotated(grad_k[hs, :, cs], tables[0, :, cs], tables[1, :, cs])
                queries[l, hs, :, cs] = q.astype(bfloat)
                keys[l, hs, :, cs] = k.astype(bfloat)
                for g in range(3):
                    rows_major[three * 3 + g, cs, :HEAD] = k[g].T.astype(bfloat)

        small = bound * EXPONENT**2 <= 1e4

        @pl.when(small)
        def _():
            pairs = lanes(tiles)
            ahead = 3

            def some(three):
                scores = {}

                def score(m):
                    for side, (g, j, k) in enumerate(pairs[m]):
                        scores[m, side] = dot(
                            rows_major[three * 3 + g, k * TILE : (k + 1) * TILE, :HEAD],
                            queries[l, three * 3 + g, :, j * TILE : (j + 1) * TILE],
                        )

                for m in range(ahead):
                    score(m)
                totals = {}
                for m, pair in enumerate(pairs):
                    if m == TURN_AT and (three + 1) * 3 < heads:
                        turn(three + 1)
                    if m + ahead < len(pairs):
                        score(m + ahead)
                    ready = []
                    for side, (g, j, k) in enumerate(pair):
                        e = jnp.exp2(scores.pop((m, side)) * EXPONENT)
                        if k == j:
                            e = jnp.where(causal(e), e, 0.0)
                        e = e.astype(bfloat)
                        first = tile_start(j) + k * TILE
                        exponents[l, three * 3 + g, first : first + TILE, :] = e.T
                        ready.append(e)
                    for side, (g, j, k) in enumerate(pair):
                        h = three * 3 + g
                        part = dot(values[l, h, :, k * TILE : (k + 1) * TILE], ready[side])
                        totals[g, j] = totals[g, j] + part if k else part
                        if k == j:
                            finish(h, j, totals.pop((g, j)))

            turn(0)
            for three in range(heads // 3):
                some(three)

        @pl.when(jnp.logical_not(small))
        def _():
            for three in range(heads // 3):
                turn(three)

            def one(h, carry):
                for j in range(tiles):
                    count = (j + 1) * TILE
                    js = slice(j * TILE, (j + 1) * TILE)
                    score = dot(rows_major[h, :count, :HEAD], queries[l, h, :, js]) * EXPONENT
                    rows = lax.broadcasted_iota(jnp.int32, score.shape, 0)
                    columns = lax.broadcasted_iota(jnp.int32, score.shape, 1) + j * TILE
                    score = jnp.where(rows <= columns, score, -1e30)
                    e = jnp.exp2(score - jnp.max(score, axis=0, keepdims=True)).astype(bfloat)
                    for k in range(j + 1):
                        first = tile_start(j) + k * TILE
                        exponents[l, h, first : first + TILE, :] = e[k * TILE : (k + 1) * TILE].T
                    finish(h, j, dot(values[l, h, :, :count], e))
                return carry

            lax.fori_loop(0, heads, one, 0)

        for cs in chunks:
            res = inputs[l, :, cs] + dot(out_t[l], attended[l, :, :, cs].reshape(width, CHUNK))
            residual[l, :, cs] = res
            inv = rms_scale(res)
            inverse2[l, :, cs] = inv
            mid[l, :, cs] = (res * inv * gain_of(l, 1)).astype(bfloat)
        for cs in columns:
            low = mid[l, :, cs]
            for n in range(0, hidden, ROWS):
                half = dot(gate_up_t[l, n : n + ROWS], low)
                up = dot(gate_up_t[l, hidden + n : hidden + n + ROWS], low)
                t = jnp.tanh(half)
                twice = 1.0 + t
                swish = half * twice
                gate_up[l, n : n + ROWS, cs] = up * (twice + swish * (1.0 - t))
                gate_up[l, hidden + n : hidden + n + ROWS, cs] = swish
                activated[l, n : n + ROWS, cs] = (swish * up).astype(bfloat)
        for cs in chunks:
            result = residual[l, :, cs] + dot(down_t[l], activated[l, :, cs])
            inputs[l + 1, :, cs] = result.astype(bfloat).astype(single)
        return carry

    lax.fori_loop(0, 2, forward, 0)

    def backward(turn, carry):
        l = 1 - turn
        slot = lax.rem(l + section, 2)
        for cs in columns:
            low = grad[:, cs].astype(bfloat)
            grad_low[:, cs] = low
            for n in range(0, hidden, ROWS):
                grad_act = dot(down_w[l, n : n + ROWS], low)
                for m in (n, hidden + n):
                    factor = gate_up[l, m : m + ROWS, cs]
                    grad_pre[m : m + ROWS, cs] = (grad_act * factor).astype(bfloat)
        for cs in chunks:
            g = grad[:, cs]
            grad_mid = dot(gate_up_w[l], grad_pre[:, cs])
            res, inv = residual[l, :, cs], inverse2[l, :, cs]
            grad_res, partial = rms_backward(grad_mid, res, inv, gain_of(l, 1))
            grad_gains[slot, 1] += partial
            grad_res = grad_res + g
            grad[:, cs] = grad_res
            low = grad_res.astype(bfloat)
            grad_res_low[:, cs] = low
            back = dot(out_w[l], low).astype(bfloat).astype(single).reshape(heads, HEAD, CHUNK)
            inverse = reciprocal[l, :, :, cs]
            mean = jnp.sum(back * attended32[l, :, :, cs], axis=1, keepdims=True) * -inverse
            coarse = mean.astype(bfloat).astype(single)
            row = lax.broadcasted_iota(jnp.int32, (heads, HALF, CHUNK), 1)
            extra = jnp.where(row == 0, coarse, jnp.where(row == 1, mean - coarse, 0.0))
            rest = jnp.zeros((heads, HALF, CHUNK), single)
            grad_att[:, :, cs] = jnp.concatenate([back * inverse, extra, rest], axis=1).astype(bfloat)
        grad_down[slot] += dot_nt(grad_low[...], activated[l])
        grad_gate_up[slot] += dot_nt(mid[l], grad_pre[...])
        grad_out[slot] += dot_nt(attended[l].reshape(width, length), grad_res_low[...])

        def turn(three):
            for h in range(three * 3, three * 3 + 3):
                rows_major[h] = grad_att[h].T

        def turn_back(three):
            hs = slice(three * 3, three * 3 + 3)
            for cs in chunks:
                dq = rotated(grad_q[hs, :, cs], tables[2, :, cs], tables[3, :, cs])
                dk = rotated(grad_k[hs, :, cs], tables[2, :, cs], tables[3, :, cs])
                grad_proj[hs, :, cs] = dq.astype(bfloat)
                grad_proj[three * 3 + heads : three * 3 + heads + 3, :, cs] = dk.astype(bfloat)

        pairs = lanes(tiles)
        ahead = 2
        half = TILE // 2

        def some(three):
            products, held, sums = {}, {}, {}

            def product(m, part):
                if m < len(pairs):
                    for side, (g, j, k) in enumerate(pairs[m]):
                        first = j * TILE + part * half
                        products[m, side, part] = dot(
                            rows_major[three * 3 + g, first : first + half, :],
                            values[l, three * 3 + g, :, k * TILE : (k + 1) * TILE],
                        )

            def add(name, index, side, g, value):
                key = name, g, index, side
                sums[key] = sums[key] + value if key in sums else value

            for m in range(ahead):
                product(m, 0)
                product(m, 1)
            for m in range(len(pairs) + 1):
                if m == TURN_AT and (three + 1) * 3 < heads:
                    turn(three + 1)
                if m == BACK_AT and three > 0:
                    turn_back(three - 1)
                now = pairs[m] if m < len(pairs) else ()
                before = pairs[m - 1] if m > 0 else ()
                product(m + ahead, 0)
                exps = []
                for side, (g, j, k) in enumerate(now):
                    first = tile_start(j) + k * TILE
                    e = exponents[l, three * 3 + g, first : first + TILE, :]
                    parts = [
                        e[p * half : (p + 1) * half] * products.pop((m, side, p)).astype(bfloat)
                        for p in range(2)
                    ]
                    grad_score = jnp.concatenate(parts, axis=0)
                    flipped[m % 2, side] = grad_score.T
                    held[m, side] = grad_score
                    exps.append(e)
                for side, (g, j, k) in enumerate(now):
                    js = slice(j * TILE, (j + 1) * TILE)
                    add("v", k, side, g, dot(grad_att[three * 3 + g, :HEAD, js], exps[side]))
                product(m + ahead, 1)
                for side, (g, j, k) in enumerate(before):
                    js = slice(j * TILE, (j + 1) * TILE)
                    grad_score = held.pop((m - 1, side))
                    add("k", k, side, g, dot(queries[l, three * 3 + g, :, js], grad_score))
                for side, (g, j, k) in enumerate(before):
                    ks = slice(k * TILE, (k + 1) * TILE)
                    turned = flipped[(m - 1) % 2, side]
                    add("q", j, side, g, dot(keys[l, three * 3 + g, :, ks], turned))
            for g in range(3):
                h = three * 3 + g
                for name, ref in (("q", grad_q), ("k", grad_k), ("v", grad_proj)):
                    for t in range(tiles):
                        found = [sums[name, g, t, n] for n in range(2) if (name, g, t, n) in sums]
                        place = h + 2 * heads if name == "v" else h
                        total = sum(found[1:], found[0]).astype(ref.dtype)
                        ref[place, :, t * TILE : (t + 1) * TILE] = total

        turn(0)
        for three in range(heads // 3):
            some(three)
        turn_back(heads // 3 - 1)

        for cs in chunks:
            low = grad_proj[:, :, cs].reshape(3 * width, CHUNK)
            grad_normed = dot(qkv_w[l], low)
            u, inv = inputs[l, :, cs], inverse1[l, :, cs]
            grad_u, partial = rms_backward(grad_normed, u, inv, gain_of(l, 0))
            grad_gains[slot, 0] += partial
            grad_u = grad_u + grad[:, cs]
            grad[:, cs] = grad_u.astype(bfloat).astype(single)
            grad_inputs[l, :, cs] = grad_u
        grad_qkv[slot] += dot_nt(normed[l], grad_proj[...].reshape(3 * width, length))
        return carry

    lax.fori_loop(0, 2, backward, 0)

    grad_inputs[0] = grad_inputs[0] * inverse_spread
    kept_out[0] = inputs[section + 1].astype(bfloat)
    sent_out[0] = inputs[2 - section].astype(bfloat)
    kept_grad[0] = grad_inputs[section]
    sent_grad[0] = grad_inputs[1 - section].astype(bfloat)

    @pl.when(step == pl.num_programs(0) - 1)
    def _():
        for slot, total in ((0, own_total), (1, other_total)):
            blocks = []
            for ref in (grad_gate_up, grad_down, grad_qkv, grad_out):
                for n in range(0, ref.shape[2] - 127, 128):
                    doubled = ref is grad_gate_up and n < hidden
                    blocks.append(ref[slot, :, n : n + 128] * (0.5 if doubled else 1.0))
            lane = lax.broadcasted_iota(jnp.int32, (width, 128), 1)
            spare = grad_qkv[slot, :, 3 * width - QKV_REST :]
            out_rest = grad_out[slot, :, width - OUT_REST :]
            columns = [jnp.sum(grad_gains[slot, n], axis=1, keepdims=True) for n in range(2)]
            rest = jnp.concatenate(
                [spare, out_rest] + columns
                + [jnp.zeros((width, 128 - QKV_REST - OUT_REST - 2), single)],
                axis=1,
            )
            blocks.append(rest)
            for n, block in enumerate(blocks):
                total[n * width : (n + 1) * width, :] = block.astype(total.dtype)
            used = len(blocks) * width
            total[used:, :] = jnp.zeros((total.shape[0] - used, 128), total.dtype)


def rotary_tables(length):
    frequency = 10000.0 ** (-np.arange(HALF, dtype=np.float64) / HALF)
    frequency = frequency.astype(np.float32)
    angles = np.arange(length, dtype=np.float32)[None, :] * frequency[:, None]
    cos, sin = np.cos(angles), np.sin(angles)
    tables = [cos, sin, cos * HEAD**-0.5, -sin * HEAD**-0.5]
    return np.stack(tables).astype(np.float32)


def train(section, rows, raw, series_ids, median, scale, cotangent, own, other):
    count = raw.shape[0] // 2
    width, length = raw.shape[1:]
    heads = width // HEAD
    hidden = own[4].shape[1]
    place = jnp.stack([section, section * count]).astype(jnp.int32)
    tables = jnp.asarray(rotary_tables(length))
    operands = (raw, cotangent) + own + other + (tables,)
    smem = pl.BlockSpec(memory_space=pltpu.SMEM)

    def whole(array):
        zeros = (0,) * len(array.shape)
        return pl.BlockSpec(
            array.shape, lambda i, *_: zeros, pipeline_mode=pl.Buffered(buffer_count=1)
        )

    placed_block = pl.BlockSpec((1, width, length), lambda i, place, ids: (place[1] + i, 0, 0))
    block = pl.BlockSpec((1, width, length), lambda i, *_: (i, 0, 0))
    shape = jax.ShapeDtypeStruct
    totals = (shape((rows, 128), single), shape((rows, 128), bfloat))
    pairs = length // TILE * (length // TILE + 1) // 2
    v = pltpu.VMEM
    scratch = [
        v((2, 2, width, 128), single),
        v((2, 3 * width, width), bfloat),
        v((2, width, width), bfloat),
        v((2, 2 * hidden, width), bfloat),
        v((2, width, hidden), bfloat),
        v((2, width, 3 * width), bfloat),
        v((2, width, width), bfloat),
        v((2, width, 2 * hidden), bfloat),
        v((2, hidden, width), bfloat),
        v((2, 2, width, 128), single),
        v((2, width, 3 * width), single),
        v((2, width, width), single),
        v((2, width, 2 * hidden), single),
        v((2, width, hidden), single),
        v((3, width, length), single),
        v((2, 1, length), single),
        v((2, width, length), bfloat),
        v((2, heads, HEAD, length), bfloat),
        v((2, heads, HEAD, length), bfloat),
        v((2, heads, 2 * HEAD, length), bfloat),
        v((heads, length, 2 * HEAD), bfloat),
        v((2, heads, pairs * TILE, TILE), bfloat),
        v((2, heads, HEAD, length), single),
        v((2, heads, 1, length), single),
        v((2, heads, HEAD, length), bfloat),
        v((2, width, length), single),
        v((2, 1, length), single),
        v((2, width, length), bfloat),
        v((2, 2 * hidden, length), single),
        v((2, hidden, length), bfloat),
        v((width, length), single),
        v((width, length), bfloat),
        v((2 * hidden, length), bfloat),
        v((width, length), bfloat),
        v((heads, 2 * HEAD, length), bfloat),
        v((heads, HEAD, length), single),
        v((heads, HEAD, length), single),
        v((3 * heads, HEAD, length), bfloat),
        v((2, 2, TILE, TILE), bfloat),
        v((2, width, length), single),
    ]
    return pl.pallas_call(
        functools.partial(train_kernel, heads, hidden),
        grid_spec=pltpu.PrefetchScalarGridSpec(
            num_scalar_prefetch=2,
            grid=(count,),
            in_specs=[smem, smem, placed_block, placed_block] + [whole(a) for a in operands[2:]],
            out_specs=[placed_block, placed_block, block, block] + [whole(t) for t in totals],
            scratch_shapes=scratch,
        ),
        out_shape=(
            shape(raw.shape, bfloat),
            shape(raw.shape, single),
            shape((count, width, length), bfloat),
            shape((count, width, length), bfloat),
        )
        + totals,
        compiler_params=pltpu.CompilerParams(vmem_limit_bytes=VMEM_LIMIT),
    )(place, series_ids, median, scale, *operands)


def partner():
    return {"section": 1 - lax.axis_index("section")}


def meet(peers):
    barrier = pltpu.get_barrier_semaphore()
    for peer in peers:
        pl.semaphore_signal(barrier, inc=1, device_id=peer, device_id_type=MESH)
    pl.semaphore_wait(barrier, len(peers))


def swap_kernel(count, *refs):
    own, other, send, recv = refs[:count], refs[count : 2 * count], refs[-2], refs[-1]
    meet([partner()])
    copies = [
        pltpu.make_async_remote_copy(
            src_ref=own[n],
            dst_ref=other[n],
            send_sem=send.at[n],
            recv_sem=recv.at[n],
            device_id=partner(),
            device_id_type=MESH,
        )
        for n in range(count)
    ]
    for copy in copies:
        copy.start()
    for copy in copies:
        copy.wait()


def swap_weights(weights):
    count = len(weights)
    anywhere = pl.BlockSpec(memory_space=pl.ANY)
    return pl.pallas_call(
        functools.partial(swap_kernel, count),
        out_shape=tuple(jax.ShapeDtypeStruct(w.shape, w.dtype) for w in weights),
        in_specs=[anywhere] * count,
        out_specs=[anywhere] * count,
        scratch_shapes=[pltpu.SemaphoreType.DMA((count,)), pltpu.SemaphoreType.DMA((count,))],
        compiler_params=pltpu.CompilerParams(
            collective_id=0, has_side_effects=True, vmem_limit_bytes=VMEM_LIMIT
        ),
    )(*weights)


def group_sizes(devices):
    sizes = []
    while devices > 1:
        size = 4 if devices % 4 == 0 else devices
        sizes.append(size)
        devices //= size
    return sizes


def reduce_kernel(
    sizes,
    own_total,
    other_total,
    sent_out,
    sent_grad,
    far_out,
    far_grad,
    gathered,
    arrived,
    *scratch,
):
    count = len(sizes)
    parts = scratch[:count]
    slots = scratch[count : 2 * count]
    wholes = (gathered,) + scratch[2 * count : 3 * count - 1]
    last, swap_send, swap_recv, sum_send, sum_recv, gather_send, gather_recv = scratch[3 * count - 1 :]
    me = lax.axis_index("dp")
    places, groups = [], []
    stride = 1
    for size in sizes:
        place = lax.rem(lax.div(me, stride), size)
        peers = []
        for turn in range(1, size):
            other = lax.rem(place + turn, size)
            peers.append((other, {"dp": me + (other - place) * stride}))
        places.append(place)
        groups.append(peers)
        stride *= size
    meet([partner()] + [device for peers in groups for _, device in peers])

    def copy(source, target, send, recv, device):
        c = pltpu.make_async_remote_copy(
            src_ref=source,
            dst_ref=target,
            send_sem=send,
            recv_sem=recv,
            device_id=device,
            device_id_type=MESH,
        )
        c.start()
        return c

    near = copy(other_total, arrived, swap_send.at[0], swap_recv.at[0], partner())
    near.wait()
    far = [
        copy(sent_out, far_out, swap_send.at[1], swap_recv.at[1], partner()),
        copy(sent_grad, far_grad, swap_send.at[2], swap_recv.at[2], partner()),
    ]
    parts[0][...] = (own_total[...] + arrived[...].astype(single)).astype(bfloat)
    first = 0
    starts = []
    for n, size in enumerate(sizes):
        chunk = parts[n].shape[0] // size
        copies = []
        for turn, (other, device) in enumerate(groups[n]):
            copies.append(
                copy(
                    parts[n].at[pl.ds(pl.multiple_of(other * chunk, 16), chunk)],
                    slots[n].at[turn],
                    sum_send.at[first + turn],
                    sum_recv.at[first + turn],
                    device,
                )
            )
        total = parts[n][pl.ds(pl.multiple_of(places[n] * chunk, 16), chunk), :].astype(single)
        for turn, c in enumerate(copies):
            c.wait()
            total = total + slots[n][turn].astype(single)
        target = parts[n + 1] if n + 1 < count else last
        target[...] = total.astype(bfloat)
        starts.append(first)
        first += size - 1
    source = last
    for n in reversed(range(count)):
        chunk = parts[n].shape[0] // sizes[n]
        mine = pl.ds(pl.multiple_of(places[n] * chunk, 16), chunk)
        copies = []
        for turn, (_, device) in enumerate(groups[n]):
            k = starts[n] + turn
            copies.append(
                copy(source, wholes[n].at[mine], gather_send.at[k], gather_recv.at[k], device)
            )
        wholes[n][mine, :] = source[...]
        for c in copies:
            c.wait()
        source = wholes[n]
    for c in far:
        c.wait()


def finish_kernel(
    place,
    gathered,
    far_out,
    far_grad,
    kept_out,
    kept_grad,
    layer_outputs,
    input_grads,
    grad_gains,
    grad_qkv,
    grad_out,
    grad_gate_up,
    grad_down,
):
    layer_outputs[...] = far_out[...]
    input_grads[...] = far_grad[...].astype(single)

    @pl.when(pl.program_id(0) == 0)
    def _():
        width = grad_qkv.shape[0]
        block = 0
        for ref in (grad_gate_up, grad_down, grad_qkv, grad_out):
            for n in range(0, ref.shape[1] - 127, 128):
                rows = slice(block * width, (block + 1) * width)
                ref[:, n : n + 128] = gathered[rows, :].astype(single)
                block += 1
        rest = gathered[block * width : (block + 1) * width, :].astype(single)
        grad_qkv[:, 3 * width - QKV_REST :] = rest[:, :QKV_REST]
        grad_out[:, width - OUT_REST :] = rest[:, QKV_REST : QKV_REST + OUT_REST]
        grad_gains[...] = rest.T[QKV_REST + OUT_REST : QKV_REST + OUT_REST + 2, :]


def finish(place, gathered, far_out, far_grad, kept_out, kept_grad, hidden):
    shape = jax.ShapeDtypeStruct
    count, width, length = far_out.shape
    anywhere = pl.BlockSpec(memory_space=pl.ANY)
    block = pl.BlockSpec((1, width, length), lambda i, place: (i, 0, 0))
    placed = pl.BlockSpec((1, width, length), lambda i, place: (place[0] + i, 0, 0))
    grads = (
        shape((2, width), single),
        shape((width, 3 * width), single),
        shape((width, width), single),
        shape((width, 2 * hidden), single),
        shape((width, hidden), single),
    )

    def whole(array):
        return pl.BlockSpec(
            array.shape, lambda i, place: (0, 0), pipeline_mode=pl.Buffered(buffer_count=1)
        )

    return pl.pallas_call(
        finish_kernel,
        grid_spec=pltpu.PrefetchScalarGridSpec(
            num_scalar_prefetch=1,
            grid=(count,),
            in_specs=[whole(gathered), block, block, anywhere, anywhere],
            out_specs=[placed, placed] + [whole(g) for g in grads],
        ),
        out_shape=(shape(kept_out.shape, bfloat), shape(kept_grad.shape, single)) + grads,
        input_output_aliases={4: 0, 5: 1},
        compiler_params=pltpu.CompilerParams(vmem_limit_bytes=VMEM_LIMIT),
    )(place, gathered, far_out, far_grad, kept_out, kept_grad)


def reduce(devices, own_total, other_total, sent_out, sent_grad):
    sizes = group_sizes(devices)
    rows = own_total.shape[0]
    v = pltpu.VMEM
    shape = jax.ShapeDtypeStruct
    parts, slots, left = [], [], rows
    for size in sizes:
        parts.append(v((left, 128), bfloat))
        left //= size
        slots.append(v((size - 1, left, 128), bfloat))
    links = sum(size - 1 for size in sizes)
    dma = pltpu.SemaphoreType.DMA
    anywhere = pl.BlockSpec(memory_space=pl.ANY)
    vmem = pl.BlockSpec(memory_space=pltpu.VMEM)
    return pl.pallas_call(
        functools.partial(reduce_kernel, sizes),
        out_shape=(
            shape(sent_out.shape, bfloat),
            shape(sent_grad.shape, bfloat),
            shape((rows, 128), bfloat),
        ),
        in_specs=[vmem, vmem, anywhere, anywhere],
        out_specs=[anywhere, anywhere, vmem],
        scratch_shapes=[v((rows, 128), bfloat)]
        + parts
        + slots
        + parts[1:]
        + [v((left, 128), bfloat), dma((3,)), dma((3,))]
        + [dma((links,))] * 4,
        compiler_params=pltpu.CompilerParams(
            collective_id=1, has_side_effects=True, vmem_limit_bytes=VMEM_LIMIT
        ),
    )(own_total, other_total, sent_out, sent_grad)


def on_device(
    devices,
    raw,
    series_ids,
    median,
    scale,
    cotangent,
    norm_gains,
    qkv_weight,
    out_weight,
    gate_up_weight,
    down_weight,
):
    section = lax.axis_index("section")
    turned = lambda a: jnp.swapaxes(a, -1, -2)
    count = raw.shape[0] // 2
    width, hidden = raw.shape[2], down_weight.shape[1]
    own = (norm_gains[0], qkv_weight[0], out_weight[0], gate_up_weight[0], turned(down_weight[0]))
    other = swap_weights(own)
    blocks = 14
    rows = -(-blocks * width // (16 * devices)) * 16 * devices
    kept_out, kept_grad, sent_out, sent_grad, own_total, other_total = train(
        section, rows, turned(raw), series_ids, median, scale, turned(cotangent), own, other
    )
    far_out, far_grad, gathered = reduce(devices, own_total, other_total, sent_out, sent_grad)
    place = jnp.reshape((1 - section) * count, (1,)).astype(jnp.int32)
    layer_outputs, input_grads, gain, qkv, out, gate_up, down = finish(
        place, gathered, far_out, far_grad, kept_out, kept_grad, hidden
    )
    return (
        turned(layer_outputs)[None],
        turned(input_grads)[None],
        gain[None],
        qkv[None],
        out[None],
        gate_up[None],
        turned(down)[None],
    )


def solution(mesh):
    placed = (
        P("dp", None, None),
        P("dp"),
        P(),
        P(),
        P("dp", None, None),
        P("section", None, None),
        P("section", None, None),
        P("section", None, None),
        P("section", None, None),
        P("section", None, None),
    )
    return jax.shard_map(
        functools.partial(on_device, mesh.shape["dp"]),
        mesh=mesh,
        in_specs=placed,
        out_specs=(
            P("section", "dp", None, None),
            P("section", "dp", None, None),
            P("section", None, None),
            P("section", None, None),
            P("section", None, None),
            P("section", None, None),
            P("section", None, None),
        ),
        check_vma=False,
    )
```

```python
import functools
import math

import jax
import jax.numpy as jnp
import numpy as np
from jax import lax
from jax.experimental import pallas as pl
from jax.experimental.pallas import tpu as pltpu
from jax.sharding import PartitionSpec as P

HEAD = 16
HALF = HEAD // 2
TILE = 256
CHUNK = 512
ROWS = 128
TURN_AT = 6
BACK_AT = 8
VMEM_LIMIT = 64 * 2**20 - 2**16
EPSILON = 1e-06
EXPONENT = HEAD**-0.5 * math.log2(math.e)
QKV_REST = 48
OUT_REST = 16
MESH = pl.DeviceIdType.MESH
bfloat = jnp.bfloat16
single = jnp.float32


def dot(left, right):
    return jnp.dot(left, right, preferred_element_type=single)


def dot_nt(left, right):
    return lax.dot_general(left, right, (((1,), (1,)), ((), ())), preferred_element_type=single)


def rms_scale(values):
    return lax.rsqrt(jnp.mean(values * values, axis=0, keepdims=True) + EPSILON)


def rms_backward(grad_normed, values, inverse, gain):
    scaled = grad_normed * gain
    centre = jnp.mean(scaled * values, axis=0, keepdims=True)
    grad_values = inverse * scaled - values * (inverse * inverse * inverse * centre)
    product = grad_normed * values * inverse
    partial = product[:, :128]
    for start in range(128, product.shape[1], 128):
        partial = partial + product[:, start : start + 128]
    return grad_values, partial


def causal(block):
    rows = lax.broadcasted_iota(jnp.int32, block.shape, 0)
    columns = lax.broadcasted_iota(jnp.int32, block.shape, 1)
    return rows <= columns


def tile_start(j):
    return j * (j + 1) // 2 * TILE


def lanes(tiles, heads):
    pairs = []
    for first in range(0, heads, 3):
        full = [(j, k) for j in range(tiles) for k in range(j + 1)]
        sides = [[(first + side, j, k) for j, k in full] for side in range(2)]
        for j in reversed(range(tiles)):
            side = min(sides, key=len)
            side += [(first + 2, j, k) for k in range(j + 1)]
        pairs += zip(*sides)
    return pairs


def train_kernel(
    heads,
    hidden,
    here,
    start,
    series_ids,
    median,
    scale,
    raw,
    cotangent,
    own_gains,
    own_qkv,
    own_out,
    own_gate_up,
    own_down_t,
    other_gains,
    other_qkv,
    other_out,
    other_gate_up,
    other_down_t,
    tables,
    kept_out,
    kept_grad,
    sent_out,
    sent_grad,
    own_total,
    other_total,
    gains,
    qkv_t,
    out_t,
    gate_up_t,
    down_t,
    qkv_w,
    out_w,
    gate_up_w,
    down_w,
    grad_gains,
    grad_qkv,
    grad_out,
    grad_gate_up,
    grad_down,
    inputs,
    inverse1,
    normed,
    queries,
    keys,
    values,
    rows_major,
    exponents,
    attended32,
    reciprocal,
    attended,
    residual,
    inverse2,
    mid,
    gate_up,
    activated,
    grad,
    grad_low,
    grad_pre,
    grad_res_low,
    grad_att,
    grad_q,
    grad_k,
    grad_proj,
    flipped,
    grad_inputs,
):
    step = pl.program_id(0)
    section = here[0]
    series = start[0] + step
    number = series_ids[series]
    centre = median[number]
    inverse_spread = 1.0 / scale[number]
    width, length = inputs.shape[1:]
    tiles = length // TILE
    chunks = [slice(n, n + CHUNK) for n in range(0, length, CHUNK)]
    columns = [slice(n, n + TILE) for n in range(0, length, TILE)]

    @pl.when(step == 0)
    def _():
        for ref in (grad_gains, grad_qkv, grad_out, grad_gate_up, grad_down):
            ref[...] = jnp.zeros_like(ref)
        row = lax.broadcasted_iota(jnp.int32, (2, heads, HEAD, length), 2)
        values[:, :, HEAD:, :] = jnp.where(row < 2, 1.0, 0.0).astype(bfloat)
        turned = lambda w: w.astype(single).T.astype(bfloat)
        for l, (gain, qkv, out, both, down) in (
            (section, (own_gains, own_qkv, own_out, own_gate_up, own_down_t)),
            (1 - section, (other_gains, other_qkv, other_out, other_gate_up, other_down_t)),
        ):
            for part in range(2):
                row = jnp.broadcast_to(gain[part : part + 1, :], (128, width))
                gains[l, part] = row.T
            qkv_w[l] = qkv[...]
            qkv_t[l] = turned(qkv[...])
            out_w[l] = out[...]
            out_t[l] = turned(out[...])
            column = lax.broadcasted_iota(jnp.int32, both.shape, 1)
            halved = both[...].astype(single) * jnp.where(column < hidden, 0.5, 1.0)
            gate_up_w[l] = halved.astype(bfloat)
            gate_up_t[l] = halved.T.astype(bfloat)
            down_t[l] = down[...]
            down_w[l] = turned(down[...])

    def gain_of(l, part, count=CHUNK):
        return jnp.concatenate([gains[l, part]] * (count // 128), axis=1)

    inputs[0] = (raw[0].astype(single) - centre) * inverse_spread
    grad[...] = cotangent[0].astype(single)

    def rotated(block, cos, sin):
        a, b = block[:, :HALF], block[:, HALF:]
        return jnp.concatenate([a * cos - b * sin, b * cos + a * sin], axis=1)

    head_rows = lax.broadcasted_iota(jnp.int32, (HEAD, width), 0)
    head_columns = lax.broadcasted_iota(jnp.int32, (HEAD, width), 1)
    of_head = jnp.where(
        (head_columns >= head_rows * HEAD) & (head_columns < (head_rows + 1) * HEAD), 1.0, 0.0
    ).astype(bfloat)

    def forward(l, carry):
        largest_q = jnp.zeros((HEAD, CHUNK), single)
        largest_k = jnp.zeros((HEAD, CHUNK), single)
        for cs in chunks:
            u = inputs[l, :, cs]
            inv = rms_scale(u)
            inverse1[l, :, cs] = inv
            low = (u * inv * gain_of(l, 0)).astype(bfloat)
            normed[l, :, cs] = low
            projected = dot(qkv_t[l], low).reshape(3 * heads, HEAD, CHUNK)
            q, k = projected[:heads], projected[heads : 2 * heads]
            grad_q[:, :, cs] = q
            grad_k[:, :, cs] = k
            values[l, :, :HEAD, cs] = projected[2 * heads :].astype(bfloat)
            squares = lambda v: dot(of_head, (v * v).astype(bfloat).reshape(width, CHUNK))
            largest_q = jnp.maximum(largest_q, squares(q))
            largest_k = jnp.maximum(largest_k, squares(k))
        bound = jnp.max(
            jnp.max(largest_q, axis=1, keepdims=True) * jnp.max(largest_k, axis=1, keepdims=True)
        )

        def finish(h, j, product, total):
            js = slice(j * TILE, (j + 1) * TILE)
            inverse = 1.0 / total
            out = product * inverse
            reciprocal[l, h, :, js] = inverse
            attended32[l, h, :, js] = out
            attended[l, h, :, js] = out.astype(bfloat)

        def turn(three):
            hs = slice(three * 3, three * 3 + 3)
            for cs in chunks:
                q = rotated(grad_q[hs, :, cs], tables[0, :, cs], tables[1, :, cs])
                k = rotated(grad_k[hs, :, cs], tables[0, :, cs], tables[1, :, cs])
                queries[l, hs, :, cs] = q.astype(bfloat)
                keys[l, hs, :, cs] = k.astype(bfloat)
                for g in range(3):
                    rows_major[three * 3 + g, cs, :HEAD] = k[g].T.astype(bfloat)

        small = bound * EXPONENT**2 <= 1e4

        @pl.when(small)
        def _():
            pairs = lanes(tiles, heads)
            group = len(pairs) * 3 // heads
            ahead = 2
            scores, products, totals = {}, {}, {}

            def score(m):
                for side, (h, j, k) in enumerate(pairs[m]):
                    scores[m, side] = dot(
                        rows_major[h, k * TILE : (k + 1) * TILE, :HEAD],
                        queries[l, h, :, j * TILE : (j + 1) * TILE],
                    )

            turn(0)
            for m in range(ahead):
                score(m)
            for m, pair in enumerate(pairs):
                if m % group == TURN_AT and m + group < len(pairs):
                    turn(m // group + 1)
                if m + ahead < len(pairs):
                    score(m + ahead)
                ready = []
                for side, (h, j, k) in enumerate(pair):
                    e = jnp.exp2(scores.pop((m, side)) * EXPONENT)
                    if k == j:
                        e = jnp.where(causal(e), e, 0.0)
                    part = jnp.sum(e.reshape(TILE // 8, 8, TILE), axis=0)
                    totals[h, j] = totals[h, j] + part if k else part
                    e = e.astype(bfloat)
                    first = tile_start(j) + k * TILE
                    exponents[l, h, first : first + TILE, :] = e.T
                    ready.append(e)
                for side, (h, j, k) in enumerate(pair):
                    part = dot(values[l, h, :HEAD, k * TILE : (k + 1) * TILE], ready[side])
                    products[h, j] = products[h, j] + part if k else part
                    if k == j:
                        total = jnp.sum(totals.pop((h, j)), axis=0, keepdims=True)
                        finish(h, j, products.pop((h, j)), total)

        @pl.when(jnp.logical_not(small))
        def _():
            for three in range(heads // 3):
                turn(three)

            def one(h, carry):
                for j in range(tiles):
                    count = (j + 1) * TILE
                    js = slice(j * TILE, (j + 1) * TILE)
                    score = dot(rows_major[h, :count, :HEAD], queries[l, h, :, js]) * EXPONENT
                    rows = lax.broadcasted_iota(jnp.int32, score.shape, 0)
                    columns = lax.broadcasted_iota(jnp.int32, score.shape, 1) + j * TILE
                    score = jnp.where(rows <= columns, score, -1e30)
                    e = jnp.exp2(score - jnp.max(score, axis=0, keepdims=True))
                    total = jnp.sum(e, axis=0, keepdims=True)
                    e = e.astype(bfloat)
                    for k in range(j + 1):
                        first = tile_start(j) + k * TILE
                        exponents[l, h, first : first + TILE, :] = e[k * TILE : (k + 1) * TILE].T
                    finish(h, j, dot(values[l, h, :HEAD, :count], e), total)
                return carry

            lax.fori_loop(0, heads, one, 0)

        for cs in chunks:
            res = inputs[l, :, cs] + dot(out_t[l], attended[l, :, :, cs].reshape(width, CHUNK))
            residual[l, :, cs] = res
            inv = rms_scale(res)
            inverse2[l, :, cs] = inv
            mid[l, :, cs] = (res * inv * gain_of(l, 1)).astype(bfloat)
        for cs in columns:
            low = mid[l, :, cs]
            for n in range(0, hidden, ROWS):
                half = dot(gate_up_t[l, n : n + ROWS], low)
                up = dot(gate_up_t[l, hidden + n : hidden + n + ROWS], low)
                t = jnp.tanh(half)
                twice = 1.0 + t
                swish = half * twice
                gate_up[l, n : n + ROWS, cs] = up * (twice + swish * (1.0 - t))
                gate_up[l, hidden + n : hidden + n + ROWS, cs] = swish
                activated[l, n : n + ROWS, cs] = (swish * up).astype(bfloat)
        for cs in chunks:
            result = residual[l, :, cs] + dot(down_t[l], activated[l, :, cs])
            inputs[l + 1, :, cs] = result.astype(bfloat).astype(single)
        return carry

    lax.fori_loop(0, 2, forward, 0)

    def backward(turn, carry):
        l = 1 - turn
        slot = lax.rem(l + section, 2)
        for cs in columns:
            low = grad[:, cs].astype(bfloat)
            grad_low[:, cs] = low
            for n in range(0, hidden, ROWS):
                grad_act = dot(down_w[l, n : n + ROWS], low)
                for m in (n, hidden + n):
                    factor = gate_up[l, m : m + ROWS, cs]
                    grad_pre[m : m + ROWS, cs] = (grad_act * factor).astype(bfloat)
        grad_mids = [dot(gate_up_w[l], grad_pre[:, cs]) for cs in chunks]
        for n, cs in enumerate(chunks):
            half = slice(n * 2 * hidden // len(chunks), (n + 1) * 2 * hidden // len(chunks))
            grad_gate_up[slot, :, half] += dot_nt(mid[l], grad_pre[half, :])
            g = grad[:, cs]
            grad_mid = grad_mids[n]
            res, inv = residual[l, :, cs], inverse2[l, :, cs]
            grad_res, partial = rms_backward(grad_mid, res, inv, gain_of(l, 1))
            grad_gains[slot, 1] += partial
            grad_res = grad_res + g
            grad[:, cs] = grad_res
            low = grad_res.astype(bfloat)
            grad_res_low[:, cs] = low
            back = dot(out_w[l], low).astype(bfloat).astype(single).reshape(heads, HEAD, CHUNK)
            inverse = reciprocal[l, :, :, cs]
            mean = jnp.sum(back * attended32[l, :, :, cs], axis=1, keepdims=True) * -inverse
            coarse = mean.astype(bfloat).astype(single)
            row = lax.broadcasted_iota(jnp.int32, (heads, HALF, CHUNK), 1)
            extra = jnp.where(row == 0, coarse, jnp.where(row == 1, mean - coarse, 0.0))
            rest = jnp.zeros((heads, HALF, CHUNK), single)
            grad_att[:, :, cs] = jnp.concatenate([back * inverse, extra, rest], axis=1).astype(bfloat)
        grad_down[slot] += dot_nt(grad_low[...], activated[l])
        grad_out[slot] += dot_nt(attended[l].reshape(width, length), grad_res_low[...])

        def turn(three):
            for h in range(three * 3, three * 3 + 3):
                rows_major[h] = grad_att[h].T

        def turn_back(three):
            hs = slice(three * 3, three * 3 + 3)
            for cs in chunks:
                dq = rotated(grad_q[hs, :, cs], tables[2, :, cs], tables[3, :, cs])
                dk = rotated(grad_k[hs, :, cs], tables[2, :, cs], tables[3, :, cs])
                grad_proj[hs, :, cs] = dq.astype(bfloat)
                grad_proj[three * 3 + heads : three * 3 + heads + 3, :, cs] = dk.astype(bfloat)

        pairs = lanes(tiles, heads)
        group = len(pairs) * 3 // heads
        ahead = 2
        half = TILE // 2
        products, held, sums = {}, {}, {}

        def product(m, part):
            if m < len(pairs):
                for side, (h, j, k) in enumerate(pairs[m]):
                    first = j * TILE + part * half
                    products[m, side, part] = dot(
                        rows_major[h, first : first + half, :],
                        values[l, h, :, k * TILE : (k + 1) * TILE],
                    )

        def add(name, index, side, h, value):
            key = name, h, index, side
            sums[key] = sums[key] + value if key in sums else value

        turn(0)
        for m in range(ahead):
            product(m, 0)
            product(m, 1)
        for m in range(len(pairs) + 1):
            three = m // group
            if m % group == TURN_AT and m + group < len(pairs):
                turn(three + 1)
            if m % group == BACK_AT and three > 0:
                turn_back(three - 1)
            now = pairs[m] if m < len(pairs) else ()
            before = pairs[m - 1] if m > 0 else ()
            product(m + ahead, 0)
            exps = []
            for side, (h, j, k) in enumerate(now):
                first = tile_start(j) + k * TILE
                e = exponents[l, h, first : first + TILE, :]
                parts = [
                    e[p * half : (p + 1) * half] * products.pop((m, side, p)).astype(bfloat)
                    for p in range(2)
                ]
                grad_score = jnp.concatenate(parts, axis=0)
                flipped[m % 2, side] = grad_score.T
                held[m, side] = grad_score
                exps.append(e)
            for side, (h, j, k) in enumerate(now):
                js = slice(j * TILE, (j + 1) * TILE)
                add("v", k, side, h, dot(grad_att[h, :HEAD, js], exps[side]))
            product(m + ahead, 1)
            for side, (h, j, k) in enumerate(before):
                js = slice(j * TILE, (j + 1) * TILE)
                add("k", k, side, h, dot(queries[l, h, :, js], held.pop((m - 1, side))))
            for side, (h, j, k) in enumerate(before):
                ks = slice(k * TILE, (k + 1) * TILE)
                add("q", j, side, h, dot(keys[l, h, :, ks], flipped[(m - 1) % 2, side]))
            if m > 0 and m % group == 0:
                for h in range((three - 1) * 3, three * 3):
                    for name, ref in (("q", grad_q), ("k", grad_k), ("v", grad_proj)):
                        for t in range(tiles):
                            found = [sums.pop((name, h, t, n), None) for n in range(2)]
                            found = [f for f in found if f is not None]
                            place = h + 2 * heads if name == "v" else h
                            total = sum(found[1:], found[0]).astype(ref.dtype)
                            ref[place, :, t * TILE : (t + 1) * TILE] = total
        turn_back(heads // 3 - 1)

        lows = [grad_proj[:, :, cs].reshape(3 * width, CHUNK) for cs in chunks]
        grad_normeds = [dot(qkv_w[l], low) for low in lows]
        grad_qkv[slot] += dot_nt(normed[l], grad_proj[...].reshape(3 * width, length))
        for cs, grad_normed in zip(chunks, grad_normeds):
            u, inv = inputs[l, :, cs], inverse1[l, :, cs]
            grad_u, partial = rms_backward(grad_normed, u, inv, gain_of(l, 0))
            grad_gains[slot, 0] += partial
            grad_u = grad_u + grad[:, cs]
            grad[:, cs] = grad_u.astype(bfloat).astype(single)
            grad_inputs[l, :, cs] = grad_u
        return carry

    lax.fori_loop(0, 2, backward, 0)

    grad_inputs[0] = grad_inputs[0] * inverse_spread
    kept_out[0] = inputs[section + 1].astype(bfloat)
    sent_out[0] = inputs[2 - section].astype(bfloat)
    kept_grad[0] = grad_inputs[section]
    sent_grad[0] = grad_inputs[1 - section].astype(bfloat)

    @pl.when(step == pl.num_programs(0) - 1)
    def _():
        for slot, total in ((0, own_total), (1, other_total)):
            blocks = []
            for ref in (grad_gate_up, grad_down, grad_qkv, grad_out):
                for n in range(0, ref.shape[2] - 127, 128):
                    doubled = ref is grad_gate_up and n < hidden
                    blocks.append(ref[slot, :, n : n + 128] * (0.5 if doubled else 1.0))
            lane = lax.broadcasted_iota(jnp.int32, (width, 128), 1)
            spare = grad_qkv[slot, :, 3 * width - QKV_REST :]
            out_rest = grad_out[slot, :, width - OUT_REST :]
            columns = [jnp.sum(grad_gains[slot, n], axis=1, keepdims=True) for n in range(2)]
            rest = jnp.concatenate(
                [spare, out_rest] + columns
                + [jnp.zeros((width, 128 - QKV_REST - OUT_REST - 2), single)],
                axis=1,
            )
            blocks.append(rest)
            for n, block in enumerate(blocks):
                total[n * width : (n + 1) * width, :] = block.astype(total.dtype)
            used = len(blocks) * width
            total[used:, :] = jnp.zeros((total.shape[0] - used, 128), total.dtype)


def rotary_tables(length):
    frequency = 10000.0 ** (-np.arange(HALF, dtype=np.float64) / HALF)
    frequency = frequency.astype(np.float32)
    angles = np.arange(length, dtype=np.float32)[None, :] * frequency[:, None]
    cos, sin = np.cos(angles), np.sin(angles)
    tables = [cos, sin, cos * HEAD**-0.5, -sin * HEAD**-0.5]
    return np.stack(tables).astype(np.float32)


def train(section, rows, raw, series_ids, median, scale, cotangent, own, other):
    count = raw.shape[0] // 2
    width, length = raw.shape[1:]
    heads = width // HEAD
    hidden = own[4].shape[1]
    here = jnp.reshape(section, (1,)).astype(jnp.int32)
    start = jnp.reshape(section * count, (1,)).astype(jnp.int32)
    tables = jnp.asarray(rotary_tables(length))
    operands = (raw, cotangent) + own + other + (tables,)
    smem = pl.BlockSpec(memory_space=pltpu.SMEM)

    def whole(array):
        zeros = (0,) * len(array.shape)
        return pl.BlockSpec(
            array.shape, lambda i, *_: zeros, pipeline_mode=pl.Buffered(buffer_count=1)
        )

    placed_block = pl.BlockSpec((1, width, length), lambda i, here, start, ids: (start[0] + i, 0, 0))
    block = pl.BlockSpec((1, width, length), lambda i, *_: (i, 0, 0))
    shape = jax.ShapeDtypeStruct
    totals = (shape((rows, 128), single), shape((rows, 128), bfloat))
    pairs = length // TILE * (length // TILE + 1) // 2
    v = pltpu.VMEM
    scratch = [
        v((2, 2, width, 128), single),
        v((2, 3 * width, width), bfloat),
        v((2, width, width), bfloat),
        v((2, 2 * hidden, width), bfloat),
        v((2, width, hidden), bfloat),
        v((2, width, 3 * width), bfloat),
        v((2, width, width), bfloat),
        v((2, width, 2 * hidden), bfloat),
        v((2, hidden, width), bfloat),
        v((2, 2, width, 128), single),
        v((2, width, 3 * width), single),
        v((2, width, width), single),
        v((2, width, 2 * hidden), single),
        v((2, width, hidden), single),
        v((3, width, length), single),
        v((2, 1, length), single),
        v((2, width, length), bfloat),
        v((2, heads, HEAD, length), bfloat),
        v((2, heads, HEAD, length), bfloat),
        v((2, heads, 2 * HEAD, length), bfloat),
        v((heads, length, 2 * HEAD), bfloat),
        v((2, heads, pairs * TILE, TILE), bfloat),
        v((2, heads, HEAD, length), single),
        v((2, heads, 1, length), single),
        v((2, heads, HEAD, length), bfloat),
        v((2, width, length), single),
        v((2, 1, length), single),
        v((2, width, length), bfloat),
        v((2, 2 * hidden, length), single),
        v((2, hidden, length), bfloat),
        v((width, length), single),
        v((width, length), bfloat),
        v((2 * hidden, length), bfloat),
        v((width, length), bfloat),
        v((heads, 2 * HEAD, length), bfloat),
        v((heads, HEAD, length), single),
        v((heads, HEAD, length), single),
        v((3 * heads, HEAD, length), bfloat),
        v((2, 2, TILE, TILE), bfloat),
        v((2, width, length), single),
    ]
    return pl.pallas_call(
        functools.partial(train_kernel, heads, hidden),
        grid_spec=pltpu.PrefetchScalarGridSpec(
            num_scalar_prefetch=3,
            grid=(count,),
            in_specs=[smem, smem, placed_block, placed_block] + [whole(a) for a in operands[2:]],
            out_specs=[placed_block, placed_block, block, block] + [whole(t) for t in totals],
            scratch_shapes=scratch,
        ),
        out_shape=(
            shape(raw.shape, bfloat),
            shape(raw.shape, single),
            shape((count, width, length), bfloat),
            shape((count, width, length), bfloat),
        )
        + totals,
        compiler_params=pltpu.CompilerParams(vmem_limit_bytes=VMEM_LIMIT),
    )(here, start, series_ids, median, scale, *operands)


def partner():
    return {"section": 1 - lax.axis_index("section")}


def meet(peers):
    barrier = pltpu.get_barrier_semaphore()
    for peer in peers:
        pl.semaphore_signal(barrier, inc=1, device_id=peer, device_id_type=MESH)
    pl.semaphore_wait(barrier, len(peers))


def swap_kernel(count, *refs):
    own, other, send, recv = refs[:count], refs[count : 2 * count], refs[-2], refs[-1]
    meet([partner()])
    copies = [
        pltpu.make_async_remote_copy(
            src_ref=own[n],
            dst_ref=other[n],
            send_sem=send.at[n],
            recv_sem=recv.at[n],
            device_id=partner(),
            device_id_type=MESH,
        )
        for n in range(count)
    ]
    for copy in copies:
        copy.start()
    for copy in copies:
        copy.wait()


def swap_weights(weights):
    count = len(weights)
    anywhere = pl.BlockSpec(memory_space=pl.ANY)
    return pl.pallas_call(
        functools.partial(swap_kernel, count),
        out_shape=tuple(jax.ShapeDtypeStruct(w.shape, w.dtype) for w in weights),
        in_specs=[anywhere] * count,
        out_specs=[anywhere] * count,
        scratch_shapes=[pltpu.SemaphoreType.DMA((count,)), pltpu.SemaphoreType.DMA((count,))],
        compiler_params=pltpu.CompilerParams(
            collective_id=0, has_side_effects=True, vmem_limit_bytes=VMEM_LIMIT
        ),
    )(*weights)


def group_sizes(devices):
    sizes = []
    while devices > 1:
        size = 4 if devices % 4 == 0 else devices
        sizes.append(size)
        devices //= size
    return sizes


def reduce_kernel(
    sizes,
    own_total,
    other_total,
    sent_out,
    sent_grad,
    far_out,
    far_grad,
    gathered,
    arrived,
    *scratch,
):
    count = len(sizes)
    parts = scratch[:count]
    slots = scratch[count : 2 * count]
    wholes = (gathered,) + scratch[2 * count : 3 * count - 1]
    last, swap_send, swap_recv, sum_send, sum_recv, gather_send, gather_recv = scratch[3 * count - 1 :]
    me = lax.axis_index("dp")
    places, groups = [], []
    stride = 1
    for size in sizes:
        place = lax.rem(lax.div(me, stride), size)
        peers = []
        for turn in range(1, size):
            other = lax.rem(place + turn, size)
            peers.append((other, {"dp": me + (other - place) * stride}))
        places.append(place)
        groups.append(peers)
        stride *= size
    meet([partner()] + [device for peers in groups for _, device in peers])

    def copy(source, target, send, recv, device):
        c = pltpu.make_async_remote_copy(
            src_ref=source,
            dst_ref=target,
            send_sem=send,
            recv_sem=recv,
            device_id=device,
            device_id_type=MESH,
        )
        c.start()
        return c

    near = copy(other_total, arrived, swap_send.at[0], swap_recv.at[0], partner())
    near.wait()
    far = [
        copy(sent_out, far_out, swap_send.at[1], swap_recv.at[1], partner()),
        copy(sent_grad, far_grad, swap_send.at[2], swap_recv.at[2], partner()),
    ]
    parts[0][...] = (own_total[...] + arrived[...].astype(single)).astype(bfloat)
    first = 0
    starts = []
    for n, size in enumerate(sizes):
        chunk = parts[n].shape[0] // size
        copies = []
        for turn, (other, device) in enumerate(groups[n]):
            copies.append(
                copy(
                    parts[n].at[pl.ds(pl.multiple_of(other * chunk, 16), chunk)],
                    slots[n].at[turn],
                    sum_send.at[first + turn],
                    sum_recv.at[first + turn],
                    device,
                )
            )
        total = parts[n][pl.ds(pl.multiple_of(places[n] * chunk, 16), chunk), :].astype(single)
        for turn, c in enumerate(copies):
            c.wait()
            total = total + slots[n][turn].astype(single)
        target = parts[n + 1] if n + 1 < count else last
        target[...] = total.astype(bfloat)
        starts.append(first)
        first += size - 1
    source = last
    for n in reversed(range(count)):
        chunk = parts[n].shape[0] // sizes[n]
        mine = pl.ds(pl.multiple_of(places[n] * chunk, 16), chunk)
        copies = []
        for turn, (_, device) in enumerate(groups[n]):
            k = starts[n] + turn
            copies.append(
                copy(source, wholes[n].at[mine], gather_send.at[k], gather_recv.at[k], device)
            )
        wholes[n][mine, :] = source[...]
        for c in copies:
            c.wait()
        source = wholes[n]
    for c in far:
        c.wait()


def finish_kernel(
    place,
    gathered,
    far_out,
    far_grad,
    kept_out,
    kept_grad,
    layer_outputs,
    input_grads,
    grad_gains,
    grad_qkv,
    grad_out,
    grad_gate_up,
    grad_down,
):
    layer_outputs[...] = far_out[...]
    input_grads[...] = far_grad[...].astype(single)

    @pl.when((pl.program_id(0) == 0) & (pl.program_id(1) == 0))
    def _():
        width = grad_qkv.shape[0]
        block = 0
        for ref in (grad_gate_up, grad_down, grad_qkv, grad_out):
            for n in range(0, ref.shape[1] - 127, 128):
                rows = slice(block * width, (block + 1) * width)
                ref[:, n : n + 128] = gathered[rows, :].astype(single)
                block += 1
        rest = gathered[block * width : (block + 1) * width, :].astype(single)
        grad_qkv[:, 3 * width - QKV_REST :] = rest[:, :QKV_REST]
        grad_out[:, width - OUT_REST :] = rest[:, QKV_REST : QKV_REST + OUT_REST]
        grad_gains[...] = rest.T[QKV_REST + OUT_REST : QKV_REST + OUT_REST + 2, :]


def finish(place, gathered, far_out, far_grad, kept_out, kept_grad, hidden):
    shape = jax.ShapeDtypeStruct
    count, width, length = far_out.shape
    anywhere = pl.BlockSpec(memory_space=pl.ANY)
    part = width // 3
    block = pl.BlockSpec((1, part, length), lambda i, n, place: (i, n, 0))
    placed = pl.BlockSpec((1, part, length), lambda i, n, place: (place[0] + i, n, 0))
    grads = (
        shape((2, width), single),
        shape((width, 3 * width), single),
        shape((width, width), single),
        shape((width, 2 * hidden), single),
        shape((width, hidden), single),
    )

    def whole(array):
        return pl.BlockSpec(
            array.shape, lambda i, n, place: (0, 0), pipeline_mode=pl.Buffered(buffer_count=1)
        )

    return pl.pallas_call(
        finish_kernel,
        grid_spec=pltpu.PrefetchScalarGridSpec(
            num_scalar_prefetch=1,
            grid=(count, 3),
            in_specs=[whole(gathered), block, block, anywhere, anywhere],
            out_specs=[placed, placed] + [whole(g) for g in grads],
        ),
        out_shape=(shape(kept_out.shape, bfloat), shape(kept_grad.shape, single)) + grads,
        input_output_aliases={4: 0, 5: 1},
        compiler_params=pltpu.CompilerParams(vmem_limit_bytes=VMEM_LIMIT),
    )(place, gathered, far_out, far_grad, kept_out, kept_grad)


def reduce(devices, own_total, other_total, sent_out, sent_grad):
    sizes = group_sizes(devices)
    rows = own_total.shape[0]
    v = pltpu.VMEM
    shape = jax.ShapeDtypeStruct
    parts, slots, left = [], [], rows
    for size in sizes:
        parts.append(v((left, 128), bfloat))
        left //= size
        slots.append(v((size - 1, left, 128), bfloat))
    links = sum(size - 1 for size in sizes)
    dma = pltpu.SemaphoreType.DMA
    anywhere = pl.BlockSpec(memory_space=pl.ANY)
    vmem = pl.BlockSpec(memory_space=pltpu.VMEM)
    return pl.pallas_call(
        functools.partial(reduce_kernel, sizes),
        out_shape=(
            shape(sent_out.shape, bfloat),
            shape(sent_grad.shape, bfloat),
            shape((rows, 128), bfloat),
        ),
        in_specs=[vmem, vmem, anywhere, anywhere],
        out_specs=[anywhere, anywhere, vmem],
        scratch_shapes=[v((rows, 128), bfloat)]
        + parts
        + slots
        + parts[1:]
        + [v((left, 128), bfloat), dma((3,)), dma((3,))]
        + [dma((links,))] * 4,
        compiler_params=pltpu.CompilerParams(
            collective_id=1, has_side_effects=True, vmem_limit_bytes=VMEM_LIMIT
        ),
    )(own_total, other_total, sent_out, sent_grad)


def on_device(
    devices,
    raw,
    series_ids,
    median,
    scale,
    cotangent,
    norm_gains,
    qkv_weight,
    out_weight,
    gate_up_weight,
    down_weight,
):
    section = lax.axis_index("section")
    turned = lambda a: jnp.swapaxes(a, -1, -2)
    count = raw.shape[0] // 2
    width, hidden = raw.shape[2], down_weight.shape[1]
    own = (norm_gains[0], qkv_weight[0], out_weight[0], gate_up_weight[0], turned(down_weight[0]))
    other = swap_weights(own)
    blocks = 14
    rows = -(-blocks * width // (16 * devices)) * 16 * devices
    kept_out, kept_grad, sent_out, sent_grad, own_total, other_total = train(
        section, rows, turned(raw), series_ids, median, scale, turned(cotangent), own, other
    )
    far_out, far_grad, gathered = reduce(devices, own_total, other_total, sent_out, sent_grad)
    place = jnp.reshape((1 - section) * count, (1,)).astype(jnp.int32)
    layer_outputs, input_grads, gain, qkv, out, gate_up, down = finish(
        place, gathered, far_out, far_grad, kept_out, kept_grad, hidden
    )
    return (
        turned(layer_outputs)[None],
        turned(input_grads)[None],
        gain[None],
        qkv[None],
        out[None],
        gate_up[None],
        turned(down)[None],
    )


def solution(mesh):
    placed = (
        P("dp", None, None),
        P("dp"),
        P(),
        P(),
        P("dp", None, None),
        P("section", None, None),
        P("section", None, None),
        P("section", None, None),
        P("section", None, None),
        P("section", None, None),
    )
    return jax.shard_map(
        functools.partial(on_device, mesh.shape["dp"]),
        mesh=mesh,
        in_specs=placed,
        out_specs=(
            P("section", "dp", None, None),
            P("section", "dp", None, None),
            P("section", None, None),
            P("section", None, None),
            P("section", None, None),
            P("section", None, None),
            P("section", None, None),
        ),
        check_vma=False,
    )
```

```python
import functools
import math

import jax
import jax.numpy as jnp
import numpy as np
from jax import lax
from jax.experimental import pallas as pl
from jax.experimental.pallas import tpu as pltpu
from jax.sharding import PartitionSpec as P

HEAD = 16
HALF = HEAD // 2
TILE = 256
CHUNK = 512
ROWS = 128
TURN_AT = 6
BACK_AT = 8
VMEM_LIMIT = 64 * 2**20 - 2**16
EPSILON = 1e-06
EXPONENT = HEAD**-0.5 * math.log2(math.e)
QKV_REST = 48
OUT_REST = 16
MESH = pl.DeviceIdType.MESH
bfloat = jnp.bfloat16
single = jnp.float32


def dot(left, right):
    return jnp.dot(left, right, preferred_element_type=single)


def dot_nt(left, right):
    return lax.dot_general(left, right, (((1,), (1,)), ((), ())), preferred_element_type=single)


def rms_scale(values):
    return lax.rsqrt(jnp.mean(values * values, axis=0, keepdims=True) + EPSILON)


def rms_backward(grad_normed, values, inverse, gain):
    scaled = grad_normed * gain
    centre = jnp.mean(scaled * values, axis=0, keepdims=True)
    grad_values = inverse * scaled - values * (inverse * inverse * inverse * centre)
    product = grad_normed * values * inverse
    partial = product[:, :128]
    for start in range(128, product.shape[1], 128):
        partial = partial + product[:, start : start + 128]
    return grad_values, partial


def causal(block):
    rows = lax.broadcasted_iota(jnp.int32, block.shape, 0)
    columns = lax.broadcasted_iota(jnp.int32, block.shape, 1)
    return rows <= columns


def tile_start(j):
    return j * (j + 1) // 2 * TILE


def lanes(tiles, heads):
    pairs = []
    for first in range(0, heads, 3):
        full = [(j, k) for j in range(tiles) for k in range(j + 1)]
        sides = [[(first + side, j, k) for j, k in full] for side in range(2)]
        for j in reversed(range(tiles)):
            side = min(sides, key=len)
            side += [(first + 2, j, k) for k in range(j + 1)]
        pairs += zip(*sides)
    return pairs


def train_kernel(
    heads,
    hidden,
    here,
    start,
    series_ids,
    median,
    scale,
    raw,
    cotangent,
    own_gains,
    own_qkv,
    own_out,
    own_gate_up,
    own_down_t,
    other_gains,
    other_qkv,
    other_out,
    other_gate_up,
    other_down_t,
    tables,
    kept_out,
    kept_grad,
    sent_out,
    sent_grad,
    own_total,
    other_total,
    gains,
    qkv_t,
    out_t,
    gate_up_t,
    down_t,
    qkv_w,
    out_w,
    gate_up_w,
    down_w,
    grad_gains,
    grad_qkv,
    grad_out,
    grad_gate_up,
    grad_down,
    inputs,
    inverse1,
    normed,
    queries,
    keys,
    values,
    rows_major,
    exponents,
    attended32,
    reciprocal,
    attended,
    residual,
    inverse2,
    mid,
    gate_up,
    activated,
    grad,
    grad_low,
    grad_pre,
    grad_res_low,
    grad_att,
    grad_q,
    grad_k,
    grad_proj,
    flipped,
    grad_inputs,
):
    step = pl.program_id(0)
    section = here[0]
    series = start[0] + step
    number = series_ids[series]
    centre = median[number]
    inverse_spread = 1.0 / scale[number]
    width, length = inputs.shape[1:]
    tiles = length // TILE
    chunks = [slice(n, n + CHUNK) for n in range(0, length, CHUNK)]
    columns = [slice(n, n + TILE) for n in range(0, length, TILE)]

    @pl.when(step == 0)
    def _():
        for ref in (grad_gains, grad_qkv, grad_out, grad_gate_up, grad_down):
            ref[...] = jnp.zeros_like(ref)
        row = lax.broadcasted_iota(jnp.int32, (2, heads, HEAD, length), 2)
        values[:, :, HEAD:, :] = jnp.where(row < 2, 1.0, 0.0).astype(bfloat)
        turned = lambda w: w.astype(single).T.astype(bfloat)
        for l, (gain, qkv, out, both, down) in (
            (section, (own_gains, own_qkv, own_out, own_gate_up, own_down_t)),
            (1 - section, (other_gains, other_qkv, other_out, other_gate_up, other_down_t)),
        ):
            for part in range(2):
                row = jnp.broadcast_to(gain[part : part + 1, :], (128, width))
                gains[l, part] = row.T
            qkv_w[l] = qkv[...]
            qkv_t[l] = turned(qkv[...])
            out_w[l] = out[...]
            out_t[l] = turned(out[...])
            column = lax.broadcasted_iota(jnp.int32, both.shape, 1)
            halved = both[...].astype(single) * jnp.where(column < hidden, 0.5, 1.0)
            gate_up_w[l] = halved.astype(bfloat)
            gate_up_t[l] = halved.T.astype(bfloat)
            down_t[l] = down[...]
            down_w[l] = turned(down[...])

    def gain_of(l, part, count=CHUNK):
        return jnp.concatenate([gains[l, part]] * (count // 128), axis=1)

    inputs[0] = (raw[0].astype(single) - centre) * inverse_spread
    grad[...] = cotangent[0].astype(single)

    def rotated(block, cos, sin):
        a, b = block[:, :HALF], block[:, HALF:]
        return jnp.concatenate([a * cos - b * sin, b * cos + a * sin], axis=1)

    head_rows = lax.broadcasted_iota(jnp.int32, (HEAD, width), 0)
    head_columns = lax.broadcasted_iota(jnp.int32, (HEAD, width), 1)
    of_head = jnp.where(
        (head_columns >= head_rows * HEAD) & (head_columns < (head_rows + 1) * HEAD), 1.0, 0.0
    ).astype(bfloat)

    def forward(l, carry):
        largest_q = jnp.zeros((HEAD, CHUNK), single)
        largest_k = jnp.zeros((HEAD, CHUNK), single)
        for cs in chunks:
            u = inputs[l, :, cs]
            inv = rms_scale(u)
            inverse1[l, :, cs] = inv
            low = (u * inv * gain_of(l, 0)).astype(bfloat)
            normed[l, :, cs] = low
            projected = dot(qkv_t[l], low).reshape(3 * heads, HEAD, CHUNK)
            q, k = projected[:heads], projected[heads : 2 * heads]
            grad_q[:, :, cs] = q
            grad_k[:, :, cs] = k
            values[l, :, :HEAD, cs] = projected[2 * heads :].astype(bfloat)
            squares = lambda v: dot(of_head, (v * v).astype(bfloat).reshape(width, CHUNK))
            largest_q = jnp.maximum(largest_q, squares(q))
            largest_k = jnp.maximum(largest_k, squares(k))
        bound = jnp.max(
            jnp.max(largest_q, axis=1, keepdims=True) * jnp.max(largest_k, axis=1, keepdims=True)
        )

        def finish(h, j, product, total):
            js = slice(j * TILE, (j + 1) * TILE)
            inverse = 1.0 / total
            out = product * inverse
            reciprocal[l, h, :, js] = inverse
            attended32[l, h, :, js] = out
            attended[l, h, :, js] = out.astype(bfloat)

        def turn(three):
            hs = slice(three * 3, three * 3 + 3)
            for cs in chunks:
                q = rotated(grad_q[hs, :, cs], tables[0, :, cs], tables[1, :, cs])
                k = rotated(grad_k[hs, :, cs], tables[0, :, cs], tables[1, :, cs])
                queries[l, hs, :, cs] = q.astype(bfloat)
                keys[l, hs, :, cs] = k.astype(bfloat)
                for g in range(3):
                    rows_major[three * 3 + g, cs, :HEAD] = k[g].T.astype(bfloat)

        small = bound * EXPONENT**2 <= 1e4

        @pl.when(small)
        def _():
            pairs = lanes(tiles, heads)
            group = len(pairs) * 3 // heads
            ahead = 2
            scores, products, totals = {}, {}, {}

            def score(m):
                for side, (h, j, k) in enumerate(pairs[m]):
                    scores[m, side] = dot(
                        rows_major[h, k * TILE : (k + 1) * TILE, :HEAD],
                        queries[l, h, :, j * TILE : (j + 1) * TILE],
                    )

            turn(0)
            for m in range(ahead):
                score(m)
            for m, pair in enumerate(pairs):
                if m % group == TURN_AT and m + group < len(pairs):
                    turn(m // group + 1)
                if m + ahead < len(pairs):
                    score(m + ahead)
                ready = []
                for side, (h, j, k) in enumerate(pair):
                    e = jnp.exp2(scores.pop((m, side)) * EXPONENT)
                    if k == j:
                        e = jnp.where(causal(e), e, 0.0)
                    part = jnp.sum(e.reshape(TILE // 8, 8, TILE), axis=0)
                    totals[h, j] = totals[h, j] + part if k else part
                    e = e.astype(bfloat)
                    first = tile_start(j) + k * TILE
                    exponents[l, h, first : first + TILE, :] = e.T
                    ready.append(e)
                for side, (h, j, k) in enumerate(pair):
                    part = dot(values[l, h, :HEAD, k * TILE : (k + 1) * TILE], ready[side])
                    products[h, j] = products[h, j] + part if k else part
                    if k == j:
                        total = jnp.sum(totals.pop((h, j)), axis=0, keepdims=True)
                        finish(h, j, products.pop((h, j)), total)

        @pl.when(jnp.logical_not(small))
        def _():
            for three in range(heads // 3):
                turn(three)

            def one(h, carry):
                for j in range(tiles):
                    count = (j + 1) * TILE
                    js = slice(j * TILE, (j + 1) * TILE)
                    score = dot(rows_major[h, :count, :HEAD], queries[l, h, :, js]) * EXPONENT
                    rows = lax.broadcasted_iota(jnp.int32, score.shape, 0)
                    columns = lax.broadcasted_iota(jnp.int32, score.shape, 1) + j * TILE
                    score = jnp.where(rows <= columns, score, -1e30)
                    e = jnp.exp2(score - jnp.max(score, axis=0, keepdims=True))
                    total = jnp.sum(e, axis=0, keepdims=True)
                    e = e.astype(bfloat)
                    for k in range(j + 1):
                        first = tile_start(j) + k * TILE
                        exponents[l, h, first : first + TILE, :] = e[k * TILE : (k + 1) * TILE].T
                    finish(h, j, dot(values[l, h, :HEAD, :count], e), total)
                return carry

            lax.fori_loop(0, heads, one, 0)

        for cs in chunks:
            res = inputs[l, :, cs] + dot(out_t[l], attended[l, :, :, cs].reshape(width, CHUNK))
            residual[l, :, cs] = res
            inv = rms_scale(res)
            inverse2[l, :, cs] = inv
            mid[l, :, cs] = (res * inv * gain_of(l, 1)).astype(bfloat)
        for cs in columns:
            low = mid[l, :, cs]
            for n in range(0, hidden, ROWS):
                half = dot(gate_up_t[l, n : n + ROWS], low)
                up = dot(gate_up_t[l, hidden + n : hidden + n + ROWS], low)
                t = jnp.tanh(half)
                twice = 1.0 + t
                swish = half * twice
                gate_up[l, n : n + ROWS, cs] = up * (twice + swish * (1.0 - t))
                gate_up[l, hidden + n : hidden + n + ROWS, cs] = swish
                activated[l, n : n + ROWS, cs] = (swish * up).astype(bfloat)
        for cs in chunks:
            result = residual[l, :, cs] + dot(down_t[l], activated[l, :, cs])
            inputs[l + 1, :, cs] = result.astype(bfloat).astype(single)
        return carry

    lax.fori_loop(0, 2, forward, 0)

    def backward(turn, carry):
        l = 1 - turn
        slot = lax.rem(l + section, 2)
        for cs in columns:
            low = grad[:, cs].astype(bfloat)
            grad_low[:, cs] = low
            for n in range(0, hidden, ROWS):
                grad_act = dot(down_w[l, n : n + ROWS], low)
                for m in (n, hidden + n):
                    factor = gate_up[l, m : m + ROWS, cs]
                    grad_pre[m : m + ROWS, cs] = (grad_act * factor).astype(bfloat)
        grad_mids = [dot(gate_up_w[l], grad_pre[:, cs]) for cs in chunks]
        for n, cs in enumerate(chunks):
            half = slice(n * 2 * hidden // len(chunks), (n + 1) * 2 * hidden // len(chunks))
            grad_gate_up[slot, :, half] += dot_nt(mid[l], grad_pre[half, :])
            g = grad[:, cs]
            grad_mid = grad_mids[n]
            res, inv = residual[l, :, cs], inverse2[l, :, cs]
            grad_res, partial = rms_backward(grad_mid, res, inv, gain_of(l, 1))
            grad_gains[slot, 1] += partial
            grad_res = grad_res + g
            grad[:, cs] = grad_res
            low = grad_res.astype(bfloat)
            grad_res_low[:, cs] = low
            back = dot(out_w[l], low).astype(bfloat).astype(single).reshape(heads, HEAD, CHUNK)
            inverse = reciprocal[l, :, :, cs]
            mean = jnp.sum(back * attended32[l, :, :, cs], axis=1, keepdims=True) * -inverse
            coarse = mean.astype(bfloat).astype(single)
            row = lax.broadcasted_iota(jnp.int32, (heads, HALF, CHUNK), 1)
            extra = jnp.where(row == 0, coarse, jnp.where(row == 1, mean - coarse, 0.0))
            rest = jnp.zeros((heads, HALF, CHUNK), single)
            grad_att[:, :, cs] = jnp.concatenate([back * inverse, extra, rest], axis=1).astype(bfloat)
        grad_down[slot] += dot_nt(grad_low[...], activated[l])
        grad_out[slot] += dot_nt(attended[l].reshape(width, length), grad_res_low[...])

        def turn(three):
            for h in range(three * 3, three * 3 + 3):
                rows_major[h] = grad_att[h].T

        def turn_back(three):
            hs = slice(three * 3, three * 3 + 3)
            for cs in chunks:
                dq = rotated(grad_q[hs, :, cs], tables[2, :, cs], tables[3, :, cs])
                dk = rotated(grad_k[hs, :, cs], tables[2, :, cs], tables[3, :, cs])
                grad_proj[hs, :, cs] = dq.astype(bfloat)
                grad_proj[three * 3 + heads : three * 3 + heads + 3, :, cs] = dk.astype(bfloat)

        pairs = lanes(tiles, heads)
        group = len(pairs) * 3 // heads
        ahead = 2
        half = TILE // 2
        products, held, sums = {}, {}, {}

        def product(m, part):
            if m < len(pairs):
                for side, (h, j, k) in enumerate(pairs[m]):
                    first = j * TILE + part * half
                    products[m, side, part] = dot(
                        rows_major[h, first : first + half, :],
                        values[l, h, :, k * TILE : (k + 1) * TILE],
                    )

        def add(name, index, side, h, value):
            key = name, h, index, side
            sums[key] = sums[key] + value if key in sums else value

        turn(0)
        for m in range(ahead):
            product(m, 0)
            product(m, 1)
        for m in range(len(pairs) + 1):
            three = m // group
            if m % group == TURN_AT and m + group < len(pairs):
                turn(three + 1)
            if m % group == BACK_AT and three > 0:
                turn_back(three - 1)
            now = pairs[m] if m < len(pairs) else ()
            before = pairs[m - 1] if m > 0 else ()
            product(m + ahead, 0)
            exps = []
            for side, (h, j, k) in enumerate(now):
                first = tile_start(j) + k * TILE
                e = exponents[l, h, first : first + TILE, :]
                parts = [
                    e[p * half : (p + 1) * half] * products.pop((m, side, p)).astype(bfloat)
                    for p in range(2)
                ]
                grad_score = jnp.concatenate(parts, axis=0)
                flipped[m % 2, side] = grad_score.T
                held[m, side] = grad_score
                exps.append(e)
            for side, (h, j, k) in enumerate(now):
                js = slice(j * TILE, (j + 1) * TILE)
                add("v", k, side, h, dot(grad_att[h, :HEAD, js], exps[side]))
            product(m + ahead, 1)
            for side, (h, j, k) in enumerate(before):
                js = slice(j * TILE, (j + 1) * TILE)
                add("k", k, side, h, dot(queries[l, h, :, js], held.pop((m - 1, side))))
            for side, (h, j, k) in enumerate(before):
                ks = slice(k * TILE, (k + 1) * TILE)
                add("q", j, side, h, dot(keys[l, h, :, ks], flipped[(m - 1) % 2, side]))
            if m > 0 and m % group == 0:
                for h in range((three - 1) * 3, three * 3):
                    for name, ref in (("q", grad_q), ("k", grad_k), ("v", grad_proj)):
                        for t in range(tiles):
                            found = [sums.pop((name, h, t, n), None) for n in range(2)]
                            found = [f for f in found if f is not None]
                            place = h + 2 * heads if name == "v" else h
                            total = sum(found[1:], found[0]).astype(ref.dtype)
                            ref[place, :, t * TILE : (t + 1) * TILE] = total
        turn_back(heads // 3 - 1)

        lows = [grad_proj[:, :, cs].reshape(3 * width, CHUNK) for cs in chunks]
        grad_normeds = [dot(qkv_w[l], low) for low in lows]
        grad_qkv[slot] += dot_nt(normed[l], grad_proj[...].reshape(3 * width, length))
        for cs, grad_normed in zip(chunks, grad_normeds):
            u, inv = inputs[l, :, cs], inverse1[l, :, cs]
            grad_u, partial = rms_backward(grad_normed, u, inv, gain_of(l, 0))
            grad_gains[slot, 0] += partial
            grad_u = grad_u + grad[:, cs]
            grad[:, cs] = grad_u.astype(bfloat).astype(single)
            grad_inputs[l, :, cs] = grad_u
        return carry

    lax.fori_loop(0, 2, backward, 0)

    grad_inputs[0] = grad_inputs[0] * inverse_spread
    kept_out[0] = inputs[section + 1].astype(bfloat)
    sent_out[0] = inputs[2 - section].astype(bfloat)
    kept_grad[0] = grad_inputs[section]
    sent_grad[0] = grad_inputs[1 - section].astype(bfloat)

    @pl.when(step == pl.num_programs(0) - 1)
    def _():
        for slot, total in ((0, own_total), (1, other_total)):
            blocks = []
            for ref in (grad_gate_up, grad_down, grad_qkv, grad_out):
                for n in range(0, ref.shape[2] - 127, 128):
                    doubled = ref is grad_gate_up and n < hidden
                    blocks.append(ref[slot, :, n : n + 128] * (0.5 if doubled else 1.0))
            lane = lax.broadcasted_iota(jnp.int32, (width, 128), 1)
            spare = grad_qkv[slot, :, 3 * width - QKV_REST :]
            out_rest = grad_out[slot, :, width - OUT_REST :]
            columns = [jnp.sum(grad_gains[slot, n], axis=1, keepdims=True) for n in range(2)]
            rest = jnp.concatenate(
                [spare, out_rest] + columns
                + [jnp.zeros((width, 128 - QKV_REST - OUT_REST - 2), single)],
                axis=1,
            )
            blocks.append(rest)
            for n, block in enumerate(blocks):
                total[n * width : (n + 1) * width, :] = block.astype(total.dtype)
            used = len(blocks) * width
            total[used:, :] = jnp.zeros((total.shape[0] - used, 128), total.dtype)


def rotary_tables(length):
    frequency = 10000.0 ** (-np.arange(HALF, dtype=np.float64) / HALF)
    frequency = frequency.astype(np.float32)
    angles = np.arange(length, dtype=np.float32)[None, :] * frequency[:, None]
    cos, sin = np.cos(angles), np.sin(angles)
    tables = [cos, sin, cos * HEAD**-0.5, -sin * HEAD**-0.5]
    return np.stack(tables).astype(np.float32)


def train(section, rows, raw, series_ids, median, scale, cotangent, own, other):
    count = raw.shape[0] // 2
    width, length = raw.shape[1:]
    heads = width // HEAD
    hidden = own[4].shape[1]
    here = jnp.reshape(section, (1,)).astype(jnp.int32)
    start = jnp.reshape(section * count, (1,)).astype(jnp.int32)
    tables = jnp.asarray(rotary_tables(length))
    operands = (raw, cotangent) + own + other + (tables,)
    smem = pl.BlockSpec(memory_space=pltpu.SMEM)

    def whole(array):
        zeros = (0,) * len(array.shape)
        return pl.BlockSpec(
            array.shape, lambda i, *_: zeros, pipeline_mode=pl.Buffered(buffer_count=1)
        )

    placed_block = pl.BlockSpec((1, width, length), lambda i, here, start, ids: (start[0] + i, 0, 0))
    block = pl.BlockSpec((1, width, length), lambda i, *_: (i, 0, 0))
    shape = jax.ShapeDtypeStruct
    totals = (shape((rows, 128), single), shape((rows, 128), bfloat))
    pairs = length // TILE * (length // TILE + 1) // 2
    v = pltpu.VMEM
    scratch = [
        v((2, 2, width, 128), single),
        v((2, 3 * width, width), bfloat),
        v((2, width, width), bfloat),
        v((2, 2 * hidden, width), bfloat),
        v((2, width, hidden), bfloat),
        v((2, width, 3 * width), bfloat),
        v((2, width, width), bfloat),
        v((2, width, 2 * hidden), bfloat),
        v((2, hidden, width), bfloat),
        v((2, 2, width, 128), single),
        v((2, width, 3 * width), single),
        v((2, width, width), single),
        v((2, width, 2 * hidden), single),
        v((2, width, hidden), single),
        v((3, width, length), single),
        v((2, 1, length), single),
        v((2, width, length), bfloat),
        v((2, heads, HEAD, length), bfloat),
        v((2, heads, HEAD, length), bfloat),
        v((2, heads, 2 * HEAD, length), bfloat),
        v((heads, length, 2 * HEAD), bfloat),
        v((2, heads, pairs * TILE, TILE), bfloat),
        v((2, heads, HEAD, length), single),
        v((2, heads, 1, length), single),
        v((2, heads, HEAD, length), bfloat),
        v((2, width, length), single),
        v((2, 1, length), single),
        v((2, width, length), bfloat),
        v((2, 2 * hidden, length), single),
        v((2, hidden, length), bfloat),
        v((width, length), single),
        v((width, length), bfloat),
        v((2 * hidden, length), bfloat),
        v((width, length), bfloat),
        v((heads, 2 * HEAD, length), bfloat),
        v((heads, HEAD, length), single),
        v((heads, HEAD, length), single),
        v((3 * heads, HEAD, length), bfloat),
        v((2, 2, TILE, TILE), bfloat),
        v((2, width, length), single),
    ]
    return pl.pallas_call(
        functools.partial(train_kernel, heads, hidden),
        grid_spec=pltpu.PrefetchScalarGridSpec(
            num_scalar_prefetch=3,
            grid=(count,),
            in_specs=[smem, smem, placed_block, placed_block] + [whole(a) for a in operands[2:]],
            out_specs=[placed_block, placed_block, block, block] + [whole(t) for t in totals],
            scratch_shapes=scratch,
        ),
        out_shape=(
            shape(raw.shape, bfloat),
            shape(raw.shape, single),
            shape((count, width, length), bfloat),
            shape((count, width, length), bfloat),
        )
        + totals,
        compiler_params=pltpu.CompilerParams(vmem_limit_bytes=VMEM_LIMIT),
    )(here, start, series_ids, median, scale, *operands)


def partner():
    return {"section": 1 - lax.axis_index("section")}


def meet(peers):
    barrier = pltpu.get_barrier_semaphore()
    for peer in peers:
        pl.semaphore_signal(barrier, inc=1, device_id=peer, device_id_type=MESH)
    pl.semaphore_wait(barrier, len(peers))


def swap_kernel(count, *refs):
    own, other, send, recv = refs[:count], refs[count : 2 * count], refs[-2], refs[-1]
    meet([partner()])
    copies = [
        pltpu.make_async_remote_copy(
            src_ref=own[n],
            dst_ref=other[n],
            send_sem=send.at[n],
            recv_sem=recv.at[n],
            device_id=partner(),
            device_id_type=MESH,
        )
        for n in range(count)
    ]
    for copy in copies:
        copy.start()
    for copy in copies:
        copy.wait()


def swap_weights(weights):
    count = len(weights)
    anywhere = pl.BlockSpec(memory_space=pl.ANY)
    return pl.pallas_call(
        functools.partial(swap_kernel, count),
        out_shape=tuple(jax.ShapeDtypeStruct(w.shape, w.dtype) for w in weights),
        in_specs=[anywhere] * count,
        out_specs=[anywhere] * count,
        scratch_shapes=[pltpu.SemaphoreType.DMA((count,)), pltpu.SemaphoreType.DMA((count,))],
        compiler_params=pltpu.CompilerParams(
            collective_id=0, has_side_effects=True, vmem_limit_bytes=VMEM_LIMIT
        ),
    )(*weights)


def group_sizes(devices):
    sizes = []
    while devices > 1:
        size = 4 if devices % 4 == 0 else devices
        sizes.append(size)
        devices //= size
    return sizes


def reduce_kernel(
    sizes,
    own_total,
    other_total,
    sent_out,
    sent_grad,
    far_out,
    far_grad,
    gathered,
    arrived,
    *scratch,
):
    count = len(sizes)
    parts = scratch[:count]
    slots = scratch[count : 2 * count]
    wholes = (gathered,) + scratch[2 * count : 3 * count - 1]
    last, swap_send, swap_recv, sum_send, sum_recv, gather_send, gather_recv = scratch[3 * count - 1 :]
    me = lax.axis_index("dp")
    places, groups = [], []
    stride = 1
    for size in sizes:
        place = lax.rem(lax.div(me, stride), size)
        peers = []
        for turn in range(1, size):
            other = lax.rem(place + turn, size)
            peers.append((other, {"dp": me + (other - place) * stride}))
        places.append(place)
        groups.append(peers)
        stride *= size
    meet([partner()] + [device for peers in groups for _, device in peers])

    def copy(source, target, send, recv, device):
        c = pltpu.make_async_remote_copy(
            src_ref=source,
            dst_ref=target,
            send_sem=send,
            recv_sem=recv,
            device_id=device,
            device_id_type=MESH,
        )
        c.start()
        return c

    near = copy(other_total, arrived, swap_send.at[0], swap_recv.at[0], partner())
    near.wait()
    far = [
        copy(sent_out, far_out, swap_send.at[1], swap_recv.at[1], partner()),
        copy(sent_grad, far_grad, swap_send.at[2], swap_recv.at[2], partner()),
    ]
    parts[0][...] = (own_total[...] + arrived[...].astype(single)).astype(bfloat)
    first = 0
    starts = []
    for n, size in enumerate(sizes):
        chunk = parts[n].shape[0] // size
        copies = []
        for turn, (other, device) in enumerate(groups[n]):
            copies.append(
                copy(
                    parts[n].at[pl.ds(pl.multiple_of(other * chunk, 16), chunk)],
                    slots[n].at[turn],
                    sum_send.at[first + turn],
                    sum_recv.at[first + turn],
                    device,
                )
            )
        total = parts[n][pl.ds(pl.multiple_of(places[n] * chunk, 16), chunk), :].astype(single)
        for turn, c in enumerate(copies):
            c.wait()
            total = total + slots[n][turn].astype(single)
        target = parts[n + 1] if n + 1 < count else last
        target[...] = total.astype(bfloat)
        starts.append(first)
        first += size - 1
    source = last
    for n in reversed(range(count)):
        chunk = parts[n].shape[0] // sizes[n]
        mine = pl.ds(pl.multiple_of(places[n] * chunk, 16), chunk)
        copies = []
        for turn, (_, device) in enumerate(groups[n]):
            k = starts[n] + turn
            copies.append(
                copy(source, wholes[n].at[mine], gather_send.at[k], gather_recv.at[k], device)
            )
        wholes[n][mine, :] = source[...]
        for c in copies:
            c.wait()
        source = wholes[n]
    for c in far:
        c.wait()


def finish_kernel(
    gathered_far,
    far_out,
    far_grad,
    kept_out,
    kept_grad,
    layer_outputs,
    input_grads,
    grad_gains,
    grad_qkv,
    grad_out,
    grad_gate_up,
    grad_down,
    gathered,
    passed,
    narrow,
    wide,
    arrive,
    leave,
):
    count = far_out.shape[0]
    place = (1 - lax.axis_index("section")) * count
    outs = pltpu.make_async_copy(passed, layer_outputs.at[pl.ds(place, count)], leave.at[count])
    into = pltpu.make_async_copy(far_out, passed, arrive.at[count + 1])
    sums = pltpu.make_async_copy(gathered_far, gathered, arrive.at[count])
    reads = [pltpu.make_async_copy(far_grad.at[i], narrow.at[i], arrive.at[i]) for i in range(count)]
    writes = [
        pltpu.make_async_copy(wide.at[i], input_grads.at[place + i], leave.at[i])
        for i in range(count)
    ]
    for c in reads + [sums, into]:
        c.start()
    for i in range(count):
        reads[i].wait()
        wide[i] = narrow[i].astype(single)
        writes[i].start()
    into.wait()
    outs.start()
    sums.wait()
    width = grad_qkv.shape[0]
    block = 0
    for ref in (grad_gate_up, grad_down, grad_qkv, grad_out):
        for n in range(0, ref.shape[1] - 127, 128):
            ref[:, n : n + 128] = gathered[block * width : (block + 1) * width, :].astype(single)
            block += 1
    rest = gathered[block * width : (block + 1) * width, :].astype(single)
    grad_qkv[:, 3 * width - QKV_REST :] = rest[:, :QKV_REST]
    grad_out[:, width - OUT_REST :] = rest[:, QKV_REST : QKV_REST + OUT_REST]
    grad_gains[...] = rest.T[QKV_REST + OUT_REST : QKV_REST + OUT_REST + 2, :]
    for c in writes + [outs]:
        c.wait()


def finish(gathered, far_out, far_grad, kept_out, kept_grad, hidden):
    shape = jax.ShapeDtypeStruct
    count, width, length = far_out.shape
    anywhere = pl.BlockSpec(memory_space=pl.ANY)
    vmem = pl.BlockSpec(memory_space=pltpu.VMEM)
    v = pltpu.VMEM
    return pl.pallas_call(
        finish_kernel,
        out_shape=(
            shape(kept_out.shape, bfloat),
            shape(kept_grad.shape, single),
            shape((2, width), single),
            shape((width, 3 * width), single),
            shape((width, width), single),
            shape((width, 2 * hidden), single),
            shape((width, hidden), single),
        ),
        in_specs=[anywhere] * 5,
        out_specs=[anywhere] * 2 + [vmem] * 5,
        scratch_shapes=[
            v(gathered.shape, bfloat),
            v(far_out.shape, bfloat),
            v(far_grad.shape, bfloat),
            v(far_grad.shape, single),
            pltpu.SemaphoreType.DMA((count + 2,)),
            pltpu.SemaphoreType.DMA((count + 1,)),
        ],
        input_output_aliases={3: 0, 4: 1},
        compiler_params=pltpu.CompilerParams(vmem_limit_bytes=VMEM_LIMIT),
    )(gathered, far_out, far_grad, kept_out, kept_grad)


def reduce(devices, own_total, other_total, sent_out, sent_grad):
    sizes = group_sizes(devices)
    rows = own_total.shape[0]
    v = pltpu.VMEM
    shape = jax.ShapeDtypeStruct
    parts, slots, left = [], [], rows
    for size in sizes:
        parts.append(v((left, 128), bfloat))
        left //= size
        slots.append(v((size - 1, left, 128), bfloat))
    links = sum(size - 1 for size in sizes)
    dma = pltpu.SemaphoreType.DMA
    anywhere = pl.BlockSpec(memory_space=pl.ANY)
    vmem = pl.BlockSpec(memory_space=pltpu.VMEM)
    return pl.pallas_call(
        functools.partial(reduce_kernel, sizes),
        out_shape=(
            shape(sent_out.shape, bfloat),
            shape(sent_grad.shape, bfloat),
            shape((rows, 128), bfloat),
        ),
        in_specs=[vmem, vmem, anywhere, anywhere],
        out_specs=[anywhere, anywhere, vmem],
        scratch_shapes=[v((rows, 128), bfloat)]
        + parts
        + slots
        + parts[1:]
        + [v((left, 128), bfloat), dma((3,)), dma((3,))]
        + [dma((links,))] * 4,
        compiler_params=pltpu.CompilerParams(
            collective_id=1, has_side_effects=True, vmem_limit_bytes=VMEM_LIMIT
        ),
    )(own_total, other_total, sent_out, sent_grad)


def on_device(
    devices,
    raw,
    series_ids,
    median,
    scale,
    cotangent,
    norm_gains,
    qkv_weight,
    out_weight,
    gate_up_weight,
    down_weight,
):
    section = lax.axis_index("section")
    turned = lambda a: jnp.swapaxes(a, -1, -2)
    count = raw.shape[0] // 2
    width, hidden = raw.shape[2], down_weight.shape[1]
    own = (norm_gains[0], qkv_weight[0], out_weight[0], gate_up_weight[0], turned(down_weight[0]))
    other = swap_weights(own)
    blocks = 14
    rows = -(-blocks * width // (16 * devices)) * 16 * devices
    kept_out, kept_grad, sent_out, sent_grad, own_total, other_total = train(
        section, rows, turned(raw), series_ids, median, scale, turned(cotangent), own, other
    )
    far_out, far_grad, gathered = reduce(devices, own_total, other_total, sent_out, sent_grad)
    layer_outputs, input_grads, gain, qkv, out, gate_up, down = finish(
        gathered, far_out, far_grad, kept_out, kept_grad, hidden
    )
    return (
        turned(layer_outputs)[None],
        turned(input_grads)[None],
        gain[None],
        qkv[None],
        out[None],
        gate_up[None],
        turned(down)[None],
    )


def solution(mesh):
    placed = (
        P("dp", None, None),
        P("dp"),
        P(),
        P(),
        P("dp", None, None),
        P("section", None, None),
        P("section", None, None),
        P("section", None, None),
        P("section", None, None),
        P("section", None, None),
    )
    return jax.shard_map(
        functools.partial(on_device, mesh.shape["dp"]),
        mesh=mesh,
        in_specs=placed,
        out_specs=(
            P("section", "dp", None, None),
            P("section", "dp", None, None),
            P("section", None, None),
            P("section", None, None),
            P("section", None, None),
            P("section", None, None),
            P("section", None, None),
        ),
        check_vma=False,
    )
```

```python
import functools
import math

import jax
import jax.numpy as jnp
import numpy as np
from jax import lax
from jax.experimental import pallas as pl
from jax.experimental.pallas import tpu as pltpu
from jax.sharding import PartitionSpec as P

HEAD = 16
HALF = HEAD // 2
TILE = 256
CHUNK = 512
ROWS = 384
TURN_AT = 6
BACK_AT = 8
VMEM_LIMIT = 64 * 2**20 - 2**16
EPSILON = 1e-06
EXPONENT = HEAD**-0.5 * math.log2(math.e)
QKV_REST = 48
OUT_REST = 16
MESH = pl.DeviceIdType.MESH
bfloat = jnp.bfloat16
single = jnp.float32


def dot(left, right):
    return jnp.dot(left, right, preferred_element_type=single)


def dot_nt(left, right):
    return lax.dot_general(left, right, (((1,), (1,)), ((), ())), preferred_element_type=single)


def rms_scale(values):
    return lax.rsqrt(jnp.mean(values * values, axis=0, keepdims=True) + EPSILON)


def rms_backward(grad_normed, values, inverse, gain):
    scaled = grad_normed * gain
    centre = jnp.mean(scaled * values, axis=0, keepdims=True)
    grad_values = inverse * scaled - values * (inverse * inverse * inverse * centre)
    product = grad_normed * values * inverse
    partial = product[:, :128]
    for start in range(128, product.shape[1], 128):
        partial = partial + product[:, start : start + 128]
    return grad_values, partial


def causal(block):
    rows = lax.broadcasted_iota(jnp.int32, block.shape, 0)
    columns = lax.broadcasted_iota(jnp.int32, block.shape, 1)
    return rows <= columns


def tile_start(j):
    return j * (j + 1) // 2 * TILE


def lanes(tiles, heads):
    pairs = []
    for first in range(0, heads, 3):
        full = [(j, k) for j in range(tiles) for k in range(j + 1)]
        sides = [[(first + side, j, k) for j, k in full] for side in range(2)]
        for j in reversed(range(tiles)):
            side = min(sides, key=len)
            side += [(first + 2, j, k) for k in range(j + 1)]
        pairs += zip(*sides)
    return pairs


def train_kernel(
    heads,
    hidden,
    here,
    start,
    series_ids,
    median,
    scale,
    raw,
    cotangent,
    own_gains,
    own_qkv,
    own_out,
    own_gate_up,
    own_down_t,
    other_gains,
    other_qkv,
    other_out,
    other_gate_up,
    other_down_t,
    tables,
    kept_out,
    kept_grad,
    sent_out,
    sent_grad,
    own_total,
    other_total,
    gains,
    qkv_t,
    out_t,
    gate_up_t,
    down_t,
    qkv_w,
    out_w,
    gate_up_w,
    down_w,
    grad_gains,
    grad_qkv,
    grad_out,
    grad_gate_up,
    grad_down,
    inputs,
    inverse1,
    normed,
    queries,
    keys,
    values,
    rows_major,
    exponents,
    attended32,
    reciprocal,
    attended,
    residual,
    inverse2,
    mid,
    gate_up,
    activated,
    grad,
    grad_low,
    grad_pre,
    grad_res_low,
    grad_att,
    grad_q,
    grad_k,
    grad_proj,
    flipped,
    grad_inputs,
):
    step = pl.program_id(0)
    section = here[0]
    series = start[0] + step
    number = series_ids[series]
    centre = median[number]
    inverse_spread = 1.0 / scale[number]
    width, length = inputs.shape[1:]
    tiles = length // TILE
    chunks = [slice(n, n + CHUNK) for n in range(0, length, CHUNK)]
    columns = [slice(n, n + TILE) for n in range(0, length, TILE)]

    @pl.when(step == 0)
    def _():
        for ref in (grad_gains, grad_qkv, grad_out, grad_gate_up, grad_down):
            ref[...] = jnp.zeros_like(ref)
        row = lax.broadcasted_iota(jnp.int32, (2, heads, HEAD, length), 2)
        values[:, :, HEAD:, :] = jnp.where(row < 2, 1.0, 0.0).astype(bfloat)
        turned = lambda w: w.astype(single).T.astype(bfloat)
        for l, (gain, qkv, out, both, down) in (
            (section, (own_gains, own_qkv, own_out, own_gate_up, own_down_t)),
            (1 - section, (other_gains, other_qkv, other_out, other_gate_up, other_down_t)),
        ):
            for part in range(2):
                row = jnp.broadcast_to(gain[part : part + 1, :], (128, width))
                gains[l, part] = row.T
            qkv_w[l] = qkv[...]
            qkv_t[l] = turned(qkv[...])
            out_w[l] = out[...]
            out_t[l] = turned(out[...])
            column = lax.broadcasted_iota(jnp.int32, both.shape, 1)
            halved = both[...].astype(single) * jnp.where(column < hidden, 0.5, 1.0)
            gate_up_w[l] = halved.astype(bfloat)
            gate_up_t[l] = halved.T.astype(bfloat)
            down_t[l] = down[...]
            down_w[l] = turned(down[...])

    def gain_of(l, part, count=CHUNK):
        return jnp.concatenate([gains[l, part]] * (count // 128), axis=1)

    inputs[0] = (raw[0].astype(single) - centre) * inverse_spread
    grad[...] = cotangent[0].astype(single)

    def rotated(block, cos, sin):
        a, b = block[:, :HALF], block[:, HALF:]
        return jnp.concatenate([a * cos - b * sin, b * cos + a * sin], axis=1)

    head_rows = lax.broadcasted_iota(jnp.int32, (HEAD, width), 0)
    head_columns = lax.broadcasted_iota(jnp.int32, (HEAD, width), 1)
    of_head = jnp.where(
        (head_columns >= head_rows * HEAD) & (head_columns < (head_rows + 1) * HEAD), 1.0, 0.0
    ).astype(bfloat)

    def forward(l, carry):
        largest_q = jnp.zeros((HEAD, CHUNK), single)
        largest_k = jnp.zeros((HEAD, CHUNK), single)
        for cs in chunks:
            u = inputs[l, :, cs]
            inv = rms_scale(u)
            inverse1[l, :, cs] = inv
            low = (u * inv * gain_of(l, 0)).astype(bfloat)
            normed[l, :, cs] = low
            projected = dot(qkv_t[l], low).reshape(3 * heads, HEAD, CHUNK)
            q, k = projected[:heads], projected[heads : 2 * heads]
            grad_q[:, :, cs] = q
            grad_k[:, :, cs] = k
            values[l, :, :HEAD, cs] = projected[2 * heads :].astype(bfloat)
            squares = lambda v: dot(of_head, (v * v).astype(bfloat).reshape(width, CHUNK))
            largest_q = jnp.maximum(largest_q, squares(q))
            largest_k = jnp.maximum(largest_k, squares(k))
        bound = jnp.max(
            jnp.max(largest_q, axis=1, keepdims=True) * jnp.max(largest_k, axis=1, keepdims=True)
        )

        def finish(h, j, product, total):
            js = slice(j * TILE, (j + 1) * TILE)
            inverse = 1.0 / total
            out = product * inverse
            reciprocal[l, h, :, js] = inverse
            attended32[l, h, :, js] = out
            attended[l, h, :, js] = out.astype(bfloat)

        def turn(three):
            hs = slice(three * 3, three * 3 + 3)
            for cs in chunks:
                q = rotated(grad_q[hs, :, cs], tables[0, :, cs], tables[1, :, cs])
                k = rotated(grad_k[hs, :, cs], tables[0, :, cs], tables[1, :, cs])
                queries[l, hs, :, cs] = q.astype(bfloat)
                keys[l, hs, :, cs] = k.astype(bfloat)
                for g in range(3):
                    rows_major[three * 3 + g, cs, :HEAD] = k[g].T.astype(bfloat)

        small = bound * EXPONENT**2 <= 1e4

        @pl.when(small)
        def _():
            pairs = lanes(tiles, heads)
            group = len(pairs) * 3 // heads
            ahead = 2
            scores, products, totals = {}, {}, {}

            def score(m):
                for side, (h, j, k) in enumerate(pairs[m]):
                    scores[m, side] = dot(
                        rows_major[h, k * TILE : (k + 1) * TILE, :HEAD],
                        queries[l, h, :, j * TILE : (j + 1) * TILE],
                    )

            turn(0)
            for m in range(ahead):
                score(m)
            for m, pair in enumerate(pairs):
                if m % group == TURN_AT and m + group < len(pairs):
                    turn(m // group + 1)
                if m + ahead < len(pairs):
                    score(m + ahead)
                ready = []
                for side, (h, j, k) in enumerate(pair):
                    e = jnp.exp2(scores.pop((m, side)) * EXPONENT)
                    if k == j:
                        e = jnp.where(causal(e), e, 0.0)
                    part = jnp.sum(e.reshape(TILE // 8, 8, TILE), axis=0)
                    totals[h, j] = totals[h, j] + part if k else part
                    e = e.astype(bfloat)
                    first = tile_start(j) + k * TILE
                    exponents[l, h, first : first + TILE, :] = e.T
                    ready.append(e)
                for side, (h, j, k) in enumerate(pair):
                    part = dot(values[l, h, :HEAD, k * TILE : (k + 1) * TILE], ready[side])
                    products[h, j] = products[h, j] + part if k else part
                    if k == j:
                        total = jnp.sum(totals.pop((h, j)), axis=0, keepdims=True)
                        finish(h, j, products.pop((h, j)), total)

        @pl.when(jnp.logical_not(small))
        def _():
            for three in range(heads // 3):
                turn(three)

            def one(h, carry):
                for j in range(tiles):
                    count = (j + 1) * TILE
                    js = slice(j * TILE, (j + 1) * TILE)
                    score = dot(rows_major[h, :count, :HEAD], queries[l, h, :, js]) * EXPONENT
                    rows = lax.broadcasted_iota(jnp.int32, score.shape, 0)
                    columns = lax.broadcasted_iota(jnp.int32, score.shape, 1) + j * TILE
                    score = jnp.where(rows <= columns, score, -1e30)
                    e = jnp.exp2(score - jnp.max(score, axis=0, keepdims=True))
                    total = jnp.sum(e, axis=0, keepdims=True)
                    e = e.astype(bfloat)
                    for k in range(j + 1):
                        first = tile_start(j) + k * TILE
                        exponents[l, h, first : first + TILE, :] = e[k * TILE : (k + 1) * TILE].T
                    finish(h, j, dot(values[l, h, :HEAD, :count], e), total)
                return carry

            lax.fori_loop(0, heads, one, 0)

        for cs in chunks:
            res = inputs[l, :, cs] + dot(out_t[l], attended[l, :, :, cs].reshape(width, CHUNK))
            residual[l, :, cs] = res
            inv = rms_scale(res)
            inverse2[l, :, cs] = inv
            mid[l, :, cs] = (res * inv * gain_of(l, 1)).astype(bfloat)
        for cs in columns:
            low = mid[l, :, cs]
            for n in range(0, hidden, ROWS):
                half = dot(gate_up_t[l, n : n + ROWS], low)
                up = dot(gate_up_t[l, hidden + n : hidden + n + ROWS], low)
                t = jnp.tanh(half)
                twice = 1.0 + t
                swish = half * twice
                gate_up[l, n : n + ROWS, cs] = up * (twice + swish * (1.0 - t))
                gate_up[l, hidden + n : hidden + n + ROWS, cs] = swish
                activated[l, n : n + ROWS, cs] = (swish * up).astype(bfloat)
        for cs in chunks:
            result = residual[l, :, cs] + dot(down_t[l], activated[l, :, cs])
            inputs[l + 1, :, cs] = result.astype(bfloat).astype(single)
        return carry

    lax.fori_loop(0, 2, forward, 0)

    def backward(turn, carry):
        l = 1 - turn
        slot = lax.rem(l + section, 2)
        for cs in columns:
            low = grad[:, cs].astype(bfloat)
            grad_low[:, cs] = low
            for n in range(0, hidden, ROWS):
                grad_act = dot(down_w[l, n : n + ROWS], low)
                for m in (n, hidden + n):
                    factor = gate_up[l, m : m + ROWS, cs]
                    grad_pre[m : m + ROWS, cs] = (grad_act * factor).astype(bfloat)
        grad_mids = [dot(gate_up_w[l], grad_pre[:, cs]) for cs in chunks]
        for n, cs in enumerate(chunks):
            half = slice(n * 2 * hidden // len(chunks), (n + 1) * 2 * hidden // len(chunks))
            grad_gate_up[slot, :, half] += dot_nt(mid[l], grad_pre[half, :])
            g = grad[:, cs]
            grad_mid = grad_mids[n]
            res, inv = residual[l, :, cs], inverse2[l, :, cs]
            grad_res, partial = rms_backward(grad_mid, res, inv, gain_of(l, 1))
            grad_gains[slot, 1] += partial
            grad_res = grad_res + g
            grad[:, cs] = grad_res
            low = grad_res.astype(bfloat)
            grad_res_low[:, cs] = low
            back = dot(out_w[l], low).astype(bfloat).astype(single).reshape(heads, HEAD, CHUNK)
            inverse = reciprocal[l, :, :, cs]
            mean = jnp.sum(back * attended32[l, :, :, cs], axis=1, keepdims=True) * -inverse
            coarse = mean.astype(bfloat).astype(single)
            row = lax.broadcasted_iota(jnp.int32, (heads, HALF, CHUNK), 1)
            extra = jnp.where(row == 0, coarse, jnp.where(row == 1, mean - coarse, 0.0))
            rest = jnp.zeros((heads, HALF, CHUNK), single)
            grad_att[:, :, cs] = jnp.concatenate([back * inverse, extra, rest], axis=1).astype(bfloat)
        grad_down[slot] += dot_nt(grad_low[...], activated[l])
        grad_out[slot] += dot_nt(attended[l].reshape(width, length), grad_res_low[...])

        def turn(three):
            for h in range(three * 3, three * 3 + 3):
                rows_major[h] = grad_att[h].T

        def turn_back(three):
            hs = slice(three * 3, three * 3 + 3)
            for cs in chunks:
                dq = rotated(grad_q[hs, :, cs], tables[2, :, cs], tables[3, :, cs])
                dk = rotated(grad_k[hs, :, cs], tables[2, :, cs], tables[3, :, cs])
                grad_proj[hs, :, cs] = dq.astype(bfloat)
                grad_proj[three * 3 + heads : three * 3 + heads + 3, :, cs] = dk.astype(bfloat)

        pairs = lanes(tiles, heads)
        group = len(pairs) * 3 // heads
        ahead = 2
        half = TILE // 2
        products, held, sums = {}, {}, {}

        def product(m, part):
            if m < len(pairs):
                for side, (h, j, k) in enumerate(pairs[m]):
                    first = j * TILE + part * half
                    products[m, side, part] = dot(
                        rows_major[h, first : first + half, :],
                        values[l, h, :, k * TILE : (k + 1) * TILE],
                    )

        def add(name, index, side, h, value):
            key = name, h, index, side
            sums[key] = sums[key] + value if key in sums else value

        turn(0)
        for m in range(ahead):
            product(m, 0)
            product(m, 1)
        for m in range(len(pairs) + 1):
            three = m // group
            if m % group == TURN_AT and m + group < len(pairs):
                turn(three + 1)
            if m % group == BACK_AT and three > 0:
                turn_back(three - 1)
            now = pairs[m] if m < len(pairs) else ()
            before = pairs[m - 1] if m > 0 else ()
            product(m + ahead, 0)
            exps = []
            for side, (h, j, k) in enumerate(now):
                first = tile_start(j) + k * TILE
                e = exponents[l, h, first : first + TILE, :]
                parts = [
                    (e[p * half : (p + 1) * half].astype(single) * products.pop((m, side, p))).astype(bfloat)
                    for p in range(2)
                ]
                grad_score = jnp.concatenate(parts, axis=0)
                flipped[m % 2, side] = grad_score.T
                held[m, side] = grad_score
                exps.append(e)
            for side, (h, j, k) in enumerate(now):
                js = slice(j * TILE, (j + 1) * TILE)
                add("v", k, side, h, dot(grad_att[h, :HEAD, js], exps[side]))
            product(m + ahead, 1)
            for side, (h, j, k) in enumerate(before):
                js = slice(j * TILE, (j + 1) * TILE)
                add("k", k, side, h, dot(queries[l, h, :, js], held.pop((m - 1, side))))
            for side, (h, j, k) in enumerate(before):
                ks = slice(k * TILE, (k + 1) * TILE)
                add("q", j, side, h, dot(keys[l, h, :, ks], flipped[(m - 1) % 2, side]))
            if m > 0 and m % group == 0:
                for h in range((three - 1) * 3, three * 3):
                    for name, ref in (("q", grad_q), ("k", grad_k), ("v", grad_proj)):
                        for t in range(tiles):
                            found = [sums.pop((name, h, t, n), None) for n in range(2)]
                            found = [f for f in found if f is not None]
                            place = h + 2 * heads if name == "v" else h
                            total = sum(found[1:], found[0]).astype(ref.dtype)
                            ref[place, :, t * TILE : (t + 1) * TILE] = total
        turn_back(heads // 3 - 1)

        lows = [grad_proj[:, :, cs].reshape(3 * width, CHUNK) for cs in chunks]
        grad_normeds = [dot(qkv_w[l], low) for low in lows]
        grad_qkv[slot] += dot_nt(normed[l], grad_proj[...].reshape(3 * width, length))
        for cs, grad_normed in zip(chunks, grad_normeds):
            u, inv = inputs[l, :, cs], inverse1[l, :, cs]
            grad_u, partial = rms_backward(grad_normed, u, inv, gain_of(l, 0))
            grad_gains[slot, 0] += partial
            grad_u = grad_u + grad[:, cs]
            grad[:, cs] = grad_u.astype(bfloat).astype(single)
            grad_inputs[l, :, cs] = grad_u
        return carry

    lax.fori_loop(0, 2, backward, 0)

    grad_inputs[0] = grad_inputs[0] * inverse_spread
    kept_out[0] = inputs[section + 1].astype(bfloat)
    sent_out[0] = inputs[2 - section].astype(bfloat)
    kept_grad[0] = grad_inputs[section]
    sent_grad[0] = grad_inputs[1 - section].astype(bfloat)

    @pl.when(step == pl.num_programs(0) - 1)
    def _():
        for slot, total in ((0, own_total), (1, other_total)):
            blocks = []
            for ref in (grad_gate_up, grad_down, grad_qkv, grad_out):
                for n in range(0, ref.shape[2] - 127, 128):
                    doubled = ref is grad_gate_up and n < hidden
                    blocks.append(ref[slot, :, n : n + 128] * (0.5 if doubled else 1.0))
            lane = lax.broadcasted_iota(jnp.int32, (width, 128), 1)
            spare = grad_qkv[slot, :, 3 * width - QKV_REST :]
            out_rest = grad_out[slot, :, width - OUT_REST :]
            columns = [jnp.sum(grad_gains[slot, n], axis=1, keepdims=True) for n in range(2)]
            rest = jnp.concatenate(
                [spare, out_rest] + columns
                + [jnp.zeros((width, 128 - QKV_REST - OUT_REST - 2), single)],
                axis=1,
            )
            blocks.append(rest)
            for n, block in enumerate(blocks):
                total[n * width : (n + 1) * width, :] = block.astype(total.dtype)
            used = len(blocks) * width
            total[used:, :] = jnp.zeros((total.shape[0] - used, 128), total.dtype)


def rotary_tables(length):
    frequency = 10000.0 ** (-np.arange(HALF, dtype=np.float64) / HALF)
    frequency = frequency.astype(np.float32)
    angles = np.arange(length, dtype=np.float32)[None, :] * frequency[:, None]
    cos, sin = np.cos(angles), np.sin(angles)
    tables = [cos, sin, cos * HEAD**-0.5, -sin * HEAD**-0.5]
    return np.stack(tables).astype(np.float32)


def train(section, rows, raw, series_ids, median, scale, cotangent, own, other):
    count = raw.shape[0] // 2
    width, length = raw.shape[1:]
    heads = width // HEAD
    hidden = own[4].shape[1]
    here = jnp.reshape(section, (1,)).astype(jnp.int32)
    start = jnp.reshape(section * count, (1,)).astype(jnp.int32)
    tables = jnp.asarray(rotary_tables(length))
    operands = (raw, cotangent) + own + other + (tables,)
    smem = pl.BlockSpec(memory_space=pltpu.SMEM)

    def whole(array):
        zeros = (0,) * len(array.shape)
        return pl.BlockSpec(
            array.shape, lambda i, *_: zeros, pipeline_mode=pl.Buffered(buffer_count=1)
        )

    placed_block = pl.BlockSpec((1, width, length), lambda i, here, start, ids: (start[0] + i, 0, 0))
    block = pl.BlockSpec((1, width, length), lambda i, *_: (i, 0, 0))
    shape = jax.ShapeDtypeStruct
    totals = (shape((rows, 128), single), shape((rows, 128), bfloat))
    pairs = length // TILE * (length // TILE + 1) // 2
    v = pltpu.VMEM
    scratch = [
        v((2, 2, width, 128), single),
        v((2, 3 * width, width), bfloat),
        v((2, width, width), bfloat),
        v((2, 2 * hidden, width), bfloat),
        v((2, width, hidden), bfloat),
        v((2, width, 3 * width), bfloat),
        v((2, width, width), bfloat),
        v((2, width, 2 * hidden), bfloat),
        v((2, hidden, width), bfloat),
        v((2, 2, width, 128), single),
        v((2, width, 3 * width), single),
        v((2, width, width), single),
        v((2, width, 2 * hidden), single),
        v((2, width, hidden), single),
        v((3, width, length), single),
        v((2, 1, length), single),
        v((2, width, length), bfloat),
        v((2, heads, HEAD, length), bfloat),
        v((2, heads, HEAD, length), bfloat),
        v((2, heads, 2 * HEAD, length), bfloat),
        v((heads, length, 2 * HEAD), bfloat),
        v((2, heads, pairs * TILE, TILE), bfloat),
        v((2, heads, HEAD, length), single),
        v((2, heads, 1, length), single),
        v((2, heads, HEAD, length), bfloat),
        v((2, width, length), single),
        v((2, 1, length), single),
        v((2, width, length), bfloat),
        v((2, 2 * hidden, length), single),
        v((2, hidden, length), bfloat),
        v((width, length), single),
        v((width, length), bfloat),
        v((2 * hidden, length), bfloat),
        v((width, length), bfloat),
        v((heads, 2 * HEAD, length), bfloat),
        v((heads, HEAD, length), single),
        v((heads, HEAD, length), single),
        v((3 * heads, HEAD, length), bfloat),
        v((2, 2, TILE, TILE), bfloat),
        v((2, width, length), single),
    ]
    return pl.pallas_call(
        functools.partial(train_kernel, heads, hidden),
        grid_spec=pltpu.PrefetchScalarGridSpec(
            num_scalar_prefetch=3,
            grid=(count,),
            in_specs=[smem, smem, placed_block, placed_block] + [whole(a) for a in operands[2:]],
            out_specs=[placed_block, placed_block, block, block] + [whole(t) for t in totals],
            scratch_shapes=scratch,
        ),
        out_shape=(
            shape(raw.shape, bfloat),
            shape(raw.shape, single),
            shape((count, width, length), bfloat),
            shape((count, width, length), bfloat),
        )
        + totals,
        compiler_params=pltpu.CompilerParams(vmem_limit_bytes=VMEM_LIMIT),
    )(here, start, series_ids, median, scale, *operands)


def partner():
    return {"section": 1 - lax.axis_index("section")}


def meet(peers):
    barrier = pltpu.get_barrier_semaphore()
    for peer in peers:
        pl.semaphore_signal(barrier, inc=1, device_id=peer, device_id_type=MESH)
    pl.semaphore_wait(barrier, len(peers))


def swap_kernel(count, *refs):
    own, other, send, recv = refs[:count], refs[count : 2 * count], refs[-2], refs[-1]
    meet([partner()])
    copies = [
        pltpu.make_async_remote_copy(
            src_ref=own[n],
            dst_ref=other[n],
            send_sem=send.at[n],
            recv_sem=recv.at[n],
            device_id=partner(),
            device_id_type=MESH,
        )
        for n in range(count)
    ]
    for copy in copies:
        copy.start()
    for copy in copies:
        copy.wait()


def swap_weights(weights):
    count = len(weights)
    anywhere = pl.BlockSpec(memory_space=pl.ANY)
    return pl.pallas_call(
        functools.partial(swap_kernel, count),
        out_shape=tuple(jax.ShapeDtypeStruct(w.shape, w.dtype) for w in weights),
        in_specs=[anywhere] * count,
        out_specs=[anywhere] * count,
        scratch_shapes=[pltpu.SemaphoreType.DMA((count,)), pltpu.SemaphoreType.DMA((count,))],
        compiler_params=pltpu.CompilerParams(
            collective_id=0, has_side_effects=True, vmem_limit_bytes=VMEM_LIMIT
        ),
    )(*weights)


def group_sizes(devices):
    sizes = []
    while devices > 1:
        size = 4 if devices % 4 == 0 else devices
        sizes.append(size)
        devices //= size
    return sizes


def reduce_kernel(
    sizes,
    own_total,
    other_total,
    sent_out,
    sent_grad,
    far_out,
    far_grad,
    gathered,
    arrived,
    kept_total,
    local,
    *scratch,
):
    count = len(sizes)
    parts = scratch[:count]
    slots = scratch[count : 2 * count]
    wholes = (gathered,) + scratch[2 * count : 3 * count - 1]
    last, swap_send, swap_recv, sum_send, sum_recv, gather_send, gather_recv = scratch[3 * count - 1 :]
    me = lax.axis_index("dp")
    places, groups = [], []
    stride = 1
    for size in sizes:
        place = lax.rem(lax.div(me, stride), size)
        peers = []
        for turn in range(1, size):
            other = lax.rem(place + turn, size)
            peers.append((other, {"dp": me + (other - place) * stride}))
        places.append(place)
        groups.append(peers)
        stride *= size
    loaded = pltpu.make_async_copy(own_total, kept_total, local)
    loaded.start()
    meet([partner()] + [device for peers in groups for _, device in peers])

    def copy(source, target, send, recv, device):
        c = pltpu.make_async_remote_copy(
            src_ref=source,
            dst_ref=target,
            send_sem=send,
            recv_sem=recv,
            device_id=device,
            device_id_type=MESH,
        )
        c.start()
        return c

    near = copy(other_total, arrived, swap_send.at[0], swap_recv.at[0], partner())
    near.wait()
    far = [
        copy(sent_out, far_out, swap_send.at[1], swap_recv.at[1], partner()),
        copy(sent_grad, far_grad, swap_send.at[2], swap_recv.at[2], partner()),
    ]
    loaded.wait()
    parts[0][...] = (kept_total[...] + arrived[...].astype(single)).astype(bfloat)
    first = 0
    starts = []
    for n, size in enumerate(sizes):
        chunk = parts[n].shape[0] // size
        copies = []
        for turn, (other, device) in enumerate(groups[n]):
            copies.append(
                copy(
                    parts[n].at[pl.ds(pl.multiple_of(other * chunk, 16), chunk)],
                    slots[n].at[turn],
                    sum_send.at[first + turn],
                    sum_recv.at[first + turn],
                    device,
                )
            )
        total = parts[n][pl.ds(pl.multiple_of(places[n] * chunk, 16), chunk), :].astype(single)
        for turn, c in enumerate(copies):
            c.wait()
            total = total + slots[n][turn].astype(single)
        target = parts[n + 1] if n + 1 < count else last
        target[...] = total.astype(bfloat)
        starts.append(first)
        first += size - 1
    source = last
    for n in reversed(range(count)):
        chunk = parts[n].shape[0] // sizes[n]
        mine = pl.ds(pl.multiple_of(places[n] * chunk, 16), chunk)
        copies = []
        for turn, (_, device) in enumerate(groups[n]):
            k = starts[n] + turn
            copies.append(
                copy(source, wholes[n].at[mine], gather_send.at[k], gather_recv.at[k], device)
            )
        wholes[n][mine, :] = source[...]
        for c in copies:
            c.wait()
        source = wholes[n]
    for c in far:
        c.wait()


def finish_kernel(
    gathered_far,
    far_out,
    far_grad,
    kept_out,
    kept_grad,
    layer_outputs,
    input_grads,
    grad_gains,
    grad_qkv,
    grad_out,
    grad_gate_up,
    grad_down,
    gathered,
    passed,
    narrow,
    wide,
    arrive,
    leave,
):
    count = far_out.shape[0]
    place = (1 - lax.axis_index("section")) * count
    outs = pltpu.make_async_copy(passed, layer_outputs.at[pl.ds(place, count)], leave.at[count])
    into = pltpu.make_async_copy(far_out, passed, arrive.at[count + 1])
    sums = pltpu.make_async_copy(gathered_far, gathered, arrive.at[count])
    reads = [pltpu.make_async_copy(far_grad.at[i], narrow.at[i], arrive.at[i]) for i in range(count)]
    writes = [
        pltpu.make_async_copy(wide.at[i], input_grads.at[place + i], leave.at[i])
        for i in range(count)
    ]
    for c in reads + [sums, into]:
        c.start()
    for i in range(count):
        reads[i].wait()
        wide[i] = narrow[i].astype(single)
        writes[i].start()
    into.wait()
    outs.start()
    sums.wait()
    width = grad_qkv.shape[0]
    block = 0
    for ref in (grad_gate_up, grad_down, grad_qkv, grad_out):
        for n in range(0, ref.shape[1] - 127, 128):
            ref[:, n : n + 128] = gathered[block * width : (block + 1) * width, :].astype(single)
            block += 1
    rest = gathered[block * width : (block + 1) * width, :].astype(single)
    grad_qkv[:, 3 * width - QKV_REST :] = rest[:, :QKV_REST]
    grad_out[:, width - OUT_REST :] = rest[:, QKV_REST : QKV_REST + OUT_REST]
    grad_gains[...] = rest.T[QKV_REST + OUT_REST : QKV_REST + OUT_REST + 2, :]
    for c in writes + [outs]:
        c.wait()


def finish(gathered, far_out, far_grad, kept_out, kept_grad, hidden):
    shape = jax.ShapeDtypeStruct
    count, width, length = far_out.shape
    anywhere = pl.BlockSpec(memory_space=pl.ANY)
    vmem = pl.BlockSpec(memory_space=pltpu.VMEM)
    v = pltpu.VMEM
    return pl.pallas_call(
        finish_kernel,
        out_shape=(
            shape(kept_out.shape, bfloat),
            shape(kept_grad.shape, single),
            shape((2, width), single),
            shape((width, 3 * width), single),
            shape((width, width), single),
            shape((width, 2 * hidden), single),
            shape((width, hidden), single),
        ),
        in_specs=[anywhere] * 5,
        out_specs=[anywhere] * 2 + [vmem] * 5,
        scratch_shapes=[
            v(gathered.shape, bfloat),
            v(far_out.shape, bfloat),
            v(far_grad.shape, bfloat),
            v(far_grad.shape, single),
            pltpu.SemaphoreType.DMA((count + 2,)),
            pltpu.SemaphoreType.DMA((count + 1,)),
        ],
        input_output_aliases={3: 0, 4: 1},
        compiler_params=pltpu.CompilerParams(vmem_limit_bytes=VMEM_LIMIT),
    )(gathered, far_out, far_grad, kept_out, kept_grad)


def reduce(devices, own_total, other_total, sent_out, sent_grad):
    sizes = group_sizes(devices)
    rows = own_total.shape[0]
    v = pltpu.VMEM
    shape = jax.ShapeDtypeStruct
    parts, slots, left = [], [], rows
    for size in sizes:
        parts.append(v((left, 128), bfloat))
        left //= size
        slots.append(v((size - 1, left, 128), bfloat))
    links = sum(size - 1 for size in sizes)
    dma = pltpu.SemaphoreType.DMA
    anywhere = pl.BlockSpec(memory_space=pl.ANY)
    vmem = pl.BlockSpec(memory_space=pltpu.VMEM)
    return pl.pallas_call(
        functools.partial(reduce_kernel, sizes),
        out_shape=(
            shape(sent_out.shape, bfloat),
            shape(sent_grad.shape, bfloat),
            shape((rows, 128), bfloat),
        ),
        in_specs=[anywhere] * 4,
        out_specs=[anywhere, anywhere, vmem],
        scratch_shapes=[v((rows, 128), bfloat), v((rows, 128), single), dma]
        + parts
        + slots
        + parts[1:]
        + [v((left, 128), bfloat), dma((3,)), dma((3,))]
        + [dma((links,))] * 4,
        compiler_params=pltpu.CompilerParams(
            collective_id=1, has_side_effects=True, vmem_limit_bytes=VMEM_LIMIT
        ),
    )(own_total, other_total, sent_out, sent_grad)


def on_device(
    devices,
    raw,
    series_ids,
    median,
    scale,
    cotangent,
    norm_gains,
    qkv_weight,
    out_weight,
    gate_up_weight,
    down_weight,
):
    section = lax.axis_index("section")
    turned = lambda a: jnp.swapaxes(a, -1, -2)
    count = raw.shape[0] // 2
    width, hidden = raw.shape[2], down_weight.shape[1]
    own = (norm_gains[0], qkv_weight[0], out_weight[0], gate_up_weight[0], turned(down_weight[0]))
    other = swap_weights(own)
    blocks = 14
    rows = -(-blocks * width // (16 * devices)) * 16 * devices
    kept_out, kept_grad, sent_out, sent_grad, own_total, other_total = train(
        section, rows, turned(raw), series_ids, median, scale, turned(cotangent), own, other
    )
    far_out, far_grad, gathered = reduce(devices, own_total, other_total, sent_out, sent_grad)
    layer_outputs, input_grads, gain, qkv, out, gate_up, down = finish(
        gathered, far_out, far_grad, kept_out, kept_grad, hidden
    )
    return (
        turned(layer_outputs)[None],
        turned(input_grads)[None],
        gain[None],
        qkv[None],
        out[None],
        gate_up[None],
        turned(down)[None],
    )


def solution(mesh):
    placed = (
        P("dp", None, None),
        P("dp"),
        P(),
        P(),
        P("dp", None, None),
        P("section", None, None),
        P("section", None, None),
        P("section", None, None),
        P("section", None, None),
        P("section", None, None),
    )
    return jax.shard_map(
        functools.partial(on_device, mesh.shape["dp"]),
        mesh=mesh,
        in_specs=placed,
        out_specs=(
            P("section", "dp", None, None),
            P("section", "dp", None, None),
            P("section", None, None),
            P("section", None, None),
            P("section", None, None),
            P("section", None, None),
            P("section", None, None),
        ),
        check_vma=False,
    )
```

```python
import functools
import math

import jax
import jax.numpy as jnp
import numpy as np
from jax import lax
from jax.experimental import pallas as pl
from jax.experimental.pallas import tpu as pltpu
from jax.sharding import PartitionSpec as P

HEAD = 16
HALF = HEAD // 2
TILE = 256
CHUNK = 512
ROWS = 384
TURN_AT = 9
BACK_AT = 8
VMEM_LIMIT = 64 * 2**20 - 2**16
EPSILON = 1e-06
EXPONENT = HEAD**-0.5 * math.log2(math.e)
QKV_REST = 48
OUT_REST = 16
MESH = pl.DeviceIdType.MESH
bfloat = jnp.bfloat16
single = jnp.float32


def dot(left, right):
    return jnp.dot(left, right, preferred_element_type=single)


def dot_nt(left, right):
    return lax.dot_general(left, right, (((1,), (1,)), ((), ())), preferred_element_type=single)


def rms_scale(values):
    return lax.rsqrt(jnp.mean(values * values, axis=0, keepdims=True) + EPSILON)


def rms_backward(grad_normed, values, inverse, gain):
    scaled = grad_normed * gain
    centre = jnp.mean(scaled * values, axis=0, keepdims=True)
    grad_values = inverse * scaled - values * (inverse * inverse * inverse * centre)
    product = grad_normed * values * inverse
    partial = product[:, :128]
    for start in range(128, product.shape[1], 128):
        partial = partial + product[:, start : start + 128]
    return grad_values, partial


def causal(block):
    rows = lax.broadcasted_iota(jnp.int32, block.shape, 0)
    columns = lax.broadcasted_iota(jnp.int32, block.shape, 1)
    return rows <= columns


def tile_start(j):
    return j * (j + 1) // 2 * TILE


def lanes(tiles, heads):
    pairs = []
    for first in range(0, heads, 3):
        full = [(j, k) for j in range(tiles) for k in range(j + 1)]
        sides = [[(first + side, j, k) for j, k in full] for side in range(2)]
        for j in reversed(range(tiles)):
            side = min(sides, key=len)
            side += [(first + 2, j, k) for k in range(j + 1)]
        pairs += zip(*sides)
    return pairs


def train_kernel(
    heads,
    hidden,
    here,
    start,
    series_ids,
    median,
    scale,
    raw,
    cotangent,
    own_gains,
    own_qkv,
    own_out,
    own_gate_up,
    own_down_t,
    other_gains,
    other_qkv,
    other_out,
    other_gate_up,
    other_down_t,
    tables,
    kept_out,
    kept_grad,
    sent_out,
    sent_grad,
    own_total,
    other_total,
    gains,
    qkv_t,
    out_t,
    gate_up_t,
    down_t,
    qkv_w,
    out_w,
    gate_up_w,
    down_w,
    grad_gains,
    grad_qkv,
    grad_out,
    grad_gate_up,
    grad_down,
    inputs,
    inverse1,
    normed,
    queries,
    keys,
    values,
    rows_major,
    exponents,
    attended32,
    reciprocal,
    attended,
    residual,
    inverse2,
    mid,
    gate_up,
    activated,
    grad,
    grad_low,
    grad_pre,
    grad_res_low,
    grad_att,
    grad_q,
    grad_k,
    grad_proj,
    flipped,
    grad_inputs,
):
    step = pl.program_id(0)
    section = here[0]
    series = start[0] + step
    number = series_ids[series]
    centre = median[number]
    inverse_spread = 1.0 / scale[number]
    width, length = inputs.shape[1:]
    tiles = length // TILE
    chunks = [slice(n, n + CHUNK) for n in range(0, length, CHUNK)]
    columns = [slice(n, n + TILE) for n in range(0, length, TILE)]

    @pl.when(step == 0)
    def _():
        for ref in (grad_gains, grad_qkv, grad_out, grad_gate_up, grad_down):
            ref[...] = jnp.zeros_like(ref)
        row = lax.broadcasted_iota(jnp.int32, (2, heads, HEAD, length), 2)
        values[:, :, HEAD:, :] = jnp.where(row < 2, 1.0, 0.0).astype(bfloat)
        turned = lambda w: w.astype(single).T.astype(bfloat)
        for l, (gain, qkv, out, both, down) in (
            (section, (own_gains, own_qkv, own_out, own_gate_up, own_down_t)),
            (1 - section, (other_gains, other_qkv, other_out, other_gate_up, other_down_t)),
        ):
            for part in range(2):
                row = jnp.broadcast_to(gain[part : part + 1, :], (128, width))
                gains[l, part] = row.T
            qkv_w[l] = qkv[...]
            qkv_t[l] = turned(qkv[...])
            out_w[l] = out[...]
            out_t[l] = turned(out[...])
            column = lax.broadcasted_iota(jnp.int32, both.shape, 1)
            halved = both[...].astype(single) * jnp.where(column < hidden, 0.5, 1.0)
            gate_up_w[l] = halved.astype(bfloat)
            gate_up_t[l] = halved.T.astype(bfloat)
            down_t[l] = down[...]
            down_w[l] = turned(down[...])

    def gain_of(l, part, count=CHUNK):
        return jnp.concatenate([gains[l, part]] * (count // 128), axis=1)

    inputs[0] = (raw[0].astype(single) - centre) * inverse_spread
    grad[...] = cotangent[0].astype(single)

    def rotated(block, cos, sin):
        a, b = block[:, :HALF], block[:, HALF:]
        return jnp.concatenate([a * cos - b * sin, b * cos + a * sin], axis=1)

    head_rows = lax.broadcasted_iota(jnp.int32, (HEAD, width), 0)
    head_columns = lax.broadcasted_iota(jnp.int32, (HEAD, width), 1)
    of_head = jnp.where(
        (head_columns >= head_rows * HEAD) & (head_columns < (head_rows + 1) * HEAD), 1.0, 0.0
    ).astype(bfloat)

    def forward(l, carry):
        largest_q = jnp.zeros((HEAD, CHUNK), single)
        largest_k = jnp.zeros((HEAD, CHUNK), single)
        for cs in chunks:
            u = inputs[l, :, cs]
            inv = rms_scale(u)
            inverse1[l, :, cs] = inv
            low = (u * inv * gain_of(l, 0)).astype(bfloat)
            normed[l, :, cs] = low
            projected = dot(qkv_t[l], low).reshape(3 * heads, HEAD, CHUNK)
            q, k = projected[:heads], projected[heads : 2 * heads]
            grad_q[:, :, cs] = q
            grad_k[:, :, cs] = k
            values[l, :, :HEAD, cs] = projected[2 * heads :].astype(bfloat)
            squares = lambda v: dot(of_head, (v * v).astype(bfloat).reshape(width, CHUNK))
            largest_q = jnp.maximum(largest_q, squares(q))
            largest_k = jnp.maximum(largest_k, squares(k))
        bound = jnp.max(
            jnp.max(largest_q, axis=1, keepdims=True) * jnp.max(largest_k, axis=1, keepdims=True)
        )

        def finish(h, j, product, total):
            js = slice(j * TILE, (j + 1) * TILE)
            inverse = 1.0 / total
            out = product * inverse
            reciprocal[l, h, :, js] = inverse
            attended32[l, h, :, js] = out
            attended[l, h, :, js] = out.astype(bfloat)

        def turn(three):
            hs = slice(three * 3, three * 3 + 3)
            for cs in chunks:
                q = rotated(grad_q[hs, :, cs], tables[0, :, cs], tables[1, :, cs])
                k = rotated(grad_k[hs, :, cs], tables[0, :, cs], tables[1, :, cs])
                queries[l, hs, :, cs] = q.astype(bfloat)
                keys[l, hs, :, cs] = k.astype(bfloat)
                for g in range(3):
                    rows_major[three * 3 + g, cs, :HEAD] = k[g].T.astype(bfloat)

        small = bound * EXPONENT**2 <= 1e4

        @pl.when(small)
        def _():
            pairs = lanes(tiles, heads)
            group = len(pairs) * 3 // heads
            ahead = 2
            scores, products, totals = {}, {}, {}

            def score(m):
                for side, (h, j, k) in enumerate(pairs[m]):
                    scores[m, side] = dot(
                        rows_major[h, k * TILE : (k + 1) * TILE, :HEAD],
                        queries[l, h, :, j * TILE : (j + 1) * TILE],
                    )

            turn(0)
            for m in range(ahead):
                score(m)
            for m, pair in enumerate(pairs):
                if m % group == TURN_AT and m + group < len(pairs):
                    turn(m // group + 1)
                if m + ahead < len(pairs):
                    score(m + ahead)
                ready = []
                for side, (h, j, k) in enumerate(pair):
                    e = jnp.exp2(scores.pop((m, side)) * EXPONENT)
                    if k == j:
                        e = jnp.where(causal(e), e, 0.0)
                    part = jnp.sum(e.reshape(TILE // 8, 8, TILE), axis=0)
                    totals[h, j] = totals[h, j] + part if k else part
                    e = e.astype(bfloat)
                    first = tile_start(j) + k * TILE
                    exponents[l, h, first : first + TILE, :] = e.T
                    ready.append(e)
                for side, (h, j, k) in enumerate(pair):
                    part = dot(values[l, h, :HEAD, k * TILE : (k + 1) * TILE], ready[side])
                    products[h, j] = products[h, j] + part if k else part
                    if k == j:
                        total = jnp.sum(totals.pop((h, j)), axis=0, keepdims=True)
                        finish(h, j, products.pop((h, j)), total)

        @pl.when(jnp.logical_not(small))
        def _():
            for three in range(heads // 3):
                turn(three)

            def one(h, carry):
                for j in range(tiles):
                    count = (j + 1) * TILE
                    js = slice(j * TILE, (j + 1) * TILE)
                    score = dot(rows_major[h, :count, :HEAD], queries[l, h, :, js]) * EXPONENT
                    rows = lax.broadcasted_iota(jnp.int32, score.shape, 0)
                    columns = lax.broadcasted_iota(jnp.int32, score.shape, 1) + j * TILE
                    score = jnp.where(rows <= columns, score, -1e30)
                    e = jnp.exp2(score - jnp.max(score, axis=0, keepdims=True))
                    total = jnp.sum(e, axis=0, keepdims=True)
                    e = e.astype(bfloat)
                    for k in range(j + 1):
                        first = tile_start(j) + k * TILE
                        exponents[l, h, first : first + TILE, :] = e[k * TILE : (k + 1) * TILE].T
                    finish(h, j, dot(values[l, h, :HEAD, :count], e), total)
                return carry

            lax.fori_loop(0, heads, one, 0)

        for cs in chunks:
            res = inputs[l, :, cs] + dot(out_t[l], attended[l, :, :, cs].reshape(width, CHUNK))
            residual[l, :, cs] = res
            inv = rms_scale(res)
            inverse2[l, :, cs] = inv
            mid[l, :, cs] = (res * inv * gain_of(l, 1)).astype(bfloat)
        for cs in columns:
            low = mid[l, :, cs]
            for n in range(0, hidden, ROWS):
                half = dot(gate_up_t[l, n : n + ROWS], low)
                up = dot(gate_up_t[l, hidden + n : hidden + n + ROWS], low)
                t = jnp.tanh(half)
                twice = 1.0 + t
                swish = half * twice
                gate_up[l, n : n + ROWS, cs] = up * (twice + swish * (1.0 - t))
                gate_up[l, hidden + n : hidden + n + ROWS, cs] = swish
                activated[l, n : n + ROWS, cs] = (swish * up).astype(bfloat)
        for cs in chunks:
            result = residual[l, :, cs] + dot(down_t[l], activated[l, :, cs])
            inputs[l + 1, :, cs] = result.astype(bfloat).astype(single)
        return carry

    lax.fori_loop(0, 2, forward, 0)

    def backward(turn, carry):
        l = 1 - turn
        slot = lax.rem(l + section, 2)
        for cs in columns:
            low = grad[:, cs].astype(bfloat)
            grad_low[:, cs] = low
            for n in range(0, hidden, ROWS):
                grad_act = dot(down_w[l, n : n + ROWS], low)
                for m in (n, hidden + n):
                    factor = gate_up[l, m : m + ROWS, cs]
                    grad_pre[m : m + ROWS, cs] = (grad_act * factor).astype(bfloat)
        grad_mids = [dot(gate_up_w[l], grad_pre[:, cs]) for cs in chunks]
        for n, cs in enumerate(chunks):
            half = slice(n * 2 * hidden // len(chunks), (n + 1) * 2 * hidden // len(chunks))
            grad_gate_up[slot, :, half] += dot_nt(mid[l], grad_pre[half, :])
            g = grad[:, cs]
            grad_mid = grad_mids[n]
            res, inv = residual[l, :, cs], inverse2[l, :, cs]
            grad_res, partial = rms_backward(grad_mid, res, inv, gain_of(l, 1))
            grad_gains[slot, 1] += partial
            grad_res = grad_res + g
            grad[:, cs] = grad_res
            low = grad_res.astype(bfloat)
            grad_res_low[:, cs] = low
            back = dot(out_w[l], low).astype(bfloat).astype(single).reshape(heads, HEAD, CHUNK)
            inverse = reciprocal[l, :, :, cs]
            mean = jnp.sum(back * attended32[l, :, :, cs], axis=1, keepdims=True) * -inverse
            coarse = mean.astype(bfloat).astype(single)
            row = lax.broadcasted_iota(jnp.int32, (heads, HALF, CHUNK), 1)
            extra = jnp.where(row == 0, coarse, jnp.where(row == 1, mean - coarse, 0.0))
            rest = jnp.zeros((heads, HALF, CHUNK), single)
            grad_att[:, :, cs] = jnp.concatenate([back * inverse, extra, rest], axis=1).astype(bfloat)
        grad_down[slot] += dot_nt(activated[l], grad_low[...])
        grad_out[slot] += dot_nt(attended[l].reshape(width, length), grad_res_low[...])

        def turn(three):
            for h in range(three * 3, three * 3 + 3):
                rows_major[h] = grad_att[h].T

        def turn_back(three):
            hs = slice(three * 3, three * 3 + 3)
            for cs in chunks:
                dq = rotated(grad_q[hs, :, cs], tables[2, :, cs], tables[3, :, cs])
                dk = rotated(grad_k[hs, :, cs], tables[2, :, cs], tables[3, :, cs])
                grad_proj[hs, :, cs] = dq.astype(bfloat)
                grad_proj[three * 3 + heads : three * 3 + heads + 3, :, cs] = dk.astype(bfloat)

        pairs = lanes(tiles, heads)
        group = len(pairs) * 3 // heads
        ahead = 2
        half = TILE // 2
        products, held, sums = {}, {}, {}

        def product(m, part):
            if m < len(pairs):
                for side, (h, j, k) in enumerate(pairs[m]):
                    first = j * TILE + part * half
                    products[m, side, part] = dot(
                        rows_major[h, first : first + half, :],
                        values[l, h, :, k * TILE : (k + 1) * TILE],
                    )

        def add(name, index, side, h, value):
            key = name, h, index, side
            sums[key] = sums[key] + value if key in sums else value

        turn(0)
        for m in range(ahead):
            product(m, 0)
            product(m, 1)
        for m in range(len(pairs) + 1):
            three = m // group
            if m % group == TURN_AT and m + group < len(pairs):
                turn(three + 1)
            if m % group == BACK_AT and three > 0:
                turn_back(three - 1)
            now = pairs[m] if m < len(pairs) else ()
            before = pairs[m - 1] if m > 0 else ()
            product(m + ahead, 0)
            exps = []
            for side, (h, j, k) in enumerate(now):
                first = tile_start(j) + k * TILE
                e = exponents[l, h, first : first + TILE, :]
                parts = [
                    (e[p * half : (p + 1) * half].astype(single) * products.pop((m, side, p))).astype(bfloat)
                    for p in range(2)
                ]
                grad_score = jnp.concatenate(parts, axis=0)
                flipped[m % 2, side] = grad_score.T
                held[m, side] = grad_score
                exps.append(e)
            for side, (h, j, k) in enumerate(now):
                js = slice(j * TILE, (j + 1) * TILE)
                add("v", k, side, h, dot(grad_att[h, :HEAD, js], exps[side]))
            product(m + ahead, 1)
            for side, (h, j, k) in enumerate(before):
                ks = slice(k * TILE, (k + 1) * TILE)
                add("q", j, side, h, dot(keys[l, h, :, ks], flipped[(m - 1) % 2, side]))
            for side, (h, j, k) in enumerate(before):
                js = slice(j * TILE, (j + 1) * TILE)
                add("k", k, side, h, dot(queries[l, h, :, js], held.pop((m - 1, side))))
            if m > 0 and m % group == 0:
                for h in range((three - 1) * 3, three * 3):
                    for name, ref in (("q", grad_q), ("k", grad_k), ("v", grad_proj)):
                        for t in range(tiles):
                            found = [sums.pop((name, h, t, n), None) for n in range(2)]
                            found = [f for f in found if f is not None]
                            place = h + 2 * heads if name == "v" else h
                            total = sum(found[1:], found[0]).astype(ref.dtype)
                            ref[place, :, t * TILE : (t + 1) * TILE] = total
        turn_back(heads // 3 - 1)

        lows = [grad_proj[:, :, cs].reshape(3 * width, CHUNK) for cs in chunks]
        grad_normeds = [dot(qkv_w[l], low) for low in lows]
        grad_qkv[slot] += dot_nt(normed[l], grad_proj[...].reshape(3 * width, length))
        for cs, grad_normed in zip(chunks, grad_normeds):
            u, inv = inputs[l, :, cs], inverse1[l, :, cs]
            grad_u, partial = rms_backward(grad_normed, u, inv, gain_of(l, 0))
            grad_gains[slot, 0] += partial
            grad_u = grad_u + grad[:, cs]
            grad[:, cs] = grad_u.astype(bfloat).astype(single)
            grad_inputs[l, :, cs] = grad_u
        return carry

    lax.fori_loop(0, 2, backward, 0)

    grad_inputs[0] = grad_inputs[0] * inverse_spread
    kept_out[0] = inputs[section + 1].astype(bfloat)
    sent_out[0] = inputs[2 - section].astype(bfloat)
    kept_grad[0] = grad_inputs[section]
    sent_grad[0] = grad_inputs[1 - section].astype(bfloat)

    @pl.when(step == pl.num_programs(0) - 1)
    def _():
        for slot, total in ((0, own_total), (1, other_total)):
            blocks = []
            for ref in (grad_gate_up, grad_down, grad_qkv, grad_out):
                sums = ref[slot].T if ref is grad_down else ref[slot]
                for n in range(0, sums.shape[1] - 127, 128):
                    doubled = ref is grad_gate_up and n < hidden
                    blocks.append(sums[:, n : n + 128] * (0.5 if doubled else 1.0))
            lane = lax.broadcasted_iota(jnp.int32, (width, 128), 1)
            spare = grad_qkv[slot, :, 3 * width - QKV_REST :]
            out_rest = grad_out[slot, :, width - OUT_REST :]
            columns = [jnp.sum(grad_gains[slot, n], axis=1, keepdims=True) for n in range(2)]
            rest = jnp.concatenate(
                [spare, out_rest] + columns
                + [jnp.zeros((width, 128 - QKV_REST - OUT_REST - 2), single)],
                axis=1,
            )
            blocks.append(rest)
            for n, block in enumerate(blocks):
                total[n * width : (n + 1) * width, :] = block.astype(total.dtype)
            used = len(blocks) * width
            total[used:, :] = jnp.zeros((total.shape[0] - used, 128), total.dtype)


def rotary_tables(length):
    frequency = 10000.0 ** (-np.arange(HALF, dtype=np.float64) / HALF)
    frequency = frequency.astype(np.float32)
    angles = np.arange(length, dtype=np.float32)[None, :] * frequency[:, None]
    cos, sin = np.cos(angles), np.sin(angles)
    tables = [cos, sin, cos * HEAD**-0.5, -sin * HEAD**-0.5]
    return np.stack(tables).astype(np.float32)


def train(section, rows, raw, series_ids, median, scale, cotangent, own, other):
    count = raw.shape[0] // 2
    width, length = raw.shape[1:]
    heads = width // HEAD
    hidden = own[4].shape[1]
    here = jnp.reshape(section, (1,)).astype(jnp.int32)
    start = jnp.reshape(section * count, (1,)).astype(jnp.int32)
    tables = jnp.asarray(rotary_tables(length))
    operands = (raw, cotangent) + own + other + (tables,)
    smem = pl.BlockSpec(memory_space=pltpu.SMEM)

    def whole(array):
        zeros = (0,) * len(array.shape)
        return pl.BlockSpec(
            array.shape, lambda i, *_: zeros, pipeline_mode=pl.Buffered(buffer_count=1)
        )

    placed_block = pl.BlockSpec((1, width, length), lambda i, here, start, ids: (start[0] + i, 0, 0))
    block = pl.BlockSpec((1, width, length), lambda i, *_: (i, 0, 0))
    shape = jax.ShapeDtypeStruct
    totals = (shape((rows, 128), single), shape((rows, 128), bfloat))
    pairs = length // TILE * (length // TILE + 1) // 2
    v = pltpu.VMEM
    scratch = [
        v((2, 2, width, 128), single),
        v((2, 3 * width, width), bfloat),
        v((2, width, width), bfloat),
        v((2, 2 * hidden, width), bfloat),
        v((2, width, hidden), bfloat),
        v((2, width, 3 * width), bfloat),
        v((2, width, width), bfloat),
        v((2, width, 2 * hidden), bfloat),
        v((2, hidden, width), bfloat),
        v((2, 2, width, 128), single),
        v((2, width, 3 * width), single),
        v((2, width, width), single),
        v((2, width, 2 * hidden), single),
        v((2, hidden, width), single),
        v((3, width, length), single),
        v((2, 1, length), single),
        v((2, width, length), bfloat),
        v((2, heads, HEAD, length), bfloat),
        v((2, heads, HEAD, length), bfloat),
        v((2, heads, 2 * HEAD, length), bfloat),
        v((heads, length, 2 * HEAD), bfloat),
        v((2, heads, pairs * TILE, TILE), bfloat),
        v((2, heads, HEAD, length), single),
        v((2, heads, 1, length), single),
        v((2, heads, HEAD, length), bfloat),
        v((2, width, length), single),
        v((2, 1, length), single),
        v((2, width, length), bfloat),
        v((2, 2 * hidden, length), single),
        v((2, hidden, length), bfloat),
        v((width, length), single),
        v((width, length), bfloat),
        v((2 * hidden, length), bfloat),
        v((width, length), bfloat),
        v((heads, 2 * HEAD, length), bfloat),
        v((heads, HEAD, length), single),
        v((heads, HEAD, length), single),
        v((3 * heads, HEAD, length), bfloat),
        v((2, 2, TILE, TILE), bfloat),
        v((2, width, length), single),
    ]
    return pl.pallas_call(
        functools.partial(train_kernel, heads, hidden),
        grid_spec=pltpu.PrefetchScalarGridSpec(
            num_scalar_prefetch=3,
            grid=(count,),
            in_specs=[smem, smem, placed_block, placed_block] + [whole(a) for a in operands[2:]],
            out_specs=[placed_block, placed_block, block, block] + [whole(t) for t in totals],
            scratch_shapes=scratch,
        ),
        out_shape=(
            shape(raw.shape, bfloat),
            shape(raw.shape, single),
            shape((count, width, length), bfloat),
            shape((count, width, length), bfloat),
        )
        + totals,
        compiler_params=pltpu.CompilerParams(vmem_limit_bytes=VMEM_LIMIT),
    )(here, start, series_ids, median, scale, *operands)


def partner():
    return {"section": 1 - lax.axis_index("section")}


def meet(peers):
    barrier = pltpu.get_barrier_semaphore()
    for peer in peers:
        pl.semaphore_signal(barrier, inc=1, device_id=peer, device_id_type=MESH)
    pl.semaphore_wait(barrier, len(peers))


def swap_kernel(count, *refs):
    own, other, send, recv = refs[:count], refs[count : 2 * count], refs[-2], refs[-1]
    meet([partner()])
    copies = [
        pltpu.make_async_remote_copy(
            src_ref=own[n],
            dst_ref=other[n],
            send_sem=send.at[n],
            recv_sem=recv.at[n],
            device_id=partner(),
            device_id_type=MESH,
        )
        for n in range(count)
    ]
    for copy in copies:
        copy.start()
    for copy in copies:
        copy.wait()


def swap_weights(weights):
    count = len(weights)
    anywhere = pl.BlockSpec(memory_space=pl.ANY)
    return pl.pallas_call(
        functools.partial(swap_kernel, count),
        out_shape=tuple(jax.ShapeDtypeStruct(w.shape, w.dtype) for w in weights),
        in_specs=[anywhere] * count,
        out_specs=[anywhere] * count,
        scratch_shapes=[pltpu.SemaphoreType.DMA((count,)), pltpu.SemaphoreType.DMA((count,))],
        compiler_params=pltpu.CompilerParams(
            collective_id=0, has_side_effects=True, vmem_limit_bytes=VMEM_LIMIT
        ),
    )(*weights)


def group_sizes(devices):
    sizes = []
    while devices > 1:
        size = 4 if devices % 4 == 0 else devices
        sizes.append(size)
        devices //= size
    return sizes


def reduce_kernel(
    sizes,
    own_total,
    other_total,
    sent_out,
    sent_grad,
    far_out,
    far_grad,
    gathered,
    arrived,
    kept_total,
    local,
    *scratch,
):
    count = len(sizes)
    parts = scratch[:count]
    slots = scratch[count : 2 * count]
    wholes = (gathered,) + scratch[2 * count : 3 * count - 1]
    last, swap_send, swap_recv, sum_send, sum_recv, gather_send, gather_recv = scratch[3 * count - 1 :]
    me = lax.axis_index("dp")
    places, groups = [], []
    stride = 1
    for size in sizes:
        place = lax.rem(lax.div(me, stride), size)
        peers = []
        for turn in range(1, size):
            other = lax.rem(place + turn, size)
            peers.append((other, {"dp": me + (other - place) * stride}))
        places.append(place)
        groups.append(peers)
        stride *= size
    loaded = pltpu.make_async_copy(own_total, kept_total, local)
    loaded.start()
    meet([partner()] + [device for peers in groups for _, device in peers])

    def copy(source, target, send, recv, device):
        c = pltpu.make_async_remote_copy(
            src_ref=source,
            dst_ref=target,
            send_sem=send,
            recv_sem=recv,
            device_id=device,
            device_id_type=MESH,
        )
        c.start()
        return c

    near = copy(other_total, arrived, swap_send.at[0], swap_recv.at[0], partner())
    near.wait_recv()
    sent = [near]
    far = [
        copy(sent_out, far_out, swap_send.at[1], swap_recv.at[1], partner()),
        copy(sent_grad, far_grad, swap_send.at[2], swap_recv.at[2], partner()),
    ]
    loaded.wait()
    parts[0][...] = (kept_total[...] + arrived[...].astype(single)).astype(bfloat)
    first = 0
    starts = []
    for n, size in enumerate(sizes):
        chunk = parts[n].shape[0] // size
        copies = []
        for turn, (other, device) in enumerate(groups[n]):
            copies.append(
                copy(
                    parts[n].at[pl.ds(pl.multiple_of(other * chunk, 16), chunk)],
                    slots[n].at[turn],
                    sum_send.at[first + turn],
                    sum_recv.at[first + turn],
                    device,
                )
            )
        total = parts[n][pl.ds(pl.multiple_of(places[n] * chunk, 16), chunk), :].astype(single)
        for turn, c in enumerate(copies):
            c.wait_recv()
            total = total + slots[n][turn].astype(single)
        sent += copies
        target = parts[n + 1] if n + 1 < count else last
        target[...] = total.astype(bfloat)
        starts.append(first)
        first += size - 1
    source = last
    for n in reversed(range(count)):
        chunk = parts[n].shape[0] // sizes[n]
        mine = pl.ds(pl.multiple_of(places[n] * chunk, 16), chunk)
        copies = []
        for turn, (_, device) in enumerate(groups[n]):
            k = starts[n] + turn
            copies.append(
                copy(source, wholes[n].at[mine], gather_send.at[k], gather_recv.at[k], device)
            )
        wholes[n][mine, :] = source[...]
        for c in copies:
            c.wait_recv()
        sent += copies
        source = wholes[n]
    for c in sent:
        c.wait_send()
    for c in far:
        c.wait()


def finish_kernel(
    gathered_far,
    far_out,
    far_grad,
    kept_out,
    kept_grad,
    layer_outputs,
    input_grads,
    grad_gains,
    grad_qkv,
    grad_out,
    grad_gate_up,
    grad_down,
    gathered,
    passed,
    narrow,
    wide,
    arrive,
    leave,
):
    count = far_out.shape[0]
    place = (1 - lax.axis_index("section")) * count
    outs = pltpu.make_async_copy(passed, layer_outputs.at[pl.ds(place, count)], leave.at[count])
    into = pltpu.make_async_copy(far_out, passed, arrive.at[count + 1])
    sums = pltpu.make_async_copy(gathered_far, gathered, arrive.at[count])
    reads = [pltpu.make_async_copy(far_grad.at[i], narrow.at[i], arrive.at[i]) for i in range(count)]
    writes = [
        pltpu.make_async_copy(wide.at[i], input_grads.at[place + i], leave.at[i])
        for i in range(count)
    ]
    for c in reads + [sums, into]:
        c.start()
    for i in range(count):
        reads[i].wait()
        wide[i] = narrow[i].astype(single)
        writes[i].start()
    into.wait()
    outs.start()
    sums.wait()
    width = grad_qkv.shape[0]
    block = 0
    for ref in (grad_gate_up, grad_down, grad_qkv, grad_out):
        for n in range(0, ref.shape[1] - 127, 128):
            ref[:, n : n + 128] = gathered[block * width : (block + 1) * width, :].astype(single)
            block += 1
    rest = gathered[block * width : (block + 1) * width, :].astype(single)
    grad_qkv[:, 3 * width - QKV_REST :] = rest[:, :QKV_REST]
    grad_out[:, width - OUT_REST :] = rest[:, QKV_REST : QKV_REST + OUT_REST]
    grad_gains[...] = rest.T[QKV_REST + OUT_REST : QKV_REST + OUT_REST + 2, :]
    for c in writes + [outs]:
        c.wait()


def finish(gathered, far_out, far_grad, kept_out, kept_grad, hidden):
    shape = jax.ShapeDtypeStruct
    count, width, length = far_out.shape
    anywhere = pl.BlockSpec(memory_space=pl.ANY)
    vmem = pl.BlockSpec(memory_space=pltpu.VMEM)
    v = pltpu.VMEM
    return pl.pallas_call(
        finish_kernel,
        out_shape=(
            shape(kept_out.shape, bfloat),
            shape(kept_grad.shape, single),
            shape((2, width), single),
            shape((width, 3 * width), single),
            shape((width, width), single),
            shape((width, 2 * hidden), single),
            shape((width, hidden), single),
        ),
        in_specs=[anywhere] * 5,
        out_specs=[anywhere] * 2 + [vmem] * 5,
        scratch_shapes=[
            v(gathered.shape, bfloat),
            v(far_out.shape, bfloat),
            v(far_grad.shape, bfloat),
            v(far_grad.shape, single),
            pltpu.SemaphoreType.DMA((count + 2,)),
            pltpu.SemaphoreType.DMA((count + 1,)),
        ],
        input_output_aliases={3: 0, 4: 1},
        compiler_params=pltpu.CompilerParams(vmem_limit_bytes=VMEM_LIMIT),
    )(gathered, far_out, far_grad, kept_out, kept_grad)


def reduce(devices, own_total, other_total, sent_out, sent_grad):
    sizes = group_sizes(devices)
    rows = own_total.shape[0]
    v = pltpu.VMEM
    shape = jax.ShapeDtypeStruct
    parts, slots, left = [], [], rows
    for size in sizes:
        parts.append(v((left, 128), bfloat))
        left //= size
        slots.append(v((size - 1, left, 128), bfloat))
    links = sum(size - 1 for size in sizes)
    dma = pltpu.SemaphoreType.DMA
    anywhere = pl.BlockSpec(memory_space=pl.ANY)
    vmem = pl.BlockSpec(memory_space=pltpu.VMEM)
    return pl.pallas_call(
        functools.partial(reduce_kernel, sizes),
        out_shape=(
            shape(sent_out.shape, bfloat),
            shape(sent_grad.shape, bfloat),
            shape((rows, 128), bfloat),
        ),
        in_specs=[anywhere] * 4,
        out_specs=[anywhere, anywhere, vmem],
        scratch_shapes=[v((rows, 128), bfloat), v((rows, 128), single), dma]
        + parts
        + slots
        + parts[1:]
        + [v((left, 128), bfloat), dma((3,)), dma((3,))]
        + [dma((links,))] * 4,
        compiler_params=pltpu.CompilerParams(
            collective_id=1, has_side_effects=True, vmem_limit_bytes=VMEM_LIMIT
        ),
    )(own_total, other_total, sent_out, sent_grad)


def on_device(
    devices,
    raw,
    series_ids,
    median,
    scale,
    cotangent,
    norm_gains,
    qkv_weight,
    out_weight,
    gate_up_weight,
    down_weight,
):
    section = lax.axis_index("section")
    turned = lambda a: jnp.swapaxes(a, -1, -2)
    count = raw.shape[0] // 2
    width, hidden = raw.shape[2], down_weight.shape[1]
    own = (norm_gains[0], qkv_weight[0], out_weight[0], gate_up_weight[0], turned(down_weight[0]))
    other = swap_weights(own)
    blocks = 14
    rows = -(-blocks * width // (16 * devices)) * 16 * devices
    kept_out, kept_grad, sent_out, sent_grad, own_total, other_total = train(
        section, rows, turned(raw), series_ids, median, scale, turned(cotangent), own, other
    )
    far_out, far_grad, gathered = reduce(devices, own_total, other_total, sent_out, sent_grad)
    layer_outputs, input_grads, gain, qkv, out, gate_up, down = finish(
        gathered, far_out, far_grad, kept_out, kept_grad, hidden
    )
    return (
        turned(layer_outputs)[None],
        turned(input_grads)[None],
        gain[None],
        qkv[None],
        out[None],
        gate_up[None],
        turned(down)[None],
    )


def solution(mesh):
    placed = (
        P("dp", None, None),
        P("dp"),
        P(),
        P(),
        P("dp", None, None),
        P("section", None, None),
        P("section", None, None),
        P("section", None, None),
        P("section", None, None),
        P("section", None, None),
    )
    return jax.shard_map(
        functools.partial(on_device, mesh.shape["dp"]),
        mesh=mesh,
        in_specs=placed,
        out_specs=(
            P("section", "dp", None, None),
            P("section", "dp", None, None),
            P("section", None, None),
            P("section", None, None),
            P("section", None, None),
            P("section", None, None),
            P("section", None, None),
        ),
        check_vma=False,
    )
```
